512 devices in a mesh: ctx: 64 (over z_hi, y, x), tp: 8 (over z_lo, core).
Axes of the slice: x: 4, y: 8, z: 8 (z_hi: 2, z_lo: 4; z = z_hi * 4 + z_lo), core: 2. Of those that a mesh axis runs over, the one named last changes fastest.
Arguments:
- hidden_in: bfloat16 [10240, 2048], P('ctx'), may hold values from -8 to 8
- norm_gain: float32 [2048], replicated, may hold values from 0.1 to 1.9
- snap_qkv: bfloat16 [64, 3, 2048, 2048], P('ctx', None, None, 'tp'), may hold values from -1 to 1
- snap_out: bfloat16 [64, 2048, 2048], P('ctx', 'tp'), may hold values from -0.125 to 0.125
- owner_index: int32 [1], replicated, may hold values from 0 to 63
- block_order: int32 [64], replicated, may hold values from 0 to 63, each once
Outputs:
- attention_out: bfloat16 [10240, 2048], P('ctx', 'tp')
The draws below stay inside these ranges and needn't reach their ends.
Inputs may be any that keep to these rules, and one draw needn't show every extreme that they name: `block_order`: each block appears once.
All inputs are finite; a program needn't handle non-finite values.
Results may differ from the reference program's by a relative error of at most 0.02.
Values may be sent and summed in bfloat16 or wider, within the bound.
No kernel may reach another device: no remote copies, remote signals or barrier semaphores. Data moves between devices by JAX's collectives and lax.ppermute only.
A program may use at most 128 MiB of HBM per device.

```python
import jax
import jax.numpy as jnp
from jax import lax

D = 2048
HEADS = 16
HD = 128
TOK_DEV = 160
BLOCKS = 64
SEQ = 10240
N_CTX = 64


def draw_hidden_in(key, part):
    key = jax.random.fold_in(key, 3)
    jitter_key = jax.random.fold_in(key, 0)
    return jnp.clip(jax.random.normal(jitter_key, (SEQ, D), jnp.float32), -6.0, 6.0).astype(jnp.bfloat16)


def draw_snap_qkv(key, part):
    key = jax.random.fold_in(key, 5)
    weight_key = jax.random.fold_in(key, 0)
    result = jax.random.truncated_normal(weight_key, -3.0, 3.0, (BLOCKS, 3, D, HEADS * HD), jnp.float32) * D ** (-0.5)
    return result.astype(jnp.bfloat16)


def steps_of(own_key, dims, shards, low, high):
    def one(dim, blocks):
        draws = jax.random.uniform(jax.random.fold_in(jax.random.fold_in(own_key, 6), dim), (blocks,), jnp.float32, low / len(shards), high / len(shards))
        return jnp.repeat(jnp.exp(draws), dims[dim] // blocks).reshape((-1,) + (1,) * (len(dims) - dim - 1))

    gain = one(*shards[0])
    for cut in shards[1:]:
        gain = gain * one(*cut)
    return gain


def centred(own_key, shape, spread, limit, cuts=(), kind=jnp.bfloat16):
    entries = jax.random.normal(own_key, shape, jnp.float32) * spread
    if len(cuts) > 0:
        entries = steps_of(own_key, shape, cuts, -0.22, 0.18) * entries
    return jnp.clip(entries, min=-limit, max=limit).astype(kind)


def setup_inputs(seed: int = 0) -> dict:
    streams_of = jax.random.split(jax.random.key(seed), 7)
    hidden_in = draw_hidden_in(jax.random.fold_in(streams_of[6], 71), 0)
    norm_gain = jnp.clip(1.0 + 0.18 * jax.random.normal(streams_of[1], (D,), jnp.float32), 0.1, 1.9)
    snap_qkv = draw_snap_qkv(jax.random.fold_in(streams_of[6], 71), 0)
    snap_out = centred(streams_of[3], (BLOCKS, HEADS * HD, D), (HEADS * HD) ** -0.5, 0.125, ((0, 64), (1, 8)))
    owner_index = jax.random.randint(streams_of[4], (1,), 0, N_CTX).astype(jnp.int32)
    block_order = jax.random.permutation(streams_of[5], BLOCKS).astype(jnp.int32)
    return {"hidden_in": hidden_in, "norm_gain": norm_gain, "snap_qkv": snap_qkv, "snap_out": snap_out, "owner_index": owner_index, "block_order": block_order}


def reference(hidden_in, norm_gain, snap_qkv, snap_out, owner_index, block_order):
    widened = hidden_in.astype(jnp.float32)
    normed = (widened * lax.rsqrt(lax.optimization_barrier(jnp.mean(widened * widened, axis=-1, keepdims=True)) + 1e-06) * norm_gain).astype(jnp.bfloat16)
    wqkv = snap_qkv[owner_index[0]]
    wout = snap_out[owner_index[0]]
    projected = jnp.einsum('td,jdc->jtc', normed.astype(jnp.float32), wqkv.astype(jnp.float32)).astype(jnp.bfloat16)
    positions = (block_order[:, None] * TOK_DEV + jnp.arange(TOK_DEV, dtype=jnp.int32)[None, :]).reshape(-1).astype(jnp.int32)
    queries = jnp.moveaxis(projected[0].reshape(SEQ, HEADS, HD), 1, 0)
    keys = jnp.moveaxis(projected[1].reshape(SEQ, HEADS, HD), 1, 0)
    values = jnp.moveaxis(projected[2].reshape(SEQ, HEADS, HD), 1, 0)
    scale = 1.0 / HD ** 0.5
    query_blocks = positions.reshape(BLOCKS, TOK_DEV)

    def one_head(packed):
        head_q, head_k, head_v = packed
        blocks_q = head_q.reshape(BLOCKS, TOK_DEV, HD)

        def one_block(inner):
            block_q, block_pos = inner
            scores = jnp.dot(block_q.astype(jnp.float32), head_k.astype(jnp.float32).T) * scale
            allowed = positions[None, :] <= block_pos[:, None]
            scores = jnp.where(allowed, scores, -1e+30)
            row_max = lax.optimization_barrier(jnp.max(scores, axis=-1, keepdims=True))
            weights = jnp.where(allowed, jnp.exp(scores - row_max), 0.0)
            total = lax.optimization_barrier(jnp.sum(weights, axis=-1, keepdims=True))
            summed = jnp.dot(weights.astype(jnp.bfloat16).astype(jnp.float32), head_v.astype(jnp.float32))
            return (summed / total).astype(jnp.bfloat16)
        return lax.map(one_block, (blocks_q, query_blocks)).reshape(SEQ, HD)
    context = lax.map(one_head, (queries, keys, values))
    context = jnp.moveaxis(context, 0, 1).reshape(SEQ, HEADS * HD)
    return jnp.dot(context, wout, preferred_element_type=jnp.float32).astype(jnp.bfloat16)
```

```python
import jax
import jax.numpy as jnp
import numpy as np
from jax import lax
from jax.experimental import pallas as pl
from jax.experimental.pallas import tpu as pltpu
from jax.sharding import Mesh
from jax.sharding import PartitionSpec as P

HD = 128
HIDE = -1e30
TILE = 160
CHUNK = 640


def attend_kernel(q_ref, kv_ref, qpos_ref, kpos_ref, o_ref, stat_ref, s_ref):
    factor = float(np.log2(np.e) / HD**0.5)
    rows = q_ref.shape[0]
    count = kv_ref.shape[0] // CHUNK
    q = q_ref[...]
    qpos = qpos_ref[...]
    high = jnp.full((rows, HD), HIDE, jnp.float32)
    for j in range(count):
        span = pl.ds(j * CHUNK, CHUNK)
        s = lax.dot_general(
            q, kv_ref[span, :HD], (((1,), (1,)), ((), ())), preferred_element_type=jnp.float32
        )
        s = jnp.where(kpos_ref[:, span] <= qpos, s * factor, HIDE)
        s_ref[:, span] = s
        for t in range(CHUNK // HD):
            high = jnp.maximum(high, s[:, t * HD : (t + 1) * HD])
    top = jnp.max(high, axis=1, keepdims=True)
    base = jnp.where(top <= 0.5 * HIDE, 0.0, top)
    total = jnp.zeros((rows, HD), jnp.float32)
    acc = jnp.zeros((rows, HD), jnp.float32)
    for j in range(count):
        span = pl.ds(j * CHUNK, CHUNK)
        p = jnp.exp2(s_ref[:, span] - base)
        for t in range(CHUNK // HD):
            total = total + p[:, t * HD : (t + 1) * HD]
        acc = acc + jnp.dot(
            p.astype(jnp.bfloat16), kv_ref[span, HD:], preferred_element_type=jnp.float32
        )
    total = jnp.sum(total, axis=1, keepdims=True)
    o_ref[...] = acc / jnp.where(total == 0.0, 1.0, total)
    lane = lax.broadcasted_iota(jnp.int32, (rows, HD), 1)
    stat_ref[...] = jnp.where(lane == 0, top, total)


def attend(q, kv, qpos, kpos):
    nq, nk = q.shape[0], kv.shape[0]
    return pl.pallas_call(
        attend_kernel,
        grid=(nq // TILE,),
        in_specs=[
            pl.BlockSpec((TILE, HD), lambda i: (i, 0)),
            pl.BlockSpec((nk, 2 * HD), lambda i: (0, 0)),
            pl.BlockSpec((TILE, 1), lambda i: (i, 0)),
            pl.BlockSpec((1, nk), lambda i: (0, 0)),
        ],
        out_specs=[
            pl.BlockSpec((TILE, HD), lambda i: (i, 0)),
            pl.BlockSpec((TILE, HD), lambda i: (i, 0)),
        ],
        out_shape=[
            jax.ShapeDtypeStruct((nq, HD), jnp.float32),
            jax.ShapeDtypeStruct((nq, HD), jnp.float32),
        ],
        scratch_shapes=[pltpu.VMEM((TILE, nk), jnp.float32)],
        compiler_params=pltpu.CompilerParams(vmem_limit_bytes=48 * 1024 * 1024),
        cost_estimate=pl.CostEstimate(
            flops=4 * nq * nk * HD, bytes_accessed=nk * HD * 4, transcendentals=nq * nk
        ),
    )(q, kv, qpos, kpos)


def swap(block, axis):
    return lax.ppermute(block, axis, [(0, 1), (1, 0)])


def exchange(block, axis):
    return lax.all_to_all(block, axis, 0, 0, tiled=True)


def pick(blocks, index):
    return lax.dynamic_index_in_dim(blocks, index, 0, keepdims=False)


def shards(hidden_in, norm_gain, snap_qkv, snap_out, owner_index, block_order):
    rows, width = hidden_in.shape
    zh, y, x, c = (lax.axis_index(name) for name in ("zh", "y", "x", "c"))
    ny, nx, nl = 8, 4, 4
    half = rows // 2
    owner = owner_index[0]
    zh0, y0, x0 = owner // (ny * nx), (owner // nx) % ny, owner % nx

    part = width // (2 * ny)
    w = snap_qkv[0].reshape(3, ny, 2, part, 2, HD)
    w = jnp.transpose(w, (2, 4, 1, 3, 0, 5)).reshape(2, 2, ny, part, 3 * HD)
    w = exchange(w, "c").reshape(nx, ny, part, 3 * HD)
    w = pick(exchange(w, "x"), x0)
    w = pick(exchange(w, "y"), y0)
    w = jnp.where(zh == zh0, w, swap(w, "zh"))
    w, snap_out = lax.optimization_barrier((w, snap_out))
    w = lax.all_gather(w, ("y", "c"), axis=0, tiled=True)
    w = w.reshape(width, 3 * HD)

    mine = lax.dynamic_slice_in_dim(hidden_in, c * half, half, 0).astype(jnp.float32)
    normed = (
        mine * lax.rsqrt(jnp.mean(mine * mine, axis=-1, keepdims=True) + 1e-06) * norm_gain
    ).astype(jnp.bfloat16)
    normed = lax.all_gather(normed, "x", axis=0, tiled=True)

    qkv = jnp.dot(normed, w, preferred_element_type=jnp.float32).astype(jnp.bfloat16)
    q, kv = qkv[:, :HD], qkv[:, HD:]
    q_other = swap(q, "zh")
    kv = lax.all_gather(kv, ("y", "c"), axis=0, tiled=True)

    order = block_order.reshape(2, ny, nx) * rows
    offsets = jnp.arange(half, dtype=jnp.int32)
    halves = jnp.arange(2, dtype=jnp.int32) * half
    kpos = pick(order, zh)[:, None, :, None] + halves[None, :, None, None] + offsets
    here = lax.dynamic_index_in_dim(order, y, 1, keepdims=False)
    here = jnp.stack([pick(here, zh), pick(here, 1 - zh)])
    qpos = here[:, :, None] + c * half + offsets

    cols = snap_out.shape[2] // nx
    wo = snap_out[0].reshape(ny, -1, nx, cols)
    wo = jnp.transpose(wo, (2, 0, 1, 3))
    wo = pick(exchange(wo, "x"), x0)
    wo = pick(exchange(wo, "y"), y0)
    wo = jnp.where(zh == zh0, wo, swap(wo, "zh"))
    wo = lax.all_gather(wo, ("c", "y"), axis=0, tiled=True)
    wo = lax.all_gather(wo, "x", axis=0, tiled=False)

    o, stat = attend(
        jnp.concatenate([q, q_other]), kv, qpos.reshape(-1, 1), kpos.reshape(1, -1)
    )
    n = q.shape[0]
    m, t = stat[:, 0], stat[:, 1]
    o_in = swap(o[n:].astype(jnp.bfloat16), "zh").astype(jnp.float32)
    stat_in = swap(jnp.stack([m[n:], t[n:]]), "zh")
    m_all = jnp.maximum(m[:n], stat_in[0])
    a = t[:n] * jnp.exp2(m[:n] - m_all)
    b = stat_in[1] * jnp.exp2(stat_in[0] - m_all)
    context = (o[:n] * (a / (a + b))[:, None] + o_in * (b / (a + b))[:, None]).astype(jnp.bfloat16)

    context = exchange(context.reshape(nx, half, HD), "x")
    context = jnp.transpose(context, (1, 0, 2)).reshape(half, nx * HD)
    terms = jnp.einsum("tk,nkc->ntc", context, wo.reshape(nl, -1, cols), preferred_element_type=jnp.float32)
    terms = exchange(terms.astype(jnp.bfloat16), "zl")
    out = jnp.sum(terms.astype(jnp.float32), axis=0).astype(jnp.bfloat16)
    out = jnp.transpose(out.reshape(half, 2, -1), (1, 0, 2))
    return exchange(out, "c").reshape(rows, -1)


def solution(mesh):
    fine = Mesh(mesh.devices.reshape(2, 8, 4, 4, 2), ("zh", "y", "x", "zl", "c"))
    ctx, tp = ("zh", "y", "x"), ("zl", "c")
    in_specs = (P(ctx, None), P(), P(ctx, None, None, tp), P(ctx, tp, None), P(), P())
    return jax.shard_map(shards, mesh=fine, in_specs=in_specs, out_specs=P(ctx, tp), check_vma=False)
```

```python
import jax
import jax.numpy as jnp
import numpy as np
from jax import lax
from jax.experimental import pallas as pl
from jax.experimental.pallas import tpu as pltpu
from jax.sharding import Mesh
from jax.sharding import PartitionSpec as P

HD = 128
HIDE = -1e30
CHUNK = 640
EXTRA = 16
LIMIT = pltpu.CompilerParams(vmem_limit_bytes=48 * 1024 * 1024)


def fold_kernel(w_ref, o_ref):
    part = o_ref.shape[3]
    for c in range(2):
        for h in range(2):
            for j in range(3):
                o_ref[c, h, 0, :, j * HD : (j + 1) * HD] = w_ref[
                    j, c * part : (c + 1) * part, h * HD : (h + 1) * HD
                ]


def fold(w, ny):
    part = w.shape[1] // (2 * ny)
    return pl.pallas_call(
        fold_kernel,
        grid=(ny,),
        in_specs=[pl.BlockSpec((3, 2 * part, 2 * HD), lambda i: (0, i, 0))],
        out_specs=pl.BlockSpec((2, 2, 1, part, 3 * HD), lambda i: (0, 0, i, 0, 0)),
        out_shape=jax.ShapeDtypeStruct((2, 2, ny, part, 3 * HD), w.dtype),
        compiler_params=LIMIT,
        cost_estimate=pl.CostEstimate(flops=0, bytes_accessed=4 * w.size, transcendentals=0),
    )(w)


def project_kernel(x_ref, w_ref, q_ref, kv_ref):
    out = jnp.dot(x_ref[...], w_ref[...], preferred_element_type=jnp.float32)
    q_ref[...] = out[:, :HD].astype(q_ref.dtype)
    kv_ref[...] = out[:, HD:].astype(kv_ref.dtype)


def project(x, w):
    n = x.shape[0]
    return pl.pallas_call(
        project_kernel,
        out_shape=[
            jax.ShapeDtypeStruct((n, HD), jnp.bfloat16),
            jax.ShapeDtypeStruct((n, 2 * HD), jnp.bfloat16),
        ],
        compiler_params=LIMIT,
        cost_estimate=pl.CostEstimate(
            flops=2 * n * w.size, bytes_accessed=2 * (x.size + w.size), transcendentals=0
        ),
    )(x, w)


def three_parts(value):
    first = value.astype(jnp.bfloat16).astype(jnp.float32)
    rest = value - first
    second = rest.astype(jnp.bfloat16).astype(jnp.float32)
    return first, second, rest - second


def attend_kernel(q_ref, kv_ref, qpos_ref, kpos_ref, o_ref, s_ref):
    factor = float(np.log2(np.e) / HD**0.5)
    rows = q_ref.shape[0]
    count = kv_ref.shape[0] // CHUNK
    q = q_ref[...]
    qpos = qpos_ref[...]
    high = jnp.full((rows, HD), HIDE, jnp.float32)
    for j in range(count):
        span = pl.ds(j * CHUNK, CHUNK)
        s = lax.dot_general(
            q, kv_ref[span, :HD], (((1,), (1,)), ((), ())), preferred_element_type=jnp.float32
        )
        s = jnp.where(kpos_ref[:, span] <= qpos, s * factor, HIDE)
        s_ref[:, span] = s
        for t in range(CHUNK // HD):
            high = jnp.maximum(high, s[:, t * HD : (t + 1) * HD])
    top = jnp.max(high, axis=1, keepdims=True)
    base = jnp.where(top <= 0.5 * HIDE, 0.0, top)
    total = jnp.zeros((rows, HD), jnp.float32)
    acc = jnp.zeros((rows, HD), jnp.float32)
    for j in range(count):
        span = pl.ds(j * CHUNK, CHUNK)
        p = jnp.exp2(s_ref[:, span] - base)
        for t in range(CHUNK // HD):
            total = total + p[:, t * HD : (t + 1) * HD]
        acc = acc + jnp.dot(
            p.astype(jnp.bfloat16), kv_ref[span, HD:], preferred_element_type=jnp.float32
        )
    total = jnp.sum(total, axis=1, keepdims=True)
    o = acc / jnp.where(total == 0.0, 1.0, total)
    lane = lax.broadcasted_iota(jnp.int32, (rows, HD), 1)
    stat = jnp.zeros((rows, HD), jnp.float32)
    for k, piece in enumerate(three_parts(top) + three_parts(total)):
        stat = jnp.where(lane == k, piece, stat)
    blocks, half = o_ref.shape[0], o_ref.shape[1] - EXTRA
    for b in range(blocks):
        o_ref[b, :half, :] = o[b * half : (b + 1) * half].astype(o_ref.dtype)
        block = jnp.concatenate(
            [stat[b * half : (b + 1) * half], jnp.zeros((HD - half, HD), jnp.float32)]
        )
        o_ref[b, half:, :] = block.T[:EXTRA].astype(o_ref.dtype)


def attend(q, kv, qpos, kpos, half):
    nq, nk = q.shape[0], kv.shape[0]
    tile = 2 * half
    return pl.pallas_call(
        attend_kernel,
        grid=(nq // tile,),
        in_specs=[
            pl.BlockSpec((tile, HD), lambda i: (i, 0)),
            pl.BlockSpec((nk, 2 * HD), lambda i: (0, 0)),
            pl.BlockSpec((tile, 1), lambda i: (i, 0)),
            pl.BlockSpec((1, nk), lambda i: (0, 0)),
        ],
        out_specs=pl.BlockSpec((2, half + EXTRA, HD), lambda i: (i, 0, 0)),
        out_shape=jax.ShapeDtypeStruct((nq // half, half + EXTRA, HD), jnp.bfloat16),
        scratch_shapes=[pltpu.VMEM((tile, nk), jnp.float32)],
        compiler_params=LIMIT,
        cost_estimate=pl.CostEstimate(
            flops=4 * nq * nk * HD, bytes_accessed=nk * HD * 4, transcendentals=nq * nk
        ),
    )(q, kv, qpos, kpos)


def finish_kernel(c_ref, part_ref, mine_ref, other_ref, out_ref):
    heads, half = part_ref.shape[1], part_ref.shape[2] - EXTRA
    context = []
    for h in range(heads):
        weight, values = [], []
        for k in range(2):
            stat = part_ref[k, h, half:, :].astype(jnp.float32)
            stat = jnp.concatenate([stat, jnp.zeros((HD - EXTRA, HD), jnp.float32)]).T[:half]
            weight.append((stat[:, 0:1] + stat[:, 1:2] + stat[:, 2:3], stat[:, 3:4] + stat[:, 4:5] + stat[:, 5:6]))
            values.append(part_ref[k, h, :half, :].astype(jnp.float32))
        top = jnp.maximum(weight[0][0], weight[1][0])
        a = weight[0][1] * jnp.exp2(weight[0][0] - top)
        b = weight[1][1] * jnp.exp2(weight[1][0] - top)
        context.append(((values[0] * a + values[1] * b) / (a + b)).astype(jnp.bfloat16))
    low = jnp.concatenate(context[: heads // 2], axis=1)
    high = jnp.concatenate(context[heads // 2 :], axis=1)
    first = c_ref[0] == 0
    near = jnp.where(first, low, high)
    far = jnp.where(first, high, low)
    for n in range(mine_ref.shape[0]):
        terms = jnp.dot(near, mine_ref[n], preferred_element_type=jnp.float32)
        terms += jnp.dot(far, other_ref[n], preferred_element_type=jnp.float32)
        terms = terms.astype(out_ref.dtype)
        width = out_ref.shape[2]
        out_ref[2 * n] = terms[:, :width]
        out_ref[2 * n + 1] = terms[:, width:]


def finish(core, parts, mine, other):
    half = parts.shape[2] - EXTRA
    blocks, _, cols = mine.shape
    vmem = pl.BlockSpec(memory_space=pltpu.VMEM)
    return pl.pallas_call(
        finish_kernel,
        in_specs=[pl.BlockSpec(memory_space=pltpu.SMEM), vmem, vmem, vmem],
        out_specs=vmem,
        out_shape=jax.ShapeDtypeStruct((2 * blocks, half, cols // 2), jnp.bfloat16),
        compiler_params=LIMIT,
        cost_estimate=pl.CostEstimate(
            flops=4 * half * mine.size, bytes_accessed=4 * mine.size, transcendentals=0
        ),
    )(core, parts, mine, other)


def swap(block, axis):
    return lax.ppermute(block, axis, [(0, 1), (1, 0)])


def exchange(block, axis):
    return lax.all_to_all(block, axis, 0, 0, tiled=True)


def gather(block, axis):
    count = lax.axis_size(axis)
    return exchange(jnp.broadcast_to(block[None], (count,) + block.shape), axis)


def pick(blocks, index):
    return lax.dynamic_index_in_dim(blocks, index, 0, keepdims=False)


def shards(hidden_in, norm_gain, snap_qkv, snap_out, owner_index, block_order):
    rows, width = hidden_in.shape
    zh, y, x, c = (lax.axis_index(name) for name in ("zh", "y", "x", "c"))
    ny, nx = 8, 4
    half = rows // 2
    owner = owner_index[0]
    zh0, y0, x0 = owner // (ny * nx), (owner // nx) % ny, owner % nx

    mine = lax.dynamic_slice_in_dim(hidden_in, c * half, half, 0).astype(jnp.float32)
    normed = (
        mine * lax.rsqrt(jnp.mean(mine * mine, axis=-1, keepdims=True) + 1e-06) * norm_gain
    ).astype(jnp.bfloat16)

    part = width // (2 * ny)
    w = exchange(fold(snap_qkv[0], ny), "c").reshape(nx, ny, part, 3 * HD)
    w = pick(exchange(w, "x"), x0)
    normed = lax.all_gather(normed, "x", axis=0, tiled=True)
    wo = jnp.where(x == x0, snap_out[0], jnp.zeros_like(snap_out[0]))
    wo = jnp.transpose(wo.reshape(wo.shape[0], nx, -1), (1, 0, 2))
    w, wo, normed = lax.optimization_barrier((w, wo, normed))
    wo = lax.psum_scatter(wo, "x", scatter_dimension=0)
    w = pick(exchange(w, "y"), y0)
    w = jnp.where(zh == zh0, w, swap(w, "zh"))
    w, wo = lax.optimization_barrier((w, wo))
    w = lax.all_gather(w, ("y", "c"), axis=0, tiled=True)
    wo = pick(exchange(wo.reshape(ny, -1, wo.shape[1]), "y"), y0)
    wo = jnp.where(zh == zh0, wo, swap(wo, "zh"))
    w, wo = lax.optimization_barrier((w, wo))
    wo = gather(wo, "y").reshape(-1, wo.shape[1])

    q, kv = project(normed, w)
    kv = lax.all_gather(kv, ("y", "c"), axis=0, tiled=True)
    q_other = swap(q, "zh")
    wo = gather(wo, "x")
    wo_other = swap(wo, "c")
    q0, q1 = jnp.where(zh == 0, q, q_other), jnp.where(zh == 0, q_other, q)
    q_all = jnp.concatenate([q0, q1])

    order = block_order.reshape(2, ny, nx) * rows
    offsets = jnp.arange(half, dtype=jnp.int32)
    halves = jnp.arange(2, dtype=jnp.int32) * half
    kpos = pick(order, zh)[:, None, :, None] + halves[None, :, None, None] + offsets
    here = lax.dynamic_index_in_dim(order, y, 1, keepdims=False)
    qpos = here[:, :, None] + c * half + offsets

    parts = attend(q_all, kv, qpos.reshape(-1, 1), kpos.reshape(1, -1), half)
    parts = exchange(parts, ("zh", "x")).reshape((2, nx) + parts.shape[1:])
    terms = finish(c.reshape(1), parts, wo, wo_other)
    terms = exchange(terms, ("zl", "c")).reshape(-1, rows, terms.shape[2])
    return jnp.sum(terms.astype(jnp.float32), axis=0).astype(jnp.bfloat16)


def solution(mesh):
    fine = Mesh(mesh.devices.reshape(2, 8, 4, 4, 2), ("zh", "y", "x", "zl", "c"))
    ctx, tp = ("zh", "y", "x"), ("zl", "c")
    in_specs = (P(ctx, None), P(), P(ctx, None, None, tp), P(ctx, tp, None), P(), P())
    return jax.shard_map(shards, mesh=fine, in_specs=in_specs, out_specs=P(ctx, tp), check_vma=False)
```

```python
import jax
import jax.numpy as jnp
import numpy as np
from jax import lax
from jax.experimental import pallas as pl
from jax.experimental.pallas import tpu as pltpu
from jax.sharding import Mesh
from jax.sharding import PartitionSpec as P

HD = 128
HIDE = -1e30
CHUNK = 640
EXTRA = 16
LIMIT = pltpu.CompilerParams(vmem_limit_bytes=48 * 1024 * 1024)


def fold_kernel(w_ref, o_ref):
    for c in range(2):
        for h in range(2):
            for j in range(3):
                o_ref[c, h, 0, :, j * HD : (j + 1) * HD] = w_ref[j, c, :, h * HD : (h + 1) * HD]


def fold(w, ny):
    part = w.shape[1] // (2 * ny)
    return pl.pallas_call(
        fold_kernel,
        grid=(ny,),
        in_specs=[pl.BlockSpec((3, 2, part, 2 * HD), lambda i: (0, 0, i, 0))],
        out_specs=pl.BlockSpec((2, 2, 1, part, 3 * HD), lambda i: (0, 0, i, 0, 0)),
        out_shape=jax.ShapeDtypeStruct((2, 2, ny, part, 3 * HD), w.dtype),
        compiler_params=LIMIT,
        cost_estimate=pl.CostEstimate(flops=0, bytes_accessed=4 * w.size, transcendentals=0),
    )(w.reshape(3, 2, ny * part, 2 * HD))


def near_kernel(c_ref, x_ref, w_ref, out_ref):
    depth = w_ref.shape[0]
    span = pl.ds(pl.multiple_of(c_ref[0] * depth, depth), depth)
    w = w_ref[:, : out_ref.shape[1]]
    out_ref[...] = jnp.dot(x_ref[:, span], w, preferred_element_type=jnp.float32)


def far_kernel(c_ref, x_ref, w_ref, sum_ref, q_ref, kv_ref):
    depth = w_ref.shape[0]
    span = pl.ds(pl.multiple_of((1 - c_ref[0]) * depth, depth), depth)
    w = w_ref[:, : sum_ref.shape[1]]
    out = sum_ref[...] + jnp.dot(x_ref[:, span], w, preferred_element_type=jnp.float32)
    q_ref[...] = out[:, :HD].astype(q_ref.dtype)
    kv_ref[...] = out[:, HD:].astype(kv_ref.dtype)


def project(core, x, near, far):
    n, cols = x.shape[0], 3 * HD
    smem, vmem = pl.BlockSpec(memory_space=pltpu.SMEM), pl.BlockSpec(memory_space=pltpu.VMEM)
    cost = pl.CostEstimate(
        flops=2 * n * near.shape[0] * cols, bytes_accessed=2 * (x.size + near.size), transcendentals=0
    )
    total = pl.pallas_call(
        near_kernel,
        in_specs=[smem, vmem, vmem],
        out_specs=vmem,
        out_shape=jax.ShapeDtypeStruct((n, cols), jnp.float32),
        compiler_params=LIMIT,
        cost_estimate=cost,
    )(core, x, near)
    return pl.pallas_call(
        far_kernel,
        in_specs=[smem, vmem, vmem, vmem],
        out_specs=[vmem, vmem],
        out_shape=[
            jax.ShapeDtypeStruct((n, HD), jnp.bfloat16),
            jax.ShapeDtypeStruct((n, 2 * HD), jnp.bfloat16),
        ],
        compiler_params=LIMIT,
        cost_estimate=cost,
    )(core, x, far, total)


def three_parts(value):
    first = value.astype(jnp.bfloat16).astype(jnp.float32)
    rest = value - first
    second = rest.astype(jnp.bfloat16).astype(jnp.float32)
    return first, second, rest - second


def attend_kernel(q_ref, near_ref, far_ref, qpos_ref, kpos_ref, o_ref, s_ref):
    factor = float(np.log2(np.e) / HD**0.5)
    rows = q_ref.shape[0]
    pieces = [
        (ref, j * CHUNK, i * ref.shape[0] + j * CHUNK)
        for i, ref in enumerate((near_ref, far_ref))
        for j in range(ref.shape[0] // CHUNK)
    ]
    q = q_ref[...]
    qpos = qpos_ref[...]
    high = jnp.full((rows, HD), HIDE, jnp.float32)
    for ref, at, column in pieces:
        span = pl.ds(column, CHUNK)
        s = lax.dot_general(
            q, ref[pl.ds(at, CHUNK), :HD], (((1,), (1,)), ((), ())), preferred_element_type=jnp.float32
        )
        s = jnp.where(kpos_ref[:, span] <= qpos, s * factor, HIDE)
        s_ref[:, span] = s
        for t in range(CHUNK // HD):
            high = jnp.maximum(high, s[:, t * HD : (t + 1) * HD])
    top = jnp.max(high, axis=1, keepdims=True)
    base = jnp.where(top <= 0.5 * HIDE, 0.0, top)
    total = jnp.zeros((rows, HD), jnp.float32)
    acc = jnp.zeros((rows, HD), jnp.float32)
    for ref, at, column in pieces:
        span = pl.ds(column, CHUNK)
        p = jnp.exp2(s_ref[:, span] - base)
        for t in range(CHUNK // HD):
            total = total + p[:, t * HD : (t + 1) * HD]
        acc = acc + jnp.dot(
            p.astype(jnp.bfloat16), ref[pl.ds(at, CHUNK), HD:], preferred_element_type=jnp.float32
        )
    total = jnp.sum(total, axis=1, keepdims=True)
    o = acc / jnp.where(total == 0.0, 1.0, total)
    lane = lax.broadcasted_iota(jnp.int32, (rows, HD), 1)
    stat = jnp.zeros((rows, HD), jnp.float32)
    for k, piece in enumerate(three_parts(top) + three_parts(total)):
        stat = jnp.where(lane == k, piece, stat)
    blocks, half = o_ref.shape[0], o_ref.shape[1] - EXTRA
    for b in range(blocks):
        o_ref[b, :half, :] = o[b * half : (b + 1) * half].astype(o_ref.dtype)
        block = jnp.concatenate(
            [stat[b * half : (b + 1) * half], jnp.zeros((HD - half, HD), jnp.float32)]
        )
        o_ref[b, half:, :] = block.T[:EXTRA].astype(o_ref.dtype)


def attend(q, near, far, qpos, kpos, half):
    nq, nk = q.shape[0], 2 * near.shape[0]
    tile = 2 * half
    return pl.pallas_call(
        attend_kernel,
        grid=(nq // tile,),
        in_specs=[
            pl.BlockSpec((tile, HD), lambda i: (i, 0)),
            pl.BlockSpec((nk // 2, 2 * HD), lambda i: (0, 0)),
            pl.BlockSpec((nk // 2, 2 * HD), lambda i: (0, 0)),
            pl.BlockSpec((tile, 1), lambda i: (i, 0)),
            pl.BlockSpec((1, nk), lambda i: (0, 0)),
        ],
        out_specs=pl.BlockSpec((2, half + EXTRA, HD), lambda i: (i, 0, 0)),
        out_shape=jax.ShapeDtypeStruct((nq // half, half + EXTRA, HD), jnp.bfloat16),
        scratch_shapes=[pltpu.VMEM((tile, nk), jnp.float32)],
        compiler_params=LIMIT,
        cost_estimate=pl.CostEstimate(
            flops=4 * nq * nk * HD, bytes_accessed=nk * HD * 4, transcendentals=nq * nk
        ),
    )(q, near, far, qpos, kpos)


def finish_kernel(c_ref, part_ref, mine_ref, other_ref, out_ref):
    heads, half = part_ref.shape[1], part_ref.shape[2] - EXTRA
    context = []
    for h in range(heads):
        weight, values = [], []
        for k in range(2):
            stat = part_ref[k, h, half:, :].astype(jnp.float32)
            stat = jnp.concatenate([stat, jnp.zeros((HD - EXTRA, HD), jnp.float32)]).T[:half]
            weight.append((stat[:, 0:1] + stat[:, 1:2] + stat[:, 2:3], stat[:, 3:4] + stat[:, 4:5] + stat[:, 5:6]))
            values.append(part_ref[k, h, :half, :].astype(jnp.float32))
        top = jnp.maximum(weight[0][0], weight[1][0])
        a = weight[0][1] * jnp.exp2(weight[0][0] - top)
        b = weight[1][1] * jnp.exp2(weight[1][0] - top)
        context.append(((values[0] * a + values[1] * b) / (a + b)).astype(jnp.bfloat16))
    low = jnp.concatenate(context[: heads // 2], axis=1)
    high = jnp.concatenate(context[heads // 2 :], axis=1)
    first = c_ref[0] == 0
    near = jnp.where(first, low, high)
    far = jnp.where(first, high, low)
    for n in range(mine_ref.shape[0]):
        terms = jnp.dot(near, mine_ref[n], preferred_element_type=jnp.float32)
        terms += jnp.dot(far, other_ref[n], preferred_element_type=jnp.float32)
        terms = terms.astype(out_ref.dtype)
        width = out_ref.shape[2]
        out_ref[2 * n] = terms[:, :width]
        out_ref[2 * n + 1] = terms[:, width:]


def finish(core, parts, mine, other):
    half = parts.shape[2] - EXTRA
    blocks, _, cols = mine.shape
    vmem = pl.BlockSpec(memory_space=pltpu.VMEM)
    return pl.pallas_call(
        finish_kernel,
        in_specs=[pl.BlockSpec(memory_space=pltpu.SMEM), vmem, vmem, vmem],
        out_specs=vmem,
        out_shape=jax.ShapeDtypeStruct((2 * blocks, half, cols // 2), jnp.bfloat16),
        compiler_params=LIMIT,
        cost_estimate=pl.CostEstimate(
            flops=4 * half * mine.size, bytes_accessed=4 * mine.size, transcendentals=0
        ),
    )(core, parts, mine, other)


def swap(block, axis):
    return lax.ppermute(block, axis, [(0, 1), (1, 0)])


def exchange(block, axis):
    return lax.all_to_all(block, axis, 0, 0, tiled=True)


def pick(blocks, index):
    return lax.dynamic_index_in_dim(blocks, index, 0, keepdims=False)


def spread(block, axis):
    count = lax.axis_size(axis)
    return exchange(jnp.broadcast_to(block[None], (count,) + block.shape), axis)


def shift(block, axis, distance):
    count = lax.axis_size(axis)
    return lax.ppermute(block, axis, [(i, (i + distance) % count) for i in range(count)])


def distances(axis):
    count = lax.axis_size(axis)
    return sorted(range(1, count), key=lambda s: -min(s, count - s))


def scatter_by_shifts(blocks, axis, source):
    here, count = lax.axis_index(axis), blocks.shape[0]
    result = pick(blocks, here)
    for s in distances(axis):
        got = shift(pick(blocks, (here + s) % count), axis, s)
        result = jnp.where((here - source) % count == s, got, result)
    return result


def gather_by_shifts(block, axis):
    here, count = lax.axis_index(axis), lax.axis_size(axis)
    got = {0: block}
    for s in distances(axis):
        got[s] = shift(block, axis, s)
    got = jnp.stack([got[s] for s in range(count)])
    return jnp.stack([pick(got, (here - i) % count) for i in range(count)])


def shards(hidden_in, norm_gain, snap_qkv, snap_out, owner_index, block_order):
    rows, width = hidden_in.shape
    zh, y, x, c = (lax.axis_index(name) for name in ("zh", "y", "x", "c"))
    ny, nx = 8, 4
    half = rows // 2
    core = c.reshape(1)
    owner = owner_index[0]
    zh0, y0, x0 = owner // (ny * nx), (owner // nx) % ny, owner % nx

    mine = lax.dynamic_slice_in_dim(hidden_in, c * half, half, 0).astype(jnp.float32)
    normed = (
        mine * lax.rsqrt(jnp.mean(mine * mine, axis=-1, keepdims=True) + 1e-06) * norm_gain
    ).astype(jnp.bfloat16)

    part = width // (2 * ny)
    w = exchange(fold(snap_qkv[0], ny), "c").reshape(nx, ny, part, 3 * HD)
    wo = snap_out[0].reshape(ny, -1, snap_out.shape[2])
    w = pick(exchange(w, "x"), x0)
    wo = scatter_by_shifts(wo, "y", y0)
    w, wo, normed = lax.optimization_barrier((w, wo, normed))
    w = pick(exchange(w, "y"), y0)
    normed = gather_by_shifts(normed, "x").reshape(-1, width)
    wo = jnp.transpose(wo.reshape(wo.shape[0], nx, -1), (1, 0, 2))
    wo = scatter_by_shifts(wo, "x", x0)
    wo = jnp.transpose(wo.reshape(wo.shape[0], nx, HD), (1, 0, 2)).reshape(part, HD)
    w = jnp.concatenate([w, wo], axis=1)
    w, normed = lax.optimization_barrier((w, normed))
    w = jnp.where(zh == zh0, w, swap(w, "zh"))
    w = spread(w, "y").reshape(ny * part, 4 * HD)
    q, kv = project(core, normed, w, swap(w, "c"))
    wo = w[:, 3 * HD :].reshape(ny, nx, part // nx, HD)
    wo = jnp.transpose(wo, (0, 2, 1, 3)).reshape(ny * part // nx, nx * HD)
    q, kv, wo = lax.optimization_barrier((q, kv, wo))

    near = spread(kv, "y").reshape(-1, 2 * HD)
    q_other = swap(q, "zh")
    q_all = jnp.concatenate([jnp.where(zh == 0, q, q_other), jnp.where(zh == 0, q_other, q)])
    wo = gather_by_shifts(wo, "x")
    near, q_all, wo = lax.optimization_barrier((near, q_all, wo))
    far = swap(near, "c")
    wo_far = swap(wo, "c")

    order = block_order.reshape(2, ny, nx) * rows
    offsets = jnp.arange(half, dtype=jnp.int32)
    kpos = (pick(order, zh)[:, :, None] + offsets).reshape(-1)
    kpos = jnp.concatenate([kpos + c * half, kpos + (1 - c) * half])
    here = lax.dynamic_index_in_dim(order, y, 1, keepdims=False)
    qpos = here[:, :, None] + c * half + offsets

    parts = attend(q_all, near, far, qpos.reshape(-1, 1), kpos.reshape(1, -1), half)
    parts = exchange(parts, ("zh", "x")).reshape((2, nx) + parts.shape[1:])
    terms = finish(core, parts, wo, wo_far)
    terms = exchange(terms, ("zl", "c")).reshape(-1, rows, terms.shape[2])
    return jnp.sum(terms.astype(jnp.float32), axis=0).astype(jnp.bfloat16)


def solution(mesh):
    fine = Mesh(mesh.devices.reshape(2, 8, 4, 4, 2), ("zh", "y", "x", "zl", "c"))
    ctx, tp = ("zh", "y", "x"), ("zl", "c")
    in_specs = (P(ctx, None), P(), P(ctx, None, None, tp), P(ctx, tp, None), P(), P())
    return jax.shard_map(shards, mesh=fine, in_specs=in_specs, out_specs=P(ctx, tp), check_vma=False)
```

```python
import jax
import jax.numpy as jnp
import numpy as np
from jax import lax
from jax.experimental import pallas as pl
from jax.experimental.pallas import tpu as pltpu
from jax.sharding import Mesh
from jax.sharding import PartitionSpec as P

HD = 128
HIDE = -1e30
CHUNK = 640
EXTRA = 16
LIMIT = pltpu.CompilerParams(vmem_limit_bytes=48 * 1024 * 1024)


def fold_kernel(w_ref, wo_ref, out_ref):
    span, cols = wo_ref.shape[0], wo_ref.shape[1] // 4
    for h in range(2):
        for r in range(2):
            for j in range(3):
                out_ref[2 * h + r, 0, :, j * HD : (j + 1) * HD] = w_ref[j, r, :, h * HD : (h + 1) * HD]
    for x in range(4):
        for k in range(4):
            at = x * cols + k * HD
            out_ref[x, 0, k * span : (k + 1) * span, 3 * HD :] = wo_ref[:, at : at + HD]


def fold(w, wo, ny):
    part = w.shape[1] // (2 * ny)
    return pl.pallas_call(
        fold_kernel,
        grid=(ny,),
        in_specs=[
            pl.BlockSpec((3, 2, part, 2 * HD), lambda i: (0, 0, i, 0)),
            pl.BlockSpec((wo.shape[0] // ny, wo.shape[1]), lambda i: (i, 0)),
        ],
        out_specs=pl.BlockSpec((4, 1, part, 4 * HD), lambda i: (0, i, 0, 0)),
        out_shape=jax.ShapeDtypeStruct((4, ny, part, 4 * HD), w.dtype),
        compiler_params=LIMIT,
        cost_estimate=pl.CostEstimate(flops=0, bytes_accessed=4 * (w.size + wo.size), transcendentals=0),
    )(w.reshape(3, 2, ny * part, 2 * HD), wo)


def near_kernel(c_ref, x_ref, w_ref, out_ref):
    depth = w_ref.shape[0]
    span = pl.ds(pl.multiple_of(c_ref[0] * depth, depth), depth)
    w = w_ref[:, : out_ref.shape[1]]
    out_ref[...] = jnp.dot(x_ref[:, span], w, preferred_element_type=jnp.float32)


def far_kernel(c_ref, x_ref, w_ref, sum_ref, q_ref, kv_ref):
    depth = w_ref.shape[0]
    span = pl.ds(pl.multiple_of((1 - c_ref[0]) * depth, depth), depth)
    w = w_ref[:, : sum_ref.shape[1]]
    out = sum_ref[...] + jnp.dot(x_ref[:, span], w, preferred_element_type=jnp.float32)
    q_ref[...] = out[:, :HD].astype(q_ref.dtype)
    kv_ref[...] = out[:, HD:].astype(kv_ref.dtype)


def project(core, x, near, far):
    n, cols = x.shape[0], 3 * HD
    smem, vmem = pl.BlockSpec(memory_space=pltpu.SMEM), pl.BlockSpec(memory_space=pltpu.VMEM)
    cost = pl.CostEstimate(
        flops=2 * n * near.shape[0] * cols, bytes_accessed=2 * (x.size + near.size), transcendentals=0
    )
    total = pl.pallas_call(
        near_kernel,
        in_specs=[smem, vmem, vmem],
        out_specs=vmem,
        out_shape=jax.ShapeDtypeStruct((n, cols), jnp.float32),
        compiler_params=LIMIT,
        cost_estimate=cost,
    )(core, x, near)
    return pl.pallas_call(
        far_kernel,
        in_specs=[smem, vmem, vmem, vmem],
        out_specs=[vmem, vmem],
        out_shape=[
            jax.ShapeDtypeStruct((n, HD), jnp.bfloat16),
            jax.ShapeDtypeStruct((n, 2 * HD), jnp.bfloat16),
        ],
        compiler_params=LIMIT,
        cost_estimate=cost,
    )(core, x, far, total)


def three_parts(value):
    first = value.astype(jnp.bfloat16).astype(jnp.float32)
    rest = value - first
    second = rest.astype(jnp.bfloat16).astype(jnp.float32)
    return first, second, rest - second


def attend_kernel(start_ref, q_ref, near_ref, far_ref, kpos_ref, o_ref, s_ref):
    factor = float(np.log2(np.e) / HD**0.5)
    rows = q_ref.shape[0]
    blocks, half = o_ref.shape[0], o_ref.shape[1] - EXTRA
    row = lax.broadcasted_iota(jnp.int32, (rows, 1), 0)
    first = blocks * pl.program_id(0)
    qpos = row + start_ref[first]
    for b in range(1, blocks):
        qpos = jnp.where(row < b * half, qpos, row - b * half + start_ref[first + b])
    pieces = [
        (ref, j * CHUNK, i * ref.shape[0] + j * CHUNK)
        for i, ref in enumerate((near_ref, far_ref))
        for j in range(ref.shape[0] // CHUNK)
    ]
    q = q_ref[...]
    high = jnp.full((rows, HD), HIDE, jnp.float32)
    for ref, at, column in pieces:
        span = pl.ds(column, CHUNK)
        s = lax.dot_general(
            q, ref[pl.ds(at, CHUNK), :HD], (((1,), (1,)), ((), ())), preferred_element_type=jnp.float32
        )
        s = jnp.where(kpos_ref[:, span] <= qpos, s * factor, HIDE)
        s_ref[:, span] = s
        for t in range(CHUNK // HD):
            high = jnp.maximum(high, s[:, t * HD : (t + 1) * HD])
    top = jnp.max(high, axis=1, keepdims=True)
    base = jnp.where(top <= 0.5 * HIDE, 0.0, top)
    total = jnp.zeros((rows, HD), jnp.float32)
    acc = jnp.zeros((rows, HD), jnp.float32)
    for ref, at, column in pieces:
        span = pl.ds(column, CHUNK)
        p = jnp.exp2(s_ref[:, span] - base)
        for t in range(CHUNK // HD):
            total = total + p[:, t * HD : (t + 1) * HD]
        acc = acc + jnp.dot(
            p.astype(jnp.bfloat16), ref[pl.ds(at, CHUNK), HD:], preferred_element_type=jnp.float32
        )
    total = jnp.sum(total, axis=1, keepdims=True)
    o = acc / jnp.where(total == 0.0, 1.0, total)
    lane = lax.broadcasted_iota(jnp.int32, (rows, HD), 1)
    stat = jnp.zeros((rows, HD), jnp.float32)
    for k, piece in enumerate(three_parts(top) + three_parts(total)):
        stat = jnp.where(lane == k, piece, stat)
    for b in range(blocks):
        o_ref[b, :half, :] = o[b * half : (b + 1) * half].astype(o_ref.dtype)
        block = jnp.concatenate(
            [stat[b * half : (b + 1) * half], jnp.zeros((HD - half, HD), jnp.float32)]
        )
        o_ref[b, half:, :] = block.T[:EXTRA].astype(o_ref.dtype)


def attend(start, q, near, far, kpos, half):
    nq, nk = q.shape[0], 2 * near.shape[0]
    tile = 2 * half
    return pl.pallas_call(
        attend_kernel,
        grid=(nq // tile,),
        in_specs=[
            pl.BlockSpec(memory_space=pltpu.SMEM),
            pl.BlockSpec((tile, HD), lambda i: (i, 0)),
            pl.BlockSpec((nk // 2, 2 * HD), lambda i: (0, 0)),
            pl.BlockSpec((nk // 2, 2 * HD), lambda i: (0, 0)),
            pl.BlockSpec((1, nk), lambda i: (0, 0)),
        ],
        out_specs=pl.BlockSpec((2, half + EXTRA, HD), lambda i: (i, 0, 0)),
        out_shape=jax.ShapeDtypeStruct((nq // half, half + EXTRA, HD), jnp.bfloat16),
        scratch_shapes=[pltpu.VMEM((tile, nk), jnp.float32)],
        compiler_params=LIMIT,
        cost_estimate=pl.CostEstimate(
            flops=4 * nq * nk * HD, bytes_accessed=nk * HD * 4, transcendentals=nq * nk
        ),
    )(start, q, near, far, kpos)


def finish_kernel(c_ref, part_ref, near_ref, far_ref, out_ref):
    count, nx, half = part_ref.shape[0], part_ref.shape[1], part_ref.shape[2] - EXTRA
    context = []
    for x in range(nx):
        tops, totals = [], []
        for k in range(count):
            stat = part_ref[k, x, half:, :].astype(jnp.float32)
            stat = jnp.concatenate([stat, jnp.zeros((HD - EXTRA, HD), jnp.float32)]).T[:half]
            tops.append(stat[:, 0:1] + stat[:, 1:2] + stat[:, 2:3])
            totals.append(stat[:, 3:4] + stat[:, 4:5] + stat[:, 5:6])
        top = tops[0]
        for k in range(1, count):
            top = jnp.maximum(top, tops[k])
        weights = [totals[k] * jnp.exp2(tops[k] - top) for k in range(count)]
        mixed = sum(part_ref[k, x, :half, :].astype(jnp.float32) * weights[k] for k in range(count))
        context.append((mixed / sum(weights)).astype(jnp.bfloat16))
    low = jnp.concatenate([context[0], context[2]], axis=1)
    high = jnp.concatenate([context[1], context[3]], axis=1)
    width = out_ref.shape[2]
    for ref, odd in ((near_ref, c_ref[0]), (far_ref, 1 - c_ref[0])):
        for h in range(2):
            terms = jnp.dot(low, ref[2 * h], preferred_element_type=jnp.float32)
            terms += jnp.dot(high, ref[2 * h + 1], preferred_element_type=jnp.float32)
            terms = terms.astype(out_ref.dtype)
            at = 2 * (2 * h + odd)
            out_ref[at] = terms[:, :width]
            out_ref[at + 1] = terms[:, width:]


def finish(core, parts, mine, other):
    half = parts.shape[2] - EXTRA
    blocks, _, cols = mine.shape
    vmem = pl.BlockSpec(memory_space=pltpu.VMEM)
    return pl.pallas_call(
        finish_kernel,
        in_specs=[pl.BlockSpec(memory_space=pltpu.SMEM), vmem, vmem, vmem],
        out_specs=vmem,
        out_shape=jax.ShapeDtypeStruct((2 * blocks, half, cols // 2), jnp.bfloat16),
        compiler_params=LIMIT,
        cost_estimate=pl.CostEstimate(
            flops=4 * half * mine.size, bytes_accessed=4 * mine.size, transcendentals=0
        ),
    )(core, parts, mine, other)


def swap(block, axis):
    return lax.ppermute(block, axis, [(0, 1), (1, 0)])


def exchange(block, axis):
    return lax.all_to_all(block, axis, 0, 0, tiled=True)


def pick(blocks, index):
    return lax.dynamic_index_in_dim(blocks, index, 0, keepdims=False)


def spread(block, axis):
    count = lax.axis_size(axis)
    return exchange(jnp.broadcast_to(block[None], (count,) + block.shape), axis)


def shift(block, axis, distance):
    count = lax.axis_size(axis)
    return lax.ppermute(block, axis, [(i, (i + distance) % count) for i in range(count)])


def distances(axis):
    count = lax.axis_size(axis)
    return sorted(range(1, count), key=lambda s: -min(s, count - s))


def gather_by_shifts(block, axis):
    here, count = lax.axis_index(axis), lax.axis_size(axis)
    got = {0: block}
    for s in distances(axis):
        got[s] = shift(block, axis, s)
    got = jnp.stack([got[s] for s in range(count)])
    return jnp.stack([pick(got, (here - i) % count) for i in range(count)])


def trade(block, across):
    route = []
    for z in range(2):
        for x in range(4):
            for c in range(2):
                to = ((z ^ across) * 4 + x - x % 2 + c) * 2 + x % 2
                if to != (z * 4 + x) * 2 + c:
                    route.append(((z * 4 + x) * 2 + c, to))
    return lax.ppermute(block, ("zh", "x", "c"), route)


def mirror(block, z, y):
    route = [(i, (i // 2 ^ z) * 2 + (i % 2 ^ y)) for i in range(4)]
    return lax.ppermute(block, ("zh", "yh"), route)


def shards(hidden_in, norm_gain, snap_qkv, snap_out, owner_index, block_order):
    rows, width = hidden_in.shape
    zh, yh, yl, x, c = (lax.axis_index(name) for name in ("zh", "yh", "yl", "x", "c"))
    ny, nx = 8, 4
    ys = ("yh", "yl")
    half = rows // 2
    core = c.reshape(1)
    owner = owner_index[0]
    zh0, y0, x0 = owner // (ny * nx), (owner // nx) % ny, owner % nx

    mine = lax.dynamic_slice_in_dim(hidden_in, c * half, half, 0).astype(jnp.float32)
    normed = (
        mine * lax.rsqrt(jnp.mean(mine * mine, axis=-1, keepdims=True) + 1e-06) * norm_gain
    ).astype(jnp.bfloat16)

    order = block_order.reshape(2, 2, ny // 2, nx) * rows
    offsets = jnp.arange(half, dtype=jnp.int32)
    kpos = (pick(pick(order, zh), yh)[:, :, None] + offsets).reshape(-1)
    kpos = jnp.concatenate([kpos + c * half, kpos + (1 - c) * half]).reshape(1, -1)
    start = lax.dynamic_index_in_dim(order, yl, 2, keepdims=False).reshape(-1) + c * half

    part = width // (2 * ny)
    w = fold(snap_qkv[0], snap_out[0], ny)
    w = pick(exchange(w, "x"), x0)
    w, normed, kpos, start = lax.optimization_barrier((w, normed, kpos, start))
    w = pick(exchange(w, ys), y0)
    normed = gather_by_shifts(normed, "x").reshape(-1, width)
    w, normed = lax.optimization_barrier((w, normed))
    w = jnp.where(zh == zh0, jnp.where(x % 2 == c, w, trade(w, 0)), trade(w, 1))
    w = spread(w, ys).reshape(ny * part, 4 * HD)
    q, kv = project(core, normed, w, swap(w, "c"))
    wo = w[:, 3 * HD :].reshape(ny, nx, part // nx, HD)
    wo = jnp.transpose(wo, (0, 2, 1, 3)).reshape(ny * part // nx, nx * HD)
    q, kv, wo = lax.optimization_barrier((q, kv, wo))

    near = spread(kv, "yl").reshape(-1, 2 * HD)
    other = {(0, 0): q}
    for z, y in ((1, 1), (1, 0), (0, 1)):
        other[z, y] = mirror(q, z, y)
    q_all = []
    for z in range(2):
        for y in range(2):
            same = [jnp.where(yh == y, other[k, 0], other[k, 1]) for k in range(2)]
            q_all.append(jnp.where(zh == z, same[0], same[1]))
    q_all = jnp.concatenate(q_all)
    wo = gather_by_shifts(wo, "x")
    near, q_all, wo = lax.optimization_barrier((near, q_all, wo))
    far = swap(near, "c")
    wo_far = swap(wo, "c")

    parts = attend(start, q_all, near, far, kpos, half)
    parts = exchange(parts, ("zh", "yh", "x")).reshape((4, nx) + parts.shape[1:])
    terms = finish(core, parts, wo, wo_far)
    terms = exchange(terms, ("zl", "c")).reshape(-1, rows, terms.shape[2])
    return jnp.sum(terms.astype(jnp.float32), axis=0).astype(jnp.bfloat16)


def solution(mesh):
    fine = Mesh(mesh.devices.reshape(2, 2, 4, 4, 4, 2), ("zh", "yh", "yl", "x", "zl", "c"))
    ctx, tp = ("zh", "yh", "yl", "x"), ("zl", "c")
    in_specs = (P(ctx, None), P(), P(ctx, None, None, tp), P(ctx, tp, None), P(), P())
    return jax.shard_map(shards, mesh=fine, in_specs=in_specs, out_specs=P(ctx, tp), check_vma=False)
```

```python
import jax
import jax.numpy as jnp
import numpy as np
from jax import lax
from jax.experimental import pallas as pl
from jax.experimental.pallas import tpu as pltpu
from jax.sharding import Mesh
from jax.sharding import PartitionSpec as P

HD = 128
HIDE = -1e30
CHUNK = 640
EXTRA = 16
LIMIT = pltpu.CompilerParams(vmem_limit_bytes=48 * 1024 * 1024)


def fold_kernel(w_ref, wo_ref, kv_ref, rest_ref):
    span, cols = wo_ref.shape[0], wo_ref.shape[1] // 4
    for h in range(2):
        for r in range(2):
            for ref, at, j in ((rest_ref, 0, 0), (kv_ref, 0, 1), (kv_ref, HD, 2)):
                ref[2 * h + r, 0, :, at : at + HD] = w_ref[j, r, :, h * HD : (h + 1) * HD]
    for x in range(4):
        for k in range(4):
            at = x * cols + k * HD
            rest_ref[x, 0, k * span : (k + 1) * span, HD:] = wo_ref[:, at : at + HD]


def fold(w, wo, ny):
    part = w.shape[1] // (2 * ny)
    spec = pl.BlockSpec((4, 1, part, 2 * HD), lambda i: (0, i, 0, 0))
    shape = jax.ShapeDtypeStruct((4, ny, part, 2 * HD), w.dtype)
    return pl.pallas_call(
        fold_kernel,
        grid=(ny,),
        in_specs=[
            pl.BlockSpec((3, 2, part, 2 * HD), lambda i: (0, 0, i, 0)),
            pl.BlockSpec((wo.shape[0] // ny, wo.shape[1]), lambda i: (i, 0)),
        ],
        out_specs=[spec, spec],
        out_shape=[shape, shape],
        compiler_params=LIMIT,
        cost_estimate=pl.CostEstimate(flops=0, bytes_accessed=4 * (w.size + wo.size), transcendentals=0),
    )(w.reshape(3, 2, ny * part, 2 * HD), wo)


def near_kernel(c_ref, x_ref, w_ref, out_ref):
    depth = w_ref.shape[0]
    span = pl.ds(pl.multiple_of(c_ref[0] * depth, depth), depth)
    w = w_ref[:, : out_ref.shape[1]]
    out_ref[...] = jnp.dot(x_ref[:, span], w, preferred_element_type=jnp.float32)


def far_kernel(c_ref, x_ref, w_ref, sum_ref, out_ref):
    depth = w_ref.shape[0]
    span = pl.ds(pl.multiple_of((1 - c_ref[0]) * depth, depth), depth)
    w = w_ref[:, : out_ref.shape[1]]
    out = sum_ref[...] + jnp.dot(x_ref[:, span], w, preferred_element_type=jnp.float32)
    out_ref[...] = out.astype(out_ref.dtype)


def project(core, x, near, far, cols):
    n = x.shape[0]
    smem, vmem = pl.BlockSpec(memory_space=pltpu.SMEM), pl.BlockSpec(memory_space=pltpu.VMEM)
    cost = pl.CostEstimate(
        flops=2 * n * near.shape[0] * cols, bytes_accessed=2 * (x.size + near.size), transcendentals=0
    )
    total = pl.pallas_call(
        near_kernel,
        in_specs=[smem, vmem, vmem],
        out_specs=vmem,
        out_shape=jax.ShapeDtypeStruct((n, cols), jnp.float32),
        compiler_params=LIMIT,
        cost_estimate=cost,
    )(core, x, near)
    return pl.pallas_call(
        far_kernel,
        in_specs=[smem, vmem, vmem, vmem],
        out_specs=vmem,
        out_shape=jax.ShapeDtypeStruct((n, cols), jnp.bfloat16),
        compiler_params=LIMIT,
        cost_estimate=cost,
    )(core, x, far, total)


def three_parts(value):
    first = value.astype(jnp.bfloat16).astype(jnp.float32)
    rest = value - first
    second = rest.astype(jnp.bfloat16).astype(jnp.float32)
    return first, second, rest - second


def attend_kernel(start_ref, q_ref, near_ref, far_ref, kpos_ref, o_ref, s_ref):
    factor = float(np.log2(np.e) / HD**0.5)
    rows = q_ref.shape[0]
    blocks, half = o_ref.shape[0], o_ref.shape[1] - EXTRA
    row = lax.broadcasted_iota(jnp.int32, (rows, 1), 0)
    first = blocks * pl.program_id(0)
    qpos = row + start_ref[first]
    for b in range(1, blocks):
        qpos = jnp.where(row < b * half, qpos, row - b * half + start_ref[first + b])
    pieces = [
        (ref, j * CHUNK, i * ref.shape[0] + j * CHUNK)
        for i, ref in enumerate((near_ref, far_ref))
        for j in range(ref.shape[0] // CHUNK)
    ]
    q = q_ref[...]
    high = jnp.full((rows, HD), HIDE, jnp.float32)
    for ref, at, column in pieces:
        span = pl.ds(column, CHUNK)
        s = lax.dot_general(
            q, ref[pl.ds(at, CHUNK), :HD], (((1,), (1,)), ((), ())), preferred_element_type=jnp.float32
        )
        s = jnp.where(kpos_ref[:, span] <= qpos, s * factor, HIDE)
        s_ref[:, span] = s
        for t in range(CHUNK // HD):
            high = jnp.maximum(high, s[:, t * HD : (t + 1) * HD])
    top = jnp.max(high, axis=1, keepdims=True)
    base = jnp.where(top <= 0.5 * HIDE, 0.0, top)
    total = jnp.zeros((rows, HD), jnp.float32)
    acc = jnp.zeros((rows, HD), jnp.float32)
    for ref, at, column in pieces:
        span = pl.ds(column, CHUNK)
        p = jnp.exp2(s_ref[:, span] - base)
        for t in range(CHUNK // HD):
            total = total + p[:, t * HD : (t + 1) * HD]
        acc = acc + jnp.dot(
            p.astype(jnp.bfloat16), ref[pl.ds(at, CHUNK), HD:], preferred_element_type=jnp.float32
        )
    total = jnp.sum(total, axis=1, keepdims=True)
    o = acc / jnp.where(total == 0.0, 1.0, total)
    lane = lax.broadcasted_iota(jnp.int32, (rows, HD), 1)
    stat = jnp.zeros((rows, HD), jnp.float32)
    for k, piece in enumerate(three_parts(top) + three_parts(total)):
        stat = jnp.where(lane == k, piece, stat)
    for b in range(blocks):
        o_ref[b, :half, :] = o[b * half : (b + 1) * half].astype(o_ref.dtype)
        block = jnp.concatenate(
            [stat[b * half : (b + 1) * half], jnp.zeros((HD - half, HD), jnp.float32)]
        )
        o_ref[b, half:, :] = block.T[:EXTRA].astype(o_ref.dtype)


def attend(start, q, near, far, kpos, half):
    nq, nk = q.shape[0], 2 * near.shape[0]
    tile = 2 * half
    return pl.pallas_call(
        attend_kernel,
        grid=(nq // tile,),
        in_specs=[
            pl.BlockSpec(memory_space=pltpu.SMEM),
            pl.BlockSpec((tile, HD), lambda i: (i, 0)),
            pl.BlockSpec((nk // 2, 2 * HD), lambda i: (0, 0)),
            pl.BlockSpec((nk // 2, 2 * HD), lambda i: (0, 0)),
            pl.BlockSpec((1, nk), lambda i: (0, 0)),
        ],
        out_specs=pl.BlockSpec((2, half + EXTRA, HD), lambda i: (i, 0, 0)),
        out_shape=jax.ShapeDtypeStruct((nq // half, half + EXTRA, HD), jnp.bfloat16),
        scratch_shapes=[pltpu.VMEM((tile, nk), jnp.float32)],
        compiler_params=LIMIT,
        cost_estimate=pl.CostEstimate(
            flops=4 * nq * nk * HD, bytes_accessed=nk * HD * 4, transcendentals=nq * nk
        ),
    )(start, q, near, far, kpos)


def finish_kernel(c_ref, part_ref, near_ref, far_ref, out_ref):
    count, nx, half = part_ref.shape[0], part_ref.shape[1], part_ref.shape[2] - EXTRA
    context = []
    for x in range(nx):
        tops, totals = [], []
        for k in range(count):
            stat = part_ref[k, x, half:, :].astype(jnp.float32)
            stat = jnp.concatenate([stat, jnp.zeros((HD - EXTRA, HD), jnp.float32)]).T[:half]
            tops.append(stat[:, 0:1] + stat[:, 1:2] + stat[:, 2:3])
            totals.append(stat[:, 3:4] + stat[:, 4:5] + stat[:, 5:6])
        top = tops[0]
        for k in range(1, count):
            top = jnp.maximum(top, tops[k])
        weights = [totals[k] * jnp.exp2(tops[k] - top) for k in range(count)]
        mixed = sum(part_ref[k, x, :half, :].astype(jnp.float32) * weights[k] for k in range(count))
        context.append((mixed / sum(weights)).astype(jnp.bfloat16))
    low = jnp.concatenate([context[0], context[2]], axis=1)
    high = jnp.concatenate([context[1], context[3]], axis=1)
    width = out_ref.shape[2]
    for ref, odd in ((near_ref, c_ref[0]), (far_ref, 1 - c_ref[0])):
        for h in range(2):
            terms = jnp.dot(low, ref[2 * h], preferred_element_type=jnp.float32)
            terms += jnp.dot(high, ref[2 * h + 1], preferred_element_type=jnp.float32)
            terms = terms.astype(out_ref.dtype)
            at = 2 * (2 * h + odd)
            out_ref[at] = terms[:, :width]
            out_ref[at + 1] = terms[:, width:]


def finish(core, parts, mine, other):
    half = parts.shape[2] - EXTRA
    blocks, _, cols = mine.shape
    vmem = pl.BlockSpec(memory_space=pltpu.VMEM)
    return pl.pallas_call(
        finish_kernel,
        in_specs=[pl.BlockSpec(memory_space=pltpu.SMEM), vmem, vmem, vmem],
        out_specs=vmem,
        out_shape=jax.ShapeDtypeStruct((2 * blocks, half, cols // 2), jnp.bfloat16),
        compiler_params=LIMIT,
        cost_estimate=pl.CostEstimate(
            flops=4 * half * mine.size, bytes_accessed=4 * mine.size, transcendentals=0
        ),
    )(core, parts, mine, other)


def swap(block, axis):
    return lax.ppermute(block, axis, [(0, 1), (1, 0)])


def exchange(block, axis):
    return lax.all_to_all(block, axis, 0, 0, tiled=True)


def pick(blocks, index):
    return lax.dynamic_index_in_dim(blocks, index, 0, keepdims=False)


def copies(block, axis):
    return jnp.broadcast_to(block[None], (lax.axis_size(axis),) + block.shape)


def shift(block, axis, distance):
    count = lax.axis_size(axis)
    return lax.ppermute(block, axis, [(i, (i + distance) % count) for i in range(count)])


def distances(axis):
    count = lax.axis_size(axis)
    return sorted(range(1, count), key=lambda s: -min(s, count - s))


def scatter_by_shifts(blocks, axis, source):
    here, count = lax.axis_index(axis), blocks.shape[0]
    result = pick(blocks, here)
    for s in distances(axis):
        got = shift(pick(blocks, (here + s) % count), axis, s)
        result = jnp.where((here - source) % count == s, got, result)
    return result


def in_order(got, axis):
    here, count = lax.axis_index(axis), len(got)
    got = jnp.stack(got)
    return jnp.stack([pick(got, (here - i) % count) for i in range(count)])


def gather_by_shifts(block, axis):
    got = {s: shift(block, axis, s) for s in distances(axis)}
    return in_order([block] + [got[s + 1] for s in range(len(got))], axis)


def trade(block, across):
    route = []
    for z in range(2):
        for x in range(4):
            for c in range(2):
                to = ((z ^ across) * 4 + x - x % 2 + c) * 2 + x % 2
                if to != (z * 4 + x) * 2 + c:
                    route.append(((z * 4 + x) * 2 + c, to))
    return lax.ppermute(block, ("zh", "x", "c"), route)


def shards(hidden_in, norm_gain, snap_qkv, snap_out, owner_index, block_order):
    rows, width = hidden_in.shape
    zh, y, x, c = (lax.axis_index(name) for name in ("zh", "y", "x", "c"))
    ny, nx = 8, 4
    half = rows // 2
    core = c.reshape(1)
    owner = owner_index[0]
    zh0, y0, x0 = owner // (ny * nx), (owner // nx) % ny, owner % nx

    def across(block):
        return jnp.where(zh == zh0, jnp.where(x % 2 == c, block, trade(block, 0)), trade(block, 1))

    mine = lax.dynamic_slice_in_dim(hidden_in, c * half, half, 0).astype(jnp.float32)
    normed = (
        mine * lax.rsqrt(jnp.mean(mine * mine, axis=-1, keepdims=True) + 1e-06) * norm_gain
    ).astype(jnp.bfloat16)

    order = block_order.reshape(2, ny, nx) * rows
    offsets = jnp.arange(half, dtype=jnp.int32)
    kpos = (pick(order, zh)[:, :, None] + offsets).reshape(-1)
    kpos = jnp.concatenate([kpos + c * half, kpos + (1 - c) * half]).reshape(1, -1)
    start = lax.dynamic_index_in_dim(order, y, 1, keepdims=False).reshape(-1) + c * half

    part = width // (2 * ny)
    a, b = fold(snap_qkv[0], snap_out[0], ny)
    a = pick(exchange(a, "x"), x0)
    third = shift(normed, "x", 3)
    a, b, normed, third, kpos, start = lax.optimization_barrier((a, b, normed, third, kpos, start))
    a = pick(exchange(a, "y"), y0)
    b = scatter_by_shifts(b, "x", x0)
    a, b, normed = lax.optimization_barrier((a, b, normed))
    a = copies(across(a), "y")
    b = pick(exchange(b, "y"), y0)
    first, second = shift(normed, "x", 1), shift(normed, "x", 2)
    a, b, normed, first, second = lax.optimization_barrier((a, b, normed, first, second))
    a = exchange(a, "y").reshape(ny * part, 2 * HD)
    b = copies(across(b), "y")
    normed = in_order([normed, first, second, third], "x").reshape(-1, width)
    a, b, normed = lax.optimization_barrier((a, b, normed))
    kv = copies(project(core, normed, a, swap(a, "c"), 2 * HD), "y")
    b = exchange(b, "y").reshape(ny * part, 2 * HD)
    kv, b = lax.optimization_barrier((kv, b))

    near = exchange(kv, "y").reshape(-1, 2 * HD)
    q = project(core, normed, b, swap(b, "c"), HD)
    q_other = swap(q, "zh")
    q_all = jnp.concatenate([jnp.where(zh == 0, q, q_other), jnp.where(zh == 0, q_other, q)])
    wo = b[:, HD:].reshape(ny, nx, part // nx, HD)
    wo = jnp.transpose(wo, (0, 2, 1, 3)).reshape(ny * part // nx, nx * HD)
    wo = gather_by_shifts(wo, "x")
    near, q_all, wo = lax.optimization_barrier((near, q_all, wo))
    far = swap(near, "c")
    wo_far = swap(wo, "c")

    parts = attend(start, q_all, near, far, kpos, half)
    parts = exchange(parts, ("zh", "x")).reshape((2, nx) + parts.shape[1:])
    terms = finish(core, parts, wo, wo_far)
    terms = exchange(terms, ("zl", "c")).reshape(-1, rows, terms.shape[2])
    return jnp.sum(terms.astype(jnp.float32), axis=0).astype(jnp.bfloat16)


def solution(mesh):
    fine = Mesh(mesh.devices.reshape(2, 8, 4, 4, 2), ("zh", "y", "x", "zl", "c"))
    ctx, tp = ("zh", "y", "x"), ("zl", "c")
    in_specs = (P(ctx, None), P(), P(ctx, None, None, tp), P(ctx, tp, None), P(), P())
    return jax.shard_map(shards, mesh=fine, in_specs=in_specs, out_specs=P(ctx, tp), check_vma=False)
```

```python
import jax
import jax.numpy as jnp
import numpy as np
from jax import lax
from jax.experimental import pallas as pl
from jax.experimental.pallas import tpu as pltpu
from jax.sharding import Mesh
from jax.sharding import PartitionSpec as P

HD = 128
HIDE = -1e30
CHUNK = 640
EXTRA = 16
LIMIT = pltpu.CompilerParams(vmem_limit_bytes=48 * 1024 * 1024)


def fold_kernel(w_ref, out_ref):
    for h in range(2):
        for r in range(2):
            for j in range(3):
                out_ref[2 * h + r, 0, :, j * HD : (j + 1) * HD] = w_ref[j, r, :, h * HD : (h + 1) * HD]


def fold(w, ny):
    part = w.shape[1] // (2 * ny)
    return pl.pallas_call(
        fold_kernel,
        grid=(ny,),
        in_specs=[pl.BlockSpec((3, 2, part, 2 * HD), lambda i: (0, 0, i, 0))],
        out_specs=pl.BlockSpec((4, 1, part, 3 * HD), lambda i: (0, i, 0, 0)),
        out_shape=jax.ShapeDtypeStruct((4, ny, part, 3 * HD), w.dtype),
        compiler_params=LIMIT,
        cost_estimate=pl.CostEstimate(flops=0, bytes_accessed=4 * w.size, transcendentals=0),
    )(w.reshape(3, 2, ny * part, 2 * HD))


def near_kernel(c_ref, x_ref, w_ref, out_ref):
    depth = w_ref.shape[0]
    span = pl.ds(pl.multiple_of(c_ref[0] * depth, depth), depth)
    w = w_ref[:, : out_ref.shape[1]]
    out_ref[...] = jnp.dot(x_ref[:, span], w, preferred_element_type=jnp.float32)


def far_kernel(c_ref, x_ref, w_ref, sum_ref, q_ref, kv_ref):
    depth = w_ref.shape[0]
    span = pl.ds(pl.multiple_of((1 - c_ref[0]) * depth, depth), depth)
    w = w_ref[:, : sum_ref.shape[1]]
    out = sum_ref[...] + jnp.dot(x_ref[:, span], w, preferred_element_type=jnp.float32)
    q_ref[...] = out[:, :HD].astype(q_ref.dtype)
    kv_ref[...] = out[:, HD:].astype(kv_ref.dtype)


def project(core, x, near, far):
    n, cols = x.shape[0], 3 * HD
    smem, vmem = pl.BlockSpec(memory_space=pltpu.SMEM), pl.BlockSpec(memory_space=pltpu.VMEM)
    cost = pl.CostEstimate(
        flops=2 * n * near.shape[0] * cols, bytes_accessed=2 * (x.size + near.size), transcendentals=0
    )
    total = pl.pallas_call(
        near_kernel,
        in_specs=[smem, vmem, vmem],
        out_specs=vmem,
        out_shape=jax.ShapeDtypeStruct((n, cols), jnp.float32),
        compiler_params=LIMIT,
        cost_estimate=cost,
    )(core, x, near)
    return pl.pallas_call(
        far_kernel,
        in_specs=[smem, vmem, vmem, vmem],
        out_specs=[vmem, vmem],
        out_shape=[
            jax.ShapeDtypeStruct((n, HD), jnp.bfloat16),
            jax.ShapeDtypeStruct((n, 2 * HD), jnp.bfloat16),
        ],
        compiler_params=LIMIT,
        cost_estimate=cost,
    )(core, x, far, total)


def three_parts(value):
    first = value.astype(jnp.bfloat16).astype(jnp.float32)
    rest = value - first
    second = rest.astype(jnp.bfloat16).astype(jnp.float32)
    return first, second, rest - second


def attend_kernel(start_ref, q_ref, near_ref, far_ref, kpos_ref, o_ref, s_ref):
    factor = float(np.log2(np.e) / HD**0.5)
    rows = q_ref.shape[0]
    blocks, half = o_ref.shape[0], o_ref.shape[1] - EXTRA
    row = lax.broadcasted_iota(jnp.int32, (rows, 1), 0)
    first = blocks * pl.program_id(0)
    qpos = row + start_ref[first]
    for b in range(1, blocks):
        qpos = jnp.where(row < b * half, qpos, row - b * half + start_ref[first + b])
    pieces = [
        (ref, j * CHUNK, i * ref.shape[0] + j * CHUNK)
        for i, ref in enumerate((near_ref, far_ref))
        for j in range(ref.shape[0] // CHUNK)
    ]
    q = q_ref[...]
    high = jnp.full((rows, HD), HIDE, jnp.float32)
    for ref, at, column in pieces:
        span = pl.ds(column, CHUNK)
        s = lax.dot_general(
            q, ref[pl.ds(at, CHUNK), :HD], (((1,), (1,)), ((), ())), preferred_element_type=jnp.float32
        )
        s = jnp.where(kpos_ref[:, span] <= qpos, s * factor, HIDE)
        s_ref[:, span] = s
        for t in range(CHUNK // HD):
            high = jnp.maximum(high, s[:, t * HD : (t + 1) * HD])
    top = jnp.max(high, axis=1, keepdims=True)
    base = jnp.where(top <= 0.5 * HIDE, 0.0, top)
    total = jnp.zeros((rows, HD), jnp.float32)
    acc = jnp.zeros((rows, HD), jnp.float32)
    for ref, at, column in pieces:
        span = pl.ds(column, CHUNK)
        p = jnp.exp2(s_ref[:, span] - base)
        for t in range(CHUNK // HD):
            total = total + p[:, t * HD : (t + 1) * HD]
        acc = acc + jnp.dot(
            p.astype(jnp.bfloat16), ref[pl.ds(at, CHUNK), HD:], preferred_element_type=jnp.float32
        )
    total = jnp.sum(total, axis=1, keepdims=True)
    o = acc / jnp.where(total == 0.0, 1.0, total)
    lane = lax.broadcasted_iota(jnp.int32, (rows, HD), 1)
    stat = jnp.zeros((rows, HD), jnp.float32)
    for k, piece in enumerate(three_parts(top) + three_parts(total)):
        stat = jnp.where(lane == k, piece, stat)
    for b in range(blocks):
        o_ref[b, :half, :] = o[b * half : (b + 1) * half].astype(o_ref.dtype)
        block = jnp.concatenate(
            [stat[b * half : (b + 1) * half], jnp.zeros((HD - half, HD), jnp.float32)]
        )
        o_ref[b, half:, :] = block.T[:EXTRA].astype(o_ref.dtype)


def attend(start, q, near, far, kpos, half):
    nq, nk = q.shape[0], 2 * near.shape[0]
    tile = 2 * half
    return pl.pallas_call(
        attend_kernel,
        grid=(nq // tile,),
        in_specs=[
            pl.BlockSpec(memory_space=pltpu.SMEM),
            pl.BlockSpec((tile, HD), lambda i: (i, 0)),
            pl.BlockSpec((nk // 2, 2 * HD), lambda i: (0, 0)),
            pl.BlockSpec((nk // 2, 2 * HD), lambda i: (0, 0)),
            pl.BlockSpec((1, nk), lambda i: (0, 0)),
        ],
        out_specs=pl.BlockSpec((2, half + EXTRA, HD), lambda i: (i, 0, 0)),
        out_shape=jax.ShapeDtypeStruct((nq // half, half + EXTRA, HD), jnp.bfloat16),
        scratch_shapes=[pltpu.VMEM((tile, nk), jnp.float32)],
        compiler_params=LIMIT,
        cost_estimate=pl.CostEstimate(
            flops=4 * nq * nk * HD, bytes_accessed=nk * HD * 4, transcendentals=nq * nk
        ),
    )(start, q, near, far, kpos)


def merge_kernel(near_ref, far_ref, out_ref):
    nx, half = out_ref.shape[0], out_ref.shape[1]
    for x in range(nx):
        tops, totals = [], []
        for ref in (near_ref, far_ref):
            stat = ref[x, half:, :].astype(jnp.float32)
            stat = jnp.concatenate([stat, jnp.zeros((HD - EXTRA, HD), jnp.float32)]).T[:half]
            tops.append(stat[:, 0:1] + stat[:, 1:2] + stat[:, 2:3])
            totals.append(stat[:, 3:4] + stat[:, 4:5] + stat[:, 5:6])
        top = jnp.maximum(tops[0], tops[1])
        a = totals[0] * jnp.exp2(tops[0] - top)
        b = totals[1] * jnp.exp2(tops[1] - top)
        mixed = near_ref[x, :half, :].astype(jnp.float32) * a + far_ref[x, :half, :].astype(jnp.float32) * b
        out_ref[x] = (mixed / (a + b)).astype(out_ref.dtype)


def merge(near, far):
    nx, rows = near.shape[0], near.shape[1] - EXTRA
    vmem = pl.BlockSpec(memory_space=pltpu.VMEM)
    return pl.pallas_call(
        merge_kernel,
        in_specs=[vmem, vmem],
        out_specs=vmem,
        out_shape=jax.ShapeDtypeStruct((nx, rows, HD), jnp.bfloat16),
        compiler_params=LIMIT,
        cost_estimate=pl.CostEstimate(flops=8 * near.size, bytes_accessed=6 * near.size, transcendentals=0),
    )(near, far)


def finish_kernel(c_ref, context_ref, near_ref, far_ref, out_ref):
    low = jnp.concatenate([context_ref[0], context_ref[2]], axis=1)
    high = jnp.concatenate([context_ref[1], context_ref[3]], axis=1)
    width = out_ref.shape[2]
    for ref, odd in ((near_ref, c_ref[0]), (far_ref, 1 - c_ref[0])):
        for h in range(2):
            terms = jnp.dot(low, ref[2 * h], preferred_element_type=jnp.float32)
            terms += jnp.dot(high, ref[2 * h + 1], preferred_element_type=jnp.float32)
            terms = terms.astype(out_ref.dtype)
            at = 2 * (2 * h + odd)
            out_ref[at] = terms[:, :width]
            out_ref[at + 1] = terms[:, width:]


def finish(core, context, near, far):
    half = context.shape[1]
    blocks, _, cols = near.shape
    vmem = pl.BlockSpec(memory_space=pltpu.VMEM)
    return pl.pallas_call(
        finish_kernel,
        in_specs=[pl.BlockSpec(memory_space=pltpu.SMEM), vmem, vmem, vmem],
        out_specs=vmem,
        out_shape=jax.ShapeDtypeStruct((2 * blocks, half, cols // 2), jnp.bfloat16),
        compiler_params=LIMIT,
        cost_estimate=pl.CostEstimate(
            flops=4 * half * near.size, bytes_accessed=4 * near.size, transcendentals=0
        ),
    )(core, context, near, far)


def swap(block, axis):
    return lax.ppermute(block, axis, [(0, 1), (1, 0)])


def exchange(block, axis):
    return lax.all_to_all(block, axis, 0, 0, tiled=True)


def pick(blocks, index):
    return lax.dynamic_index_in_dim(blocks, index, 0, keepdims=False)


def spread(block, axis):
    count = lax.axis_size(axis)
    return exchange(jnp.broadcast_to(block[None], (count,) + block.shape), axis)


def shift(block, axis, distance):
    count = lax.axis_size(axis)
    return lax.ppermute(block, axis, [(i, (i + distance) % count) for i in range(count)])


def distances(axis):
    count = lax.axis_size(axis)
    return sorted(range(1, count), key=lambda s: -min(s, count - s))


def scatter_by_shifts(blocks, axis, source):
    here, count = lax.axis_index(axis), blocks.shape[0]
    result = pick(blocks, here)
    for s in distances(axis):
        got = shift(pick(blocks, (here + s) % count), axis, s)
        result = jnp.where((here - source) % count == s, got, result)
    return result


def gather_by_shifts(block, axis):
    here, count = lax.axis_index(axis), lax.axis_size(axis)
    got = {0: block}
    for s in distances(axis):
        got[s] = shift(block, axis, s)
    got = jnp.stack([got[s] for s in range(count)])
    return jnp.stack([pick(got, (here - i) % count) for i in range(count)])


def trade(block, across):
    route = []
    for z in range(2):
        for x in range(4):
            for low in range(4):
                for c in range(2):
                    to_low = 3 - low if across else low
                    to = (((z ^ across) * 4 + x - x % 2 + c) * 4 + to_low) * 2 + x % 2
                    here = ((z * 4 + x) * 4 + low) * 2 + c
                    if to != here:
                        route.append((here, to))
    return lax.ppermute(block, ("zh", "x", "zl", "c"), route)


def mirror(block):
    return lax.ppermute(block, ("zh", "zl"), [(i, 7 - i) for i in range(8)])


def shards(hidden_in, norm_gain, snap_qkv, snap_out, owner_index, block_order):
    rows, width = hidden_in.shape
    zh, y, x, c = (lax.axis_index(name) for name in ("zh", "y", "x", "c"))
    ny, nx = 8, 4
    half = rows // 2
    core = c.reshape(1)
    owner = owner_index[0]
    zh0, y0, x0 = owner // (ny * nx), (owner // nx) % ny, owner % nx

    mine = lax.dynamic_slice_in_dim(hidden_in, c * half, half, 0).astype(jnp.float32)
    normed = (
        mine * lax.rsqrt(jnp.mean(mine * mine, axis=-1, keepdims=True) + 1e-06) * norm_gain
    ).astype(jnp.bfloat16)

    order = block_order.reshape(2, ny, nx) * rows
    offsets = jnp.arange(half, dtype=jnp.int32)
    kpos = (pick(order, zh)[:, :, None] + offsets).reshape(-1)
    kpos = jnp.concatenate([kpos + c * half, kpos + (1 - c) * half]).reshape(1, -1)
    here = lax.dynamic_index_in_dim(order, y, 1, keepdims=False)
    start = jnp.stack([pick(here, zh), pick(here, 1 - zh)]).reshape(-1) + c * half

    part = width // (2 * ny)
    w = fold(snap_qkv[0], ny)
    w = pick(exchange(w, "x"), x0)
    wo = scatter_by_shifts(snap_out[0].reshape(ny, -1, snap_out.shape[2]), "y", y0)
    w, wo, normed, kpos, start = lax.optimization_barrier((w, wo, normed, kpos, start))
    w = pick(exchange(w, "y"), y0)
    wo = jnp.transpose(wo.reshape(wo.shape[0], nx, -1), (1, 0, 2))
    wo = scatter_by_shifts(wo, "x", x0)
    wo = jnp.transpose(wo.reshape(wo.shape[0], nx, HD), (1, 0, 2)).reshape(part, HD)
    w = jnp.concatenate([w, wo], axis=1)
    w, normed = lax.optimization_barrier((w, normed))
    w = jnp.where(zh == zh0, jnp.where(x % 2 == c, w, trade(w, 0)), trade(w, 1))
    w = spread(w, "y").reshape(ny * part, 4 * HD)
    normed = gather_by_shifts(normed, "x").reshape(-1, width)
    q, kv = project(core, normed, w, swap(w, "c"))
    wo = w[:, 3 * HD :].reshape(ny, nx, part // nx, HD)
    wo = jnp.transpose(wo, (0, 2, 1, 3)).reshape(ny * part // nx, nx * HD)
    q, kv, wo = lax.optimization_barrier((q, kv, wo))

    near = spread(kv, "y").reshape(-1, 2 * HD)
    q_all = jnp.concatenate([q, mirror(q)])
    wo = gather_by_shifts(wo, "x")
    near, q_all, wo = lax.optimization_barrier((near, q_all, wo))
    far = swap(near, "c")
    wo_far = swap(wo, "c")

    parts = attend(start, q_all, near, far, kpos, half)
    context = merge(parts[:nx], mirror(parts[nx:]))
    context = exchange(context, "x")
    terms = finish(core, context, wo, wo_far)
    terms = exchange(terms, ("zl", "c")).reshape(-1, rows, terms.shape[2])
    return jnp.sum(terms.astype(jnp.float32), axis=0).astype(jnp.bfloat16)


def solution(mesh):
    fine = Mesh(mesh.devices.reshape(2, 8, 4, 4, 2), ("zh", "y", "x", "zl", "c"))
    ctx, tp = ("zh", "y", "x"), ("zl", "c")
    in_specs = (P(ctx, None), P(), P(ctx, None, None, tp), P(ctx, tp, None), P(), P())
    return jax.shard_map(shards, mesh=fine, in_specs=in_specs, out_specs=P(ctx, tp), check_vma=False)
```

```python
import functools

import jax
import jax.numpy as jnp
import numpy as np
from jax import lax
from jax.experimental import pallas as pl
from jax.experimental.pallas import tpu as pltpu
from jax.sharding import Mesh
from jax.sharding import PartitionSpec as P

HD = 128
HIDE = -1e30
CHUNK = 640
EXTRA = 16
LIMIT = pltpu.CompilerParams(vmem_limit_bytes=48 * 1024 * 1024)


def fold_kernel(w_ref, out_ref, done):
    copies = []
    for h in range(2):
        for r in range(2):
            for j in range(3):
                copies.append(
                    pltpu.make_async_copy(
                        w_ref.at[j, r, :, :, pl.ds(h * HD, HD)],
                        out_ref.at[2 * h + r, :, :, pl.ds(j * HD, HD)],
                        done.at[len(copies)],
                    )
                )
    for copy in copies:
        copy.start()
    for copy in copies:
        copy.wait()


def fold(w, ny):
    part = w.shape[1] // (2 * ny)
    return pl.pallas_call(
        fold_kernel,
        in_specs=[pl.BlockSpec(memory_space=pl.ANY)],
        out_specs=pl.BlockSpec(memory_space=pl.ANY),
        out_shape=jax.ShapeDtypeStruct((4, ny, part, 3 * HD), w.dtype),
        scratch_shapes=[pltpu.SemaphoreType.DMA((12,))],
        cost_estimate=pl.CostEstimate(flops=0, bytes_accessed=4 * w.size, transcendentals=0),
    )(w.reshape(3, 2, ny, part, 2 * HD))


def near_kernel(c_ref, x_ref, w_ref, out_ref):
    depth = w_ref.shape[0]
    span = pl.ds(pl.multiple_of(c_ref[0] * depth, depth), depth)
    w = w_ref[:, : out_ref.shape[1]]
    out_ref[...] = jnp.dot(x_ref[:, span], w, preferred_element_type=jnp.float32)


def far_kernel(c_ref, x_ref, w_ref, sum_ref, q_ref, kv_ref):
    depth = w_ref.shape[0]
    span = pl.ds(pl.multiple_of((1 - c_ref[0]) * depth, depth), depth)
    w = w_ref[:, : sum_ref.shape[1]]
    out = sum_ref[...] + jnp.dot(x_ref[:, span], w, preferred_element_type=jnp.float32)
    q_ref[...] = out[:, :HD].astype(q_ref.dtype)
    kv_ref[...] = out[:, HD:].astype(kv_ref.dtype)


def project(core, x, near, far):
    n, cols = x.shape[0], 3 * HD
    smem, vmem = pl.BlockSpec(memory_space=pltpu.SMEM), pl.BlockSpec(memory_space=pltpu.VMEM)
    cost = pl.CostEstimate(
        flops=2 * n * near.shape[0] * cols, bytes_accessed=2 * (x.size + near.size), transcendentals=0
    )
    total = pl.pallas_call(
        near_kernel,
        in_specs=[smem, vmem, vmem],
        out_specs=vmem,
        out_shape=jax.ShapeDtypeStruct((n, cols), jnp.float32),
        compiler_params=LIMIT,
        cost_estimate=cost,
    )(core, x, near)
    return pl.pallas_call(
        far_kernel,
        in_specs=[smem, vmem, vmem, vmem],
        out_specs=[vmem, vmem],
        out_shape=[
            jax.ShapeDtypeStruct((n, HD), jnp.bfloat16),
            jax.ShapeDtypeStruct((n, 2 * HD), jnp.bfloat16),
        ],
        compiler_params=LIMIT,
        cost_estimate=cost,
    )(core, x, far, total)


def three_parts(value):
    first = value.astype(jnp.bfloat16).astype(jnp.float32)
    rest = value - first
    second = rest.astype(jnp.bfloat16).astype(jnp.float32)
    return first, second, rest - second


def positions(start_ref, rows, half):
    blocks = rows // half
    row = lax.broadcasted_iota(jnp.int32, (rows, 1), 0)
    first = blocks * pl.program_id(0)
    qpos = row + start_ref[first]
    for b in range(1, blocks):
        qpos = jnp.where(row < b * half, qpos, row - b * half + start_ref[first + b])
    return qpos


def score(q, qpos, kv_ref, kpos_ref, s_ref):
    factor = float(np.log2(np.e) / HD**0.5)
    high = jnp.full((q.shape[0], HD), HIDE, jnp.float32)
    for j in range(kv_ref.shape[0] // CHUNK):
        span = pl.ds(j * CHUNK, CHUNK)
        s = lax.dot_general(
            q, kv_ref[span, :HD], (((1,), (1,)), ((), ())), preferred_element_type=jnp.float32
        )
        s = jnp.where(kpos_ref[:, span] <= qpos, s * factor, HIDE)
        s_ref[:, span] = s
        for t in range(CHUNK // HD):
            high = jnp.maximum(high, s[:, t * HD : (t + 1) * HD])
    return jnp.max(high, axis=1, keepdims=True)


def weigh(top, kv_ref, s_ref):
    rows = s_ref.shape[0]
    base = jnp.where(top <= 0.5 * HIDE, 0.0, top)
    total = jnp.zeros((rows, HD), jnp.float32)
    acc = jnp.zeros((rows, HD), jnp.float32)
    for j in range(kv_ref.shape[0] // CHUNK):
        span = pl.ds(j * CHUNK, CHUNK)
        p = jnp.exp2(s_ref[:, span] - base)
        for t in range(CHUNK // HD):
            total = total + p[:, t * HD : (t + 1) * HD]
        acc = acc + jnp.dot(
            p.astype(jnp.bfloat16), kv_ref[span, HD:], preferred_element_type=jnp.float32
        )
    return jnp.sum(total, axis=1, keepdims=True), acc


def attend_near_kernel(half, start_ref, q_ref, kv_ref, kpos_ref, acc_ref, stat_ref, s_ref):
    rows = q_ref.shape[0]
    top = score(q_ref[...], positions(start_ref, rows, half), kv_ref, kpos_ref, s_ref)
    total, acc_ref[...] = weigh(top, kv_ref, s_ref)
    lane = lax.broadcasted_iota(jnp.int32, (rows, HD), 1)
    stat_ref[...] = jnp.where(lane == 0, top, total)


def attend_far_kernel(half, start_ref, q_ref, kv_ref, kpos_ref, acc_ref, stat_ref, o_ref, s_ref):
    rows = q_ref.shape[0]
    top = score(q_ref[...], positions(start_ref, rows, half), kv_ref, kpos_ref, s_ref)
    before = stat_ref[:, 0:1]
    top = jnp.maximum(top, before)
    total, acc = weigh(top, kv_ref, s_ref)
    keep = jnp.exp2(before - top)
    total = total + stat_ref[:, 1:2] * keep
    acc = acc + acc_ref[...] * keep
    o = acc / jnp.where(total == 0.0, 1.0, total)
    lane = lax.broadcasted_iota(jnp.int32, (rows, HD), 1)
    stat = jnp.zeros((rows, HD), jnp.float32)
    for k, piece in enumerate(three_parts(top) + three_parts(total)):
        stat = jnp.where(lane == k, piece, stat)
    for b in range(o_ref.shape[0]):
        o_ref[b, :half, :] = o[b * half : (b + 1) * half].astype(o_ref.dtype)
        block = jnp.concatenate(
            [stat[b * half : (b + 1) * half], jnp.zeros((HD - half, HD), jnp.float32)]
        )
        o_ref[b, half:, :] = block.T[:EXTRA].astype(o_ref.dtype)


def attend(start, q, kv, kpos, half, state=None):
    nq, nk = q.shape[0], kv.shape[0]
    tile = 2 * half
    row = pl.BlockSpec((tile, HD), lambda i: (i, 0))
    in_specs = [
        pl.BlockSpec(memory_space=pltpu.SMEM),
        row,
        pl.BlockSpec((nk, 2 * HD), lambda i: (0, 0)),
        pl.BlockSpec((1, nk), lambda i: (0, 0)),
    ]
    if state is None:
        body, state = attend_near_kernel, ()
        out_specs, out_shape = [row, row], [jax.ShapeDtypeStruct((nq, HD), jnp.float32)] * 2
    else:
        body = attend_far_kernel
        out_specs = pl.BlockSpec((2, half + EXTRA, HD), lambda i: (i, 0, 0))
        out_shape = jax.ShapeDtypeStruct((nq // half, half + EXTRA, HD), jnp.bfloat16)
    return pl.pallas_call(
        functools.partial(body, half),
        grid=(nq // tile,),
        in_specs=in_specs + [row] * len(state),
        out_specs=out_specs,
        out_shape=out_shape,
        scratch_shapes=[pltpu.VMEM((tile, nk), jnp.float32)],
        compiler_params=LIMIT,
        cost_estimate=pl.CostEstimate(
            flops=4 * nq * nk * HD, bytes_accessed=nk * HD * 4, transcendentals=nq * nk
        ),
    )(start, q, kv, kpos, *state)


def merge_kernel(near_ref, far_ref, out_ref):
    nx, half = out_ref.shape[0], out_ref.shape[1]
    for x in range(nx):
        tops, totals = [], []
        for ref in (near_ref, far_ref):
            stat = ref[x, half:, :].astype(jnp.float32)
            stat = jnp.concatenate([stat, jnp.zeros((HD - EXTRA, HD), jnp.float32)]).T[:half]
            tops.append(stat[:, 0:1] + stat[:, 1:2] + stat[:, 2:3])
            totals.append(stat[:, 3:4] + stat[:, 4:5] + stat[:, 5:6])
        top = jnp.maximum(tops[0], tops[1])
        a = totals[0] * jnp.exp2(tops[0] - top)
        b = totals[1] * jnp.exp2(tops[1] - top)
        mixed = near_ref[x, :half, :].astype(jnp.float32) * a + far_ref[x, :half, :].astype(jnp.float32) * b
        out_ref[x] = (mixed / (a + b)).astype(out_ref.dtype)


def merge(near, far):
    nx, rows = near.shape[0], near.shape[1] - EXTRA
    vmem = pl.BlockSpec(memory_space=pltpu.VMEM)
    return pl.pallas_call(
        merge_kernel,
        in_specs=[vmem, vmem],
        out_specs=vmem,
        out_shape=jax.ShapeDtypeStruct((nx, rows, HD), jnp.bfloat16),
        compiler_params=LIMIT,
        cost_estimate=pl.CostEstimate(flops=8 * near.size, bytes_accessed=6 * near.size, transcendentals=0),
    )(near, far)


def finish_kernel(c_ref, context_ref, near_ref, far_ref, out_ref):
    low = jnp.concatenate([context_ref[0], context_ref[2]], axis=1)
    high = jnp.concatenate([context_ref[1], context_ref[3]], axis=1)
    width = out_ref.shape[2]
    for ref, odd in ((near_ref, c_ref[0]), (far_ref, 1 - c_ref[0])):
        for h in range(2):
            terms = jnp.dot(low, ref[2 * h], preferred_element_type=jnp.float32)
            terms += jnp.dot(high, ref[2 * h + 1], preferred_element_type=jnp.float32)
            terms = terms.astype(out_ref.dtype)
            at = 2 * (2 * h + odd)
            out_ref[at] = terms[:, :width]
            out_ref[at + 1] = terms[:, width:]


def finish(core, context, near, far):
    half = context.shape[1]
    blocks, _, cols = near.shape
    vmem = pl.BlockSpec(memory_space=pltpu.VMEM)
    return pl.pallas_call(
        finish_kernel,
        in_specs=[pl.BlockSpec(memory_space=pltpu.SMEM), vmem, vmem, vmem],
        out_specs=vmem,
        out_shape=jax.ShapeDtypeStruct((2 * blocks, half, cols // 2), jnp.bfloat16),
        compiler_params=LIMIT,
        cost_estimate=pl.CostEstimate(
            flops=4 * half * near.size, bytes_accessed=4 * near.size, transcendentals=0
        ),
    )(core, context, near, far)


def swap(block, axis):
    return lax.ppermute(block, axis, [(0, 1), (1, 0)])


def exchange(block, axis):
    return lax.all_to_all(block, axis, 0, 0, tiled=True)


def pick(blocks, index):
    return lax.dynamic_index_in_dim(blocks, index, 0, keepdims=False)


def spread(block, axis):
    count = lax.axis_size(axis)
    return exchange(jnp.broadcast_to(block[None], (count,) + block.shape), axis)


def shift(block, axis, distance):
    count = lax.axis_size(axis)
    return lax.ppermute(block, axis, [(i, (i + distance) % count) for i in range(count)])


def distances(axis):
    count = lax.axis_size(axis)
    return sorted(range(1, count), key=lambda s: -min(s, count - s))


def scatter_by_shifts(blocks, axis, source):
    here, count = lax.axis_index(axis), blocks.shape[0]
    result = pick(blocks, here)
    for s in distances(axis):
        got = shift(pick(blocks, (here + s) % count), axis, s)
        result = jnp.where((here - source) % count == s, got, result)
    return result


def gather_by_shifts(block, axis):
    here, count = lax.axis_index(axis), lax.axis_size(axis)
    got = {0: block}
    for s in distances(axis):
        got[s] = shift(block, axis, s)
    got = jnp.stack([got[s] for s in range(count)])
    return jnp.stack([pick(got, (here - i) % count) for i in range(count)])


def trade(block, across):
    route = []
    for z in range(2):
        for x in range(4):
            for low in range(4):
                for c in range(2):
                    to_low = 3 - low if across else low
                    to = (((z ^ across) * 4 + x - x % 2 + c) * 4 + to_low) * 2 + x % 2
                    here = ((z * 4 + x) * 4 + low) * 2 + c
                    if to != here:
                        route.append((here, to))
    return lax.ppermute(block, ("zh", "x", "zl", "c"), route)


def mirror(block):
    return lax.ppermute(block, ("zh", "zl"), [(i, 7 - i) for i in range(8)])


def shards(hidden_in, norm_gain, snap_qkv, snap_out, owner_index, block_order):
    rows, width = hidden_in.shape
    zh, y, x, c = (lax.axis_index(name) for name in ("zh", "y", "x", "c"))
    ny, nx = 8, 4
    half = rows // 2
    core = c.reshape(1)
    owner = owner_index[0]
    zh0, y0, x0 = owner // (ny * nx), (owner // nx) % ny, owner % nx

    mine = lax.dynamic_slice_in_dim(hidden_in, c * half, half, 0).astype(jnp.float32)
    normed = (
        mine * lax.rsqrt(jnp.mean(mine * mine, axis=-1, keepdims=True) + 1e-06) * norm_gain
    ).astype(jnp.bfloat16)

    order = block_order.reshape(2, ny, nx) * rows
    offsets = jnp.arange(half, dtype=jnp.int32)
    kpos = (pick(order, zh)[:, :, None] + offsets).reshape(-1)
    kpos = jnp.stack([kpos + c * half, kpos + (1 - c) * half])
    here = lax.dynamic_index_in_dim(order, y, 1, keepdims=False)
    start = jnp.stack([pick(here, zh), pick(here, 1 - zh)]).reshape(-1) + c * half

    part = width // (2 * ny)
    w = fold(snap_qkv[0], ny)
    w = pick(exchange(w, "x"), x0)
    wo = scatter_by_shifts(snap_out[0].reshape(ny, -1, snap_out.shape[2]), "y", y0)
    w, wo, normed, kpos, start = lax.optimization_barrier((w, wo, normed, kpos, start))
    w = pick(exchange(w, "y"), y0)
    wo = jnp.transpose(wo.reshape(wo.shape[0], nx, -1), (1, 0, 2))
    wo = scatter_by_shifts(wo, "x", x0)
    wo = jnp.transpose(wo.reshape(wo.shape[0], nx, HD), (1, 0, 2)).reshape(part, HD)
    w = jnp.concatenate([w, wo], axis=1)
    w, normed = lax.optimization_barrier((w, normed))
    w = jnp.where(zh == zh0, jnp.where(x % 2 == c, w, trade(w, 0)), trade(w, 1))
    w = spread(w, "y").reshape(ny * part, 4 * HD)
    normed = gather_by_shifts(normed, "x").reshape(-1, width)
    q, kv = project(core, normed, w, swap(w, "c"))
    wo = w[:, 3 * HD :].reshape(ny, nx, part // nx, HD)
    wo = jnp.transpose(wo, (0, 2, 1, 3)).reshape(ny * part // nx, nx * HD)
    q, kv, wo = lax.optimization_barrier((q, kv, wo))

    near = spread(kv, "y").reshape(-1, 2 * HD)
    q_all = jnp.concatenate([q, mirror(q)])
    wo = gather_by_shifts(wo, "x")
    near, q_all, wo = lax.optimization_barrier((near, q_all, wo))
    far = swap(near, "c")
    wo_far = swap(wo, "c")

    state = attend(start, q_all, near, kpos[:1], half)
    parts = attend(start, q_all, far, kpos[1:], half, state)
    context = merge(parts[:nx], mirror(parts[nx:]))
    context = exchange(context, "x")
    terms = finish(core, context, wo, wo_far)
    terms = exchange(terms, ("zl", "c")).reshape(-1, rows, terms.shape[2])
    return jnp.sum(terms.astype(jnp.float32), axis=0).astype(jnp.bfloat16)


def solution(mesh):
    fine = Mesh(mesh.devices.reshape(2, 8, 4, 4, 2), ("zh", "y", "x", "zl", "c"))
    ctx, tp = ("zh", "y", "x"), ("zl", "c")
    in_specs = (P(ctx, None), P(), P(ctx, None, None, tp), P(ctx, tp, None), P(), P())
    return jax.shard_map(shards, mesh=fine, in_specs=in_specs, out_specs=P(ctx, tp), check_vma=False)
```

```python
import jax
import jax.numpy as jnp
import numpy as np
from jax import lax
from jax.experimental import pallas as pl
from jax.experimental.pallas import tpu as pltpu
from jax.sharding import Mesh
from jax.sharding import PartitionSpec as P

HD = 128
HIDE = -1e30
CHUNK = 640
EXTRA = 16
LIMIT = pltpu.CompilerParams(vmem_limit_bytes=48 * 1024 * 1024)


def fold_kernel(w_ref, out_ref):
    for h in range(2):
        for r in range(2):
            for j in range(3):
                out_ref[2 * h + r, 0, :, j * HD : (j + 1) * HD] = w_ref[j, r, :, h * HD : (h + 1) * HD]


def fold(w, ny):
    part = w.shape[1] // (2 * ny)
    return pl.pallas_call(
        fold_kernel,
        grid=(ny,),
        in_specs=[pl.BlockSpec((3, 2, part, 2 * HD), lambda i: (0, 0, i, 0))],
        out_specs=pl.BlockSpec((4, 1, part, 3 * HD), lambda i: (0, i, 0, 0)),
        out_shape=jax.ShapeDtypeStruct((4, ny, part, 3 * HD), w.dtype),
        compiler_params=LIMIT,
        cost_estimate=pl.CostEstimate(flops=0, bytes_accessed=4 * w.size, transcendentals=0),
    )(w.reshape(3, 2, ny * part, 2 * HD))


def near_kernel(c_ref, x_ref, w_ref, out_ref):
    depth = w_ref.shape[0]
    span = pl.ds(pl.multiple_of(c_ref[0] * depth, depth), depth)
    w = w_ref[:, : out_ref.shape[1]]
    out_ref[...] = jnp.dot(x_ref[:, span], w, preferred_element_type=jnp.float32)


def far_kernel(c_ref, x_ref, w_ref, sum_ref, q_ref, kv_ref):
    depth = w_ref.shape[0]
    span = pl.ds(pl.multiple_of((1 - c_ref[0]) * depth, depth), depth)
    w = w_ref[:, : sum_ref.shape[1]]
    out = sum_ref[...] + jnp.dot(x_ref[:, span], w, preferred_element_type=jnp.float32)
    q_ref[...] = out[:, :HD].astype(q_ref.dtype)
    kv = out[:, HD:].astype(kv_ref.dtype)
    for i in range(kv_ref.shape[0]):
        kv_ref[i] = kv


def project(core, x, near, far, count):
    n, cols = x.shape[0], 3 * HD
    smem, vmem = pl.BlockSpec(memory_space=pltpu.SMEM), pl.BlockSpec(memory_space=pltpu.VMEM)
    cost = pl.CostEstimate(
        flops=2 * n * near.shape[0] * cols, bytes_accessed=2 * (x.size + near.size), transcendentals=0
    )
    total = pl.pallas_call(
        near_kernel,
        in_specs=[smem, vmem, vmem],
        out_specs=vmem,
        out_shape=jax.ShapeDtypeStruct((n, cols), jnp.float32),
        compiler_params=LIMIT,
        cost_estimate=cost,
    )(core, x, near)
    return pl.pallas_call(
        far_kernel,
        in_specs=[smem, vmem, vmem, vmem],
        out_specs=[vmem, vmem],
        out_shape=[
            jax.ShapeDtypeStruct((n, HD), jnp.bfloat16),
            jax.ShapeDtypeStruct((count, n, 2 * HD), jnp.bfloat16),
        ],
        compiler_params=LIMIT,
        cost_estimate=cost,
    )(core, x, far, total)


def three_parts(value):
    first = value.astype(jnp.bfloat16).astype(jnp.float32)
    rest = value - first
    second = rest.astype(jnp.bfloat16).astype(jnp.float32)
    return first, second, rest - second


def attend_kernel(start_ref, q_ref, near_ref, far_ref, kpos_ref, o_ref, s_ref):
    factor = float(np.log2(np.e) / HD**0.5)
    rows = q_ref.shape[0]
    blocks, half = o_ref.shape[0], o_ref.shape[1] - EXTRA
    row = lax.broadcasted_iota(jnp.int32, (rows, 1), 0)
    first = blocks * pl.program_id(0)
    qpos = row + start_ref[first]
    for b in range(1, blocks):
        qpos = jnp.where(row < b * half, qpos, row - b * half + start_ref[first + b])
    pieces = [
        (ref, j * CHUNK, i * ref.shape[0] + j * CHUNK)
        for i, ref in enumerate((near_ref, far_ref))
        for j in range(ref.shape[0] // CHUNK)
    ]
    q = q_ref[...]
    high = jnp.full((rows, HD), HIDE, jnp.float32)
    for ref, at, column in pieces:
        span = pl.ds(column, CHUNK)
        s = lax.dot_general(
            q, ref[pl.ds(at, CHUNK), :HD], (((1,), (1,)), ((), ())), preferred_element_type=jnp.float32
        )
        s = jnp.where(kpos_ref[:, span] <= qpos, s * factor, HIDE)
        s_ref[:, span] = s
        for t in range(CHUNK // HD):
            high = jnp.maximum(high, s[:, t * HD : (t + 1) * HD])
    top = jnp.max(high, axis=1, keepdims=True)
    base = jnp.where(top <= 0.5 * HIDE, 0.0, top)
    total = jnp.zeros((rows, HD), jnp.float32)
    acc = jnp.zeros((rows, HD), jnp.float32)
    for ref, at, column in pieces:
        span = pl.ds(column, CHUNK)
        p = jnp.exp2(s_ref[:, span] - base)
        for t in range(CHUNK // HD):
            total = total + p[:, t * HD : (t + 1) * HD]
        acc = acc + jnp.dot(
            p.astype(jnp.bfloat16), ref[pl.ds(at, CHUNK), HD:], preferred_element_type=jnp.float32
        )
    total = jnp.sum(total, axis=1, keepdims=True)
    o = acc / jnp.where(total == 0.0, 1.0, total)
    lane = lax.broadcasted_iota(jnp.int32, (rows, HD), 1)
    stat = jnp.zeros((rows, HD), jnp.float32)
    for k, piece in enumerate(three_parts(top) + three_parts(total)):
        stat = jnp.where(lane == k, piece, stat)
    for b in range(blocks):
        o_ref[b, :half, :] = o[b * half : (b + 1) * half].astype(o_ref.dtype)
        block = jnp.concatenate(
            [stat[b * half : (b + 1) * half], jnp.zeros((HD - half, HD), jnp.float32)]
        )
        o_ref[b, half:, :] = block.T[:EXTRA].astype(o_ref.dtype)


def attend(start, q, near, far, kpos, half):
    nq, nk = q.shape[0], 2 * near.shape[0]
    tile = 2 * half
    return pl.pallas_call(
        attend_kernel,
        grid=(nq // tile,),
        in_specs=[
            pl.BlockSpec(memory_space=pltpu.SMEM),
            pl.BlockSpec((tile, HD), lambda i: (i, 0)),
            pl.BlockSpec((nk // 2, 2 * HD), lambda i: (0, 0)),
            pl.BlockSpec((nk // 2, 2 * HD), lambda i: (0, 0)),
            pl.BlockSpec((1, nk), lambda i: (0, 0)),
        ],
        out_specs=pl.BlockSpec((2, half + EXTRA, HD), lambda i: (i, 0, 0)),
        out_shape=jax.ShapeDtypeStruct((nq // half, half + EXTRA, HD), jnp.bfloat16),
        scratch_shapes=[pltpu.VMEM((tile, nk), jnp.float32)],
        compiler_params=LIMIT,
        cost_estimate=pl.CostEstimate(
            flops=4 * nq * nk * HD, bytes_accessed=nk * HD * 4, transcendentals=nq * nk
        ),
    )(start, q, near, far, kpos)


def merge_kernel(near_ref, far_ref, out_ref):
    nx, half = out_ref.shape[0], out_ref.shape[1]
    for x in range(nx):
        tops, totals = [], []
        for ref in (near_ref, far_ref):
            stat = ref[x, half:, :].astype(jnp.float32)
            stat = jnp.concatenate([stat, jnp.zeros((HD - EXTRA, HD), jnp.float32)]).T[:half]
            tops.append(stat[:, 0:1] + stat[:, 1:2] + stat[:, 2:3])
            totals.append(stat[:, 3:4] + stat[:, 4:5] + stat[:, 5:6])
        top = jnp.maximum(tops[0], tops[1])
        a = totals[0] * jnp.exp2(tops[0] - top)
        b = totals[1] * jnp.exp2(tops[1] - top)
        mixed = near_ref[x, :half, :].astype(jnp.float32) * a + far_ref[x, :half, :].astype(jnp.float32) * b
        out_ref[x] = (mixed / (a + b)).astype(out_ref.dtype)


def merge(near, far):
    nx, rows = near.shape[0], near.shape[1] - EXTRA
    vmem = pl.BlockSpec(memory_space=pltpu.VMEM)
    return pl.pallas_call(
        merge_kernel,
        in_specs=[vmem, vmem],
        out_specs=vmem,
        out_shape=jax.ShapeDtypeStruct((nx, rows, HD), jnp.bfloat16),
        compiler_params=LIMIT,
        cost_estimate=pl.CostEstimate(flops=8 * near.size, bytes_accessed=6 * near.size, transcendentals=0),
    )(near, far)


def finish_kernel(c_ref, context_ref, near_ref, far_ref, out_ref):
    low = jnp.concatenate([context_ref[0], context_ref[2]], axis=1)
    high = jnp.concatenate([context_ref[1], context_ref[3]], axis=1)
    width = out_ref.shape[2]
    for ref, odd in ((near_ref, c_ref[0]), (far_ref, 1 - c_ref[0])):
        for h in range(2):
            terms = jnp.dot(low, ref[2 * h], preferred_element_type=jnp.float32)
            terms += jnp.dot(high, ref[2 * h + 1], preferred_element_type=jnp.float32)
            terms = terms.astype(out_ref.dtype)
            at = 2 * (2 * h + odd)
            out_ref[at] = terms[:, :width]
            out_ref[at + 1] = terms[:, width:]


def finish(core, context, near, far):
    half = context.shape[1]
    blocks, _, cols = near.shape
    vmem = pl.BlockSpec(memory_space=pltpu.VMEM)
    return pl.pallas_call(
        finish_kernel,
        in_specs=[pl.BlockSpec(memory_space=pltpu.SMEM), vmem, vmem, vmem],
        out_specs=vmem,
        out_shape=jax.ShapeDtypeStruct((2 * blocks, half, cols // 2), jnp.bfloat16),
        compiler_params=LIMIT,
        cost_estimate=pl.CostEstimate(
            flops=4 * half * near.size, bytes_accessed=4 * near.size, transcendentals=0
        ),
    )(core, context, near, far)


def swap(block, axis):
    return lax.ppermute(block, axis, [(0, 1), (1, 0)])


def exchange(block, axis):
    return lax.all_to_all(block, axis, 0, 0, tiled=True)


def pick(blocks, index):
    return lax.dynamic_index_in_dim(blocks, index, 0, keepdims=False)


def spread(block, axis):
    count = lax.axis_size(axis)
    return exchange(jnp.broadcast_to(block[None], (count,) + block.shape), axis)


def shift(block, axis, distance):
    count = lax.axis_size(axis)
    return lax.ppermute(block, axis, [(i, (i + distance) % count) for i in range(count)])


def distances(axis):
    count = lax.axis_size(axis)
    return sorted(range(1, count), key=lambda s: -min(s, count - s))


def scatter_by_shifts(blocks, axis, source):
    here, count = lax.axis_index(axis), blocks.shape[0]
    result = pick(blocks, here)
    for s in distances(axis):
        got = shift(pick(blocks, (here + s) % count), axis, s)
        result = jnp.where((here - source) % count == s, got, result)
    return result


def scatter_along_y(blocks, y0):
    yh = lax.axis_index("yh")
    blocks = blocks.reshape((2, 4) + blocks.shape[1:])
    got = lax.ppermute(pick(blocks, 1 - yh), ("yh", "yl"), [(i, 7 - i) for i in range(8)])
    home = yh == y0 // 4
    blocks = jnp.where(home, pick(blocks, yh), got)
    return scatter_by_shifts(blocks, "yl", jnp.where(home, y0 % 4, 3 - y0 % 4))


def gather_by_shifts(block, axis):
    here, count = lax.axis_index(axis), lax.axis_size(axis)
    got = {0: block}
    for s in distances(axis):
        got[s] = shift(block, axis, s)
    got = jnp.stack([got[s] for s in range(count)])
    return jnp.stack([pick(got, (here - i) % count) for i in range(count)])


def trade(block, across):
    route = []
    for z in range(2):
        for x in range(4):
            for low in range(4):
                for c in range(2):
                    to_low = 3 - low if across else low
                    to = (((z ^ across) * 4 + x - x % 2 + c) * 4 + to_low) * 2 + x % 2
                    here = ((z * 4 + x) * 4 + low) * 2 + c
                    if to != here:
                        route.append((here, to))
    return lax.ppermute(block, ("zh", "x", "zl", "c"), route)


def mirror(block):
    return lax.ppermute(block, ("zh", "zl"), [(i, 7 - i) for i in range(8)])


def shards(hidden_in, norm_gain, snap_qkv, snap_out, owner_index, block_order):
    rows, width = hidden_in.shape
    ys = ("yh", "yl")
    zh, y, x, c = (lax.axis_index(name) for name in ("zh", ys, "x", "c"))
    ny, nx = 8, 4
    half = rows // 2
    core = c.reshape(1)
    owner = owner_index[0]
    zh0, y0, x0 = owner // (ny * nx), (owner // nx) % ny, owner % nx

    mine = lax.dynamic_slice_in_dim(hidden_in, c * half, half, 0).astype(jnp.float32)
    normed = (
        mine * lax.rsqrt(jnp.mean(mine * mine, axis=-1, keepdims=True) + 1e-06) * norm_gain
    ).astype(jnp.bfloat16)

    order = block_order.reshape(2, ny, nx) * rows
    offsets = jnp.arange(half, dtype=jnp.int32)
    kpos = (pick(order, zh)[:, :, None] + offsets).reshape(-1)
    kpos = jnp.concatenate([kpos + c * half, kpos + (1 - c) * half]).reshape(1, -1)
    here = lax.dynamic_index_in_dim(order, y, 1, keepdims=False)
    start = pick(here, zh) + c * half
    start_other = pick(here, 1 - zh) + c * half

    part = width // (2 * ny)
    w = fold(snap_qkv[0], ny)
    w = pick(exchange(w, "x"), x0)
    wo = scatter_along_y(snap_out[0].reshape(ny, -1, snap_out.shape[2]), y0)
    w, wo, normed, kpos, start, start_other = lax.optimization_barrier((w, wo, normed, kpos, start, start_other))
    w = pick(exchange(w, ys), y0)
    wo = jnp.transpose(wo.reshape(wo.shape[0], nx, -1), (1, 0, 2))
    wo = scatter_by_shifts(wo, "x", x0)
    wo = jnp.transpose(wo.reshape(wo.shape[0], nx, HD), (1, 0, 2)).reshape(part, HD)
    w = jnp.concatenate([w, wo], axis=1)
    w, normed = lax.optimization_barrier((w, normed))
    w = jnp.where(zh == zh0, jnp.where(x % 2 == c, w, trade(w, 0)), trade(w, 1))
    w = spread(w, ys).reshape(ny * part, 4 * HD)
    normed = gather_by_shifts(normed, "x").reshape(-1, width)
    q, kv = project(core, normed, w, swap(w, "c"), ny)
    wo = w[:, 3 * HD :].reshape(ny, nx, part // nx, HD)
    wo = jnp.transpose(wo, (0, 2, 1, 3)).reshape(ny * part // nx, nx * HD)
    q, kv, wo = lax.optimization_barrier((q, kv, wo))

    near = exchange(kv, ys).reshape(-1, 2 * HD)
    q_other = mirror(q)
    wo = gather_by_shifts(wo, "x")
    near, q_other, wo = lax.optimization_barrier((near, q_other, wo))
    far = swap(near, "c")
    wo_far = swap(wo, "c")

    others = mirror(attend(start_other, q_other, near, far, kpos, half))
    context = merge(attend(start, q, near, far, kpos, half), others)
    context = exchange(context, "x")
    terms = finish(core, context, wo, wo_far)
    terms = exchange(terms, ("zl", "c")).reshape(-1, rows, terms.shape[2])
    return jnp.sum(terms.astype(jnp.float32), axis=0).astype(jnp.bfloat16)


def solution(mesh):
    fine = Mesh(mesh.devices.reshape(2, 2, 4, 4, 4, 2), ("zh", "yh", "yl", "x", "zl", "c"))
    ctx, tp = ("zh", "yh", "yl", "x"), ("zl", "c")
    in_specs = (P(ctx, None), P(), P(ctx, None, None, tp), P(ctx, tp, None), P(), P())
    return jax.shard_map(shards, mesh=fine, in_specs=in_specs, out_specs=P(ctx, tp), check_vma=False)
```

```python
import jax
import jax.numpy as jnp
import numpy as np
from jax import lax
from jax.experimental import pallas as pl
from jax.experimental.pallas import tpu as pltpu
from jax.sharding import Mesh
from jax.sharding import PartitionSpec as P

HD = 128
HIDE = -1e30
CHUNK = 640
EXTRA = 16
LIMIT = pltpu.CompilerParams(vmem_limit_bytes=24 * 1024 * 1024)


def fold_kernel(w_ref, out_ref):
    for h in range(2):
        for r in range(2):
            for j in range(3):
                out_ref[2 * h + r, :, :, j * HD : (j + 1) * HD] = w_ref[j, r, :, :, h * HD : (h + 1) * HD]


def fold(w, ny):
    part, steps = w.shape[1] // (2 * ny), 2
    return pl.pallas_call(
        fold_kernel,
        grid=(steps,),
        in_specs=[pl.BlockSpec((3, 2, ny // steps, part, 2 * HD), lambda i: (0, 0, i, 0, 0))],
        out_specs=pl.BlockSpec((4, ny // steps, part, 3 * HD), lambda i: (0, i, 0, 0)),
        out_shape=jax.ShapeDtypeStruct((4, ny, part, 3 * HD), w.dtype),
        compiler_params=LIMIT,
        cost_estimate=pl.CostEstimate(flops=0, bytes_accessed=4 * w.size, transcendentals=0),
    )(w.reshape(3, 2, ny, part, 2 * HD))


def near_kernel(c_ref, x_ref, w_ref, out_ref):
    depth = w_ref.shape[0]
    span = pl.ds(pl.multiple_of(c_ref[0] * depth, depth), depth)
    w = w_ref[:, : out_ref.shape[1]]
    out_ref[...] = jnp.dot(x_ref[:, span], w, preferred_element_type=jnp.float32)


def far_kernel(c_ref, x_ref, w_ref, sum_ref, q_ref, kv_ref):
    depth = w_ref.shape[0]
    span = pl.ds(pl.multiple_of((1 - c_ref[0]) * depth, depth), depth)
    w = w_ref[:, : sum_ref.shape[1]]
    out = sum_ref[...] + jnp.dot(x_ref[:, span], w, preferred_element_type=jnp.float32)
    q_ref[...] = out[:, :HD].astype(q_ref.dtype)
    kv = out[:, HD:].astype(kv_ref.dtype)
    for i in range(kv_ref.shape[0]):
        kv_ref[i] = kv


def project(core, x, near, far, count):
    n, cols = x.shape[0], 3 * HD
    smem, vmem = pl.BlockSpec(memory_space=pltpu.SMEM), pl.BlockSpec(memory_space=pltpu.VMEM)
    cost = pl.CostEstimate(
        flops=2 * n * near.shape[0] * cols, bytes_accessed=2 * (x.size + near.size), transcendentals=0
    )
    total = pl.pallas_call(
        near_kernel,
        in_specs=[smem, vmem, vmem],
        out_specs=vmem,
        out_shape=jax.ShapeDtypeStruct((n, cols), jnp.float32),
        compiler_params=LIMIT,
        cost_estimate=cost,
    )(core, x, near)
    return pl.pallas_call(
        far_kernel,
        in_specs=[smem, vmem, vmem, vmem],
        out_specs=[vmem, vmem],
        out_shape=[
            jax.ShapeDtypeStruct((n, HD), jnp.bfloat16),
            jax.ShapeDtypeStruct((count, n, 2 * HD), jnp.bfloat16),
        ],
        compiler_params=LIMIT,
        cost_estimate=cost,
    )(core, x, far, total)


def three_parts(value):
    first = value.astype(jnp.bfloat16).astype(jnp.float32)
    rest = value - first
    second = rest.astype(jnp.bfloat16).astype(jnp.float32)
    return first, second, rest - second


def attend_kernel(start_ref, q_ref, near_ref, far_ref, kpos_ref, o_ref, s_ref):
    factor = float(np.log2(np.e) / HD**0.5)
    rows = q_ref.shape[0]
    blocks, half = o_ref.shape[0], o_ref.shape[1] - EXTRA
    row = lax.broadcasted_iota(jnp.int32, (rows, 1), 0)
    first = blocks * pl.program_id(0)
    qpos = row + start_ref[first]
    for b in range(1, blocks):
        qpos = jnp.where(row < b * half, qpos, row - b * half + start_ref[first + b])
    pieces = [
        (ref, j * CHUNK, i * ref.shape[0] + j * CHUNK)
        for i, ref in enumerate((near_ref, far_ref))
        for j in range(ref.shape[0] // CHUNK)
    ]
    q = q_ref[...]
    high = jnp.full((rows, HD), HIDE, jnp.float32)
    for ref, at, column in pieces:
        span = pl.ds(column, CHUNK)
        s = lax.dot_general(
            q, ref[pl.ds(at, CHUNK), :HD], (((1,), (1,)), ((), ())), preferred_element_type=jnp.float32
        )
        s = jnp.where(kpos_ref[:, span] <= qpos, s * factor, HIDE)
        s_ref[:, span] = s
        for t in range(CHUNK // HD):
            high = jnp.maximum(high, s[:, t * HD : (t + 1) * HD])
    top = jnp.max(high, axis=1, keepdims=True)
    base = jnp.where(top <= 0.5 * HIDE, 0.0, top)
    total = jnp.zeros((rows, HD), jnp.float32)
    acc = jnp.zeros((rows, HD), jnp.float32)
    for ref, at, column in pieces:
        span = pl.ds(column, CHUNK)
        p = jnp.exp2(s_ref[:, span] - base)
        for t in range(CHUNK // HD):
            total = total + p[:, t * HD : (t + 1) * HD]
        acc = acc + jnp.dot(
            p.astype(jnp.bfloat16), ref[pl.ds(at, CHUNK), HD:], preferred_element_type=jnp.float32
        )
    total = jnp.sum(total, axis=1, keepdims=True)
    o = acc / jnp.where(total == 0.0, 1.0, total)
    lane = lax.broadcasted_iota(jnp.int32, (rows, HD), 1)
    stat = jnp.zeros((rows, HD), jnp.float32)
    for k, piece in enumerate(three_parts(top) + three_parts(total)):
        stat = jnp.where(lane == k, piece, stat)
    for b in range(blocks):
        o_ref[b, :half, :] = o[b * half : (b + 1) * half].astype(o_ref.dtype)
        block = jnp.concatenate(
            [stat[b * half : (b + 1) * half], jnp.zeros((HD - half, HD), jnp.float32)]
        )
        o_ref[b, half:, :] = block.T[:EXTRA].astype(o_ref.dtype)


def attend(start, q, near, far, kpos, half):
    nq, nk = q.shape[0], 2 * near.shape[0]
    tile = 2 * half
    return pl.pallas_call(
        attend_kernel,
        grid=(nq // tile,),
        in_specs=[
            pl.BlockSpec(memory_space=pltpu.SMEM),
            pl.BlockSpec((tile, HD), lambda i: (i, 0)),
            pl.BlockSpec((nk // 2, 2 * HD), lambda i: (0, 0)),
            pl.BlockSpec((nk // 2, 2 * HD), lambda i: (0, 0)),
            pl.BlockSpec((1, nk), lambda i: (0, 0)),
        ],
        out_specs=pl.BlockSpec((2, half + EXTRA, HD), lambda i: (i, 0, 0)),
        out_shape=jax.ShapeDtypeStruct((nq // half, half + EXTRA, HD), jnp.bfloat16),
        scratch_shapes=[pltpu.VMEM((tile, nk), jnp.float32)],
        compiler_params=LIMIT,
        cost_estimate=pl.CostEstimate(
            flops=4 * nq * nk * HD, bytes_accessed=nk * HD * 4, transcendentals=nq * nk
        ),
    )(start, q, near, far, kpos)


def merge_kernel(near_ref, far_ref, out_ref):
    nx, half = out_ref.shape[0], out_ref.shape[1]
    for x in range(nx):
        tops, totals = [], []
        for ref in (near_ref, far_ref):
            stat = ref[x, half:, :].astype(jnp.float32)
            stat = jnp.concatenate([stat, jnp.zeros((HD - EXTRA, HD), jnp.float32)]).T[:half]
            tops.append(stat[:, 0:1] + stat[:, 1:2] + stat[:, 2:3])
            totals.append(stat[:, 3:4] + stat[:, 4:5] + stat[:, 5:6])
        top = jnp.maximum(tops[0], tops[1])
        a = totals[0] * jnp.exp2(tops[0] - top)
        b = totals[1] * jnp.exp2(tops[1] - top)
        mixed = near_ref[x, :half, :].astype(jnp.float32) * a + far_ref[x, :half, :].astype(jnp.float32) * b
        out_ref[x] = (mixed / (a + b)).astype(out_ref.dtype)


def merge(near, far):
    nx, rows = near.shape[0], near.shape[1] - EXTRA
    vmem = pl.BlockSpec(memory_space=pltpu.VMEM)
    return pl.pallas_call(
        merge_kernel,
        in_specs=[vmem, vmem],
        out_specs=vmem,
        out_shape=jax.ShapeDtypeStruct((nx, rows, HD), jnp.bfloat16),
        compiler_params=LIMIT,
        cost_estimate=pl.CostEstimate(flops=8 * near.size, bytes_accessed=6 * near.size, transcendentals=0),
    )(near, far)


def finish_kernel(c_ref, context_ref, near_ref, far_ref, out_ref):
    low = jnp.concatenate([context_ref[0], context_ref[2]], axis=1)
    high = jnp.concatenate([context_ref[1], context_ref[3]], axis=1)
    width = out_ref.shape[2]
    for ref, odd in ((near_ref, c_ref[0]), (far_ref, 1 - c_ref[0])):
        for h in range(2):
            terms = jnp.dot(low, ref[2 * h], preferred_element_type=jnp.float32)
            terms += jnp.dot(high, ref[2 * h + 1], preferred_element_type=jnp.float32)
            terms = terms.astype(out_ref.dtype)
            at = 2 * (2 * h + odd)
            out_ref[at] = terms[:, :width]
            out_ref[at + 1] = terms[:, width:]


def finish(core, context, near, far):
    half = context.shape[1]
    blocks, _, cols = near.shape
    vmem = pl.BlockSpec(memory_space=pltpu.VMEM)
    return pl.pallas_call(
        finish_kernel,
        in_specs=[pl.BlockSpec(memory_space=pltpu.SMEM), vmem, vmem, vmem],
        out_specs=vmem,
        out_shape=jax.ShapeDtypeStruct((2 * blocks, half, cols // 2), jnp.bfloat16),
        compiler_params=LIMIT,
        cost_estimate=pl.CostEstimate(
            flops=4 * half * near.size, bytes_accessed=4 * near.size, transcendentals=0
        ),
    )(core, context, near, far)


def swap(block, axis):
    return lax.ppermute(block, axis, [(0, 1), (1, 0)])


def exchange(block, axis):
    return lax.all_to_all(block, axis, 0, 0, tiled=True)


def pick(blocks, index):
    return lax.dynamic_index_in_dim(blocks, index, 0, keepdims=False)


def spread(block, axis):
    count = lax.axis_size(axis)
    return exchange(jnp.broadcast_to(block[None], (count,) + block.shape), axis)


def shift(block, axis, distance):
    count = lax.axis_size(axis)
    return lax.ppermute(block, axis, [(i, (i + distance) % count) for i in range(count)])


def distances(axis):
    count = lax.axis_size(axis)
    return sorted(range(1, count), key=lambda s: -min(s, count - s))


def take_shifts(result, blocks, axis, source):
    behind = (lax.axis_index(axis) - source) % lax.axis_size(axis)
    for s, block in blocks.items():
        result = jnp.where(behind == s, shift(block, axis, s), result)
    return result


def ahead(blocks, axis):
    here, count = lax.axis_index(axis), blocks.shape[0]
    return {s: pick(blocks, (here + s) % count) for s in distances(axis)}


def gather_by_shifts(block, axis):
    here, count = lax.axis_index(axis), lax.axis_size(axis)
    got = {0: block}
    for s in distances(axis):
        got[s] = shift(block, axis, s)
    got = jnp.stack([got[s] for s in range(count)])
    return jnp.stack([pick(got, (here - i) % count) for i in range(count)])


def trade(block, across):
    route = []
    for z in range(2):
        for x in range(4):
            for low in range(4):
                for c in range(2):
                    to_low = 3 - low if across else low
                    to = (((z ^ across) * 4 + x - x % 2 + c) * 4 + to_low) * 2 + x % 2
                    here = ((z * 4 + x) * 4 + low) * 2 + c
                    if to != here:
                        route.append((here, to))
    return lax.ppermute(block, ("zh", "x", "zl", "c"), route)


def mirror(block):
    return lax.ppermute(block, ("zh", "zl"), [(i, 7 - i) for i in range(8)])


def shards(hidden_in, norm_gain, snap_qkv, snap_out, owner_index, block_order):
    rows, width = hidden_in.shape
    ys = ("yh", "yl")
    zh, y, x, c = (lax.axis_index(name) for name in ("zh", ys, "x", "c"))
    ny, nx = 8, 4
    half = rows // 2
    core = c.reshape(1)
    owner = owner_index[0]
    zh0, y0, x0 = owner // (ny * nx), (owner // nx) % ny, owner % nx

    mine = lax.dynamic_slice_in_dim(hidden_in, c * half, half, 0).astype(jnp.float32)
    normed = (
        mine * lax.rsqrt(jnp.mean(mine * mine, axis=-1, keepdims=True) + 1e-06) * norm_gain
    ).astype(jnp.bfloat16)

    order = block_order.reshape(2, ny, nx) * rows
    offsets = jnp.arange(half, dtype=jnp.int32)
    kpos = (pick(order, zh)[:, :, None] + offsets).reshape(-1)
    kpos = jnp.concatenate([kpos + c * half, kpos + (1 - c) * half]).reshape(1, -1)
    here = lax.dynamic_index_in_dim(order, y, 1, keepdims=False)
    start = pick(here, zh) + c * half
    start_other = pick(here, 1 - zh) + c * half

    part = width // (2 * ny)
    w = fold(snap_qkv[0], ny)
    w = pick(exchange(w, "x"), x0)
    wo = snap_out[0].reshape(ny, -1, snap_out.shape[2])
    blocks = ahead(wo, ys)
    after = {s: blocks.pop(s) for s in (1, ny - 1)}
    wo = take_shifts(pick(wo, y), blocks, ys, y0)
    w, wo, after, normed, kpos, start, start_other = lax.optimization_barrier(
        (w, wo, after, normed, kpos, start, start_other)
    )
    w = pick(exchange(w, ys), y0)
    wo = take_shifts(wo, after, ys, y0)
    wo = jnp.transpose(wo.reshape(wo.shape[0], nx, -1), (1, 0, 2))
    wo = take_shifts(pick(wo, x), ahead(wo, "x"), "x", x0)
    wo = jnp.transpose(wo.reshape(wo.shape[0], nx, HD), (1, 0, 2)).reshape(part, HD)
    w = jnp.concatenate([w, wo], axis=1)
    w, normed = lax.optimization_barrier((w, normed))
    w = jnp.where(zh == zh0, jnp.where(x % 2 == c, w, trade(w, 0)), trade(w, 1))
    w = spread(w, ys).reshape(ny * part, 4 * HD)
    normed = gather_by_shifts(normed, "x").reshape(-1, width)
    q, kv = project(core, normed, w, swap(w, "c"), ny)
    wo = w[:, 3 * HD :].reshape(ny, nx, part // nx, HD)
    wo = jnp.transpose(wo, (0, 2, 1, 3)).reshape(ny * part // nx, nx * HD)
    q, kv, wo = lax.optimization_barrier((q, kv, wo))

    near = exchange(kv, ys).reshape(-1, 2 * HD)
    q_other = mirror(q)
    wo = gather_by_shifts(wo, "x")
    near, q_other, wo = lax.optimization_barrier((near, q_other, wo))
    far = swap(near, "c")
    wo_far = swap(wo, "c")

    others = mirror(attend(start_other, q_other, near, far, kpos, half))
    context = merge(attend(start, q, near, far, kpos, half), others)
    context = exchange(context, "x")
    terms = finish(core, context, wo, wo_far)
    terms = exchange(terms, ("zl", "c")).reshape(-1, rows, terms.shape[2])
    return jnp.sum(terms.astype(jnp.float32), axis=0).astype(jnp.bfloat16)


def solution(mesh):
    fine = Mesh(mesh.devices.reshape(2, 2, 4, 4, 4, 2), ("zh", "yh", "yl", "x", "zl", "c"))
    ctx, tp = ("zh", "yh", "yl", "x"), ("zl", "c")
    in_specs = (P(ctx, None), P(), P(ctx, None, None, tp), P(ctx, tp, None), P(), P())
    return jax.shard_map(shards, mesh=fine, in_specs=in_specs, out_specs=P(ctx, tp), check_vma=False)
```

```python
import jax
import jax.numpy as jnp
import numpy as np
from jax import lax
from jax.experimental import pallas as pl
from jax.experimental.pallas import tpu as pltpu
from jax.sharding import Mesh
from jax.sharding import PartitionSpec as P

HD = 128
HIDE = -1e30
CHUNK = 640
EXTRA = 16
LIMIT = pltpu.CompilerParams(vmem_limit_bytes=24 * 1024 * 1024)


def fold_kernel(w_ref, out_ref):
    for h in range(2):
        for r in range(2):
            for j in range(3):
                out_ref[2 * h + r, :, :, j * HD : (j + 1) * HD] = w_ref[j, r, :, :, h * HD : (h + 1) * HD]


def fold(w, ny):
    part, steps = w.shape[1] // (2 * ny), 2
    return pl.pallas_call(
        fold_kernel,
        grid=(steps,),
        in_specs=[pl.BlockSpec((3, 2, ny // steps, part, 2 * HD), lambda i: (0, 0, i, 0, 0))],
        out_specs=pl.BlockSpec((4, ny // steps, part, 3 * HD), lambda i: (0, i, 0, 0)),
        out_shape=jax.ShapeDtypeStruct((4, ny, part, 3 * HD), w.dtype),
        compiler_params=LIMIT,
        cost_estimate=pl.CostEstimate(flops=0, bytes_accessed=4 * w.size, transcendentals=0),
    )(w.reshape(3, 2, ny, part, 2 * HD))


def near_kernel(c_ref, x_ref, w_ref, out_ref):
    depth = w_ref.shape[0]
    span = pl.ds(pl.multiple_of(c_ref[0] * depth, depth), depth)
    w = w_ref[:, : out_ref.shape[1]]
    out_ref[...] = jnp.dot(x_ref[:, span], w, preferred_element_type=jnp.float32)


def far_kernel(c_ref, x_ref, w_ref, sum_ref, q_ref, kv_ref):
    depth = w_ref.shape[0]
    span = pl.ds(pl.multiple_of((1 - c_ref[0]) * depth, depth), depth)
    w = w_ref[:, : sum_ref.shape[1]]
    out = sum_ref[...] + jnp.dot(x_ref[:, span], w, preferred_element_type=jnp.float32)
    q_ref[...] = out[:, :HD].astype(q_ref.dtype)
    kv = out[:, HD:].astype(kv_ref.dtype)
    for i in range(kv_ref.shape[0]):
        kv_ref[i] = kv


def project(core, x, near, far, count):
    n, cols = x.shape[0], 3 * HD
    smem, vmem = pl.BlockSpec(memory_space=pltpu.SMEM), pl.BlockSpec(memory_space=pltpu.VMEM)
    cost = pl.CostEstimate(
        flops=2 * n * near.shape[0] * cols, bytes_accessed=2 * (x.size + near.size), transcendentals=0
    )
    total = pl.pallas_call(
        near_kernel,
        in_specs=[smem, vmem, vmem],
        out_specs=vmem,
        out_shape=jax.ShapeDtypeStruct((n, cols), jnp.float32),
        compiler_params=LIMIT,
        cost_estimate=cost,
    )(core, x, near)
    return pl.pallas_call(
        far_kernel,
        in_specs=[smem, vmem, vmem, vmem],
        out_specs=[vmem, vmem],
        out_shape=[
            jax.ShapeDtypeStruct((n, HD), jnp.bfloat16),
            jax.ShapeDtypeStruct((count, n, 2 * HD), jnp.bfloat16),
        ],
        compiler_params=LIMIT,
        cost_estimate=cost,
    )(core, x, far, total)


def three_parts(value):
    first = value.astype(jnp.bfloat16).astype(jnp.float32)
    rest = value - first
    second = rest.astype(jnp.bfloat16).astype(jnp.float32)
    return first, second, rest - second


def attend_kernel(start_ref, q_ref, near_ref, far_ref, kpos_ref, o_ref, s_ref):
    factor = float(np.log2(np.e) / HD**0.5)
    rows = q_ref.shape[0]
    blocks, half = o_ref.shape[0], o_ref.shape[1] - EXTRA
    row = lax.broadcasted_iota(jnp.int32, (rows, 1), 0)
    first = blocks * pl.program_id(0)
    qpos = row + start_ref[first]
    for b in range(1, blocks):
        qpos = jnp.where(row < b * half, qpos, row - b * half + start_ref[first + b])
    pieces = [
        (ref, j * CHUNK, i * ref.shape[0] + j * CHUNK)
        for i, ref in enumerate((near_ref, far_ref))
        for j in range(ref.shape[0] // CHUNK)
    ]
    q = q_ref[...]
    high = jnp.full((rows, HD), HIDE, jnp.float32)
    for ref, at, column in pieces:
        span = pl.ds(column, CHUNK)
        s = lax.dot_general(
            q, ref[pl.ds(at, CHUNK), :HD], (((1,), (1,)), ((), ())), preferred_element_type=jnp.float32
        )
        s = jnp.where(kpos_ref[:, span] <= qpos, s * factor, HIDE)
        s_ref[:, span] = s
        for t in range(CHUNK // HD):
            high = jnp.maximum(high, s[:, t * HD : (t + 1) * HD])
    top = jnp.max(high, axis=1, keepdims=True)
    base = jnp.where(top <= 0.5 * HIDE, 0.0, top)
    total = jnp.zeros((rows, HD), jnp.float32)
    acc = jnp.zeros((rows, HD), jnp.float32)
    for ref, at, column in pieces:
        span = pl.ds(column, CHUNK)
        p = jnp.exp2(s_ref[:, span] - base)
        for t in range(CHUNK // HD):
            total = total + p[:, t * HD : (t + 1) * HD]
        acc = acc + jnp.dot(
            p.astype(jnp.bfloat16), ref[pl.ds(at, CHUNK), HD:], preferred_element_type=jnp.float32
        )
    total = jnp.sum(total, axis=1, keepdims=True)
    o = acc / jnp.where(total == 0.0, 1.0, total)
    lane = lax.broadcasted_iota(jnp.int32, (rows, HD), 1)
    stat = jnp.zeros((rows, HD), jnp.float32)
    for k, piece in enumerate(three_parts(top) + three_parts(total)):
        stat = jnp.where(lane == k, piece, stat)
    for b in range(blocks):
        o_ref[b, :half, :] = o[b * half : (b + 1) * half].astype(o_ref.dtype)
        block = jnp.concatenate(
            [stat[b * half : (b + 1) * half], jnp.zeros((HD - half, HD), jnp.float32)]
        )
        o_ref[b, half:, :] = block.T[:EXTRA].astype(o_ref.dtype)


def attend(start, q, near, far, kpos, half):
    nq, nk = q.shape[0], 2 * near.shape[0]
    tile = 2 * half
    return pl.pallas_call(
        attend_kernel,
        grid=(nq // tile,),
        in_specs=[
            pl.BlockSpec(memory_space=pltpu.SMEM),
            pl.BlockSpec((tile, HD), lambda i: (i, 0)),
            pl.BlockSpec((nk // 2, 2 * HD), lambda i: (0, 0)),
            pl.BlockSpec((nk // 2, 2 * HD), lambda i: (0, 0)),
            pl.BlockSpec((1, nk), lambda i: (0, 0)),
        ],
        out_specs=pl.BlockSpec((2, half + EXTRA, HD), lambda i: (i, 0, 0)),
        out_shape=jax.ShapeDtypeStruct((nq // half, half + EXTRA, HD), jnp.bfloat16),
        scratch_shapes=[pltpu.VMEM((tile, nk), jnp.float32)],
        compiler_params=LIMIT,
        cost_estimate=pl.CostEstimate(
            flops=4 * nq * nk * HD, bytes_accessed=nk * HD * 4, transcendentals=nq * nk
        ),
    )(start, q, near, far, kpos)


def merge_kernel(near_ref, far_ref, out_ref):
    nx, half = out_ref.shape[0], out_ref.shape[1]
    for x in range(nx):
        tops, totals = [], []
        for ref in (near_ref, far_ref):
            stat = ref[x, half:, :].astype(jnp.float32)
            stat = jnp.concatenate([stat, jnp.zeros((HD - EXTRA, HD), jnp.float32)]).T[:half]
            tops.append(stat[:, 0:1] + stat[:, 1:2] + stat[:, 2:3])
            totals.append(stat[:, 3:4] + stat[:, 4:5] + stat[:, 5:6])
        top = jnp.maximum(tops[0], tops[1])
        a = totals[0] * jnp.exp2(tops[0] - top)
        b = totals[1] * jnp.exp2(tops[1] - top)
        mixed = near_ref[x, :half, :].astype(jnp.float32) * a + far_ref[x, :half, :].astype(jnp.float32) * b
        out_ref[x] = (mixed / (a + b)).astype(out_ref.dtype)


def merge(near, far):
    nx, rows = near.shape[0], near.shape[1] - EXTRA
    vmem = pl.BlockSpec(memory_space=pltpu.VMEM)
    return pl.pallas_call(
        merge_kernel,
        in_specs=[vmem, vmem],
        out_specs=vmem,
        out_shape=jax.ShapeDtypeStruct((nx, rows, HD), jnp.bfloat16),
        compiler_params=LIMIT,
        cost_estimate=pl.CostEstimate(flops=8 * near.size, bytes_accessed=6 * near.size, transcendentals=0),
    )(near, far)


def finish_kernel(c_ref, context_ref, near_ref, far_ref, out_ref):
    low = jnp.concatenate([context_ref[0], context_ref[2]], axis=1)
    high = jnp.concatenate([context_ref[1], context_ref[3]], axis=1)
    width = out_ref.shape[2]
    for ref, odd in ((near_ref, c_ref[0]), (far_ref, 1 - c_ref[0])):
        for h in range(2):
            terms = jnp.dot(low, ref[2 * h], preferred_element_type=jnp.float32)
            terms += jnp.dot(high, ref[2 * h + 1], preferred_element_type=jnp.float32)
            terms = terms.astype(out_ref.dtype)
            at = 2 * (2 * h + odd)
            out_ref[at] = terms[:, :width]
            out_ref[at + 1] = terms[:, width:]


def finish(core, context, near, far):
    half = context.shape[1]
    blocks, _, cols = near.shape
    vmem = pl.BlockSpec(memory_space=pltpu.VMEM)
    return pl.pallas_call(
        finish_kernel,
        in_specs=[pl.BlockSpec(memory_space=pltpu.SMEM), vmem, vmem, vmem],
        out_specs=vmem,
        out_shape=jax.ShapeDtypeStruct((2 * blocks, half, cols // 2), jnp.bfloat16),
        compiler_params=LIMIT,
        cost_estimate=pl.CostEstimate(
            flops=4 * half * near.size, bytes_accessed=4 * near.size, transcendentals=0
        ),
    )(core, context, near, far)


def swap(block, axis):
    return lax.ppermute(block, axis, [(0, 1), (1, 0)])


def exchange(block, axis):
    return lax.all_to_all(block, axis, 0, 0, tiled=True)


def pick(blocks, index):
    return lax.dynamic_index_in_dim(blocks, index, 0, keepdims=False)


def spread(block, axis):
    count = lax.axis_size(axis)
    return exchange(jnp.broadcast_to(block[None], (count,) + block.shape), axis)


def shift(block, axis, distance):
    count = lax.axis_size(axis)
    return lax.ppermute(block, axis, [(i, (i + distance) % count) for i in range(count)])


def distances(axis):
    count = lax.axis_size(axis)
    return sorted(range(1, count), key=lambda s: -min(s, count - s))


def take_shifts(result, blocks, axis, source):
    behind = (lax.axis_index(axis) - source) % lax.axis_size(axis)
    for s, block in blocks.items():
        result = jnp.where(behind == s, shift(block, axis, s), result)
    return result


def ahead(blocks, axis):
    here, count = lax.axis_index(axis), blocks.shape[0]
    return {s: pick(blocks, (here + s) % count) for s in distances(axis)}


def gather_by_shifts(block, axis):
    here, count = lax.axis_index(axis), lax.axis_size(axis)
    got = {0: block}
    for s in distances(axis):
        got[s] = shift(block, axis, s)
    got = jnp.stack([got[s] for s in range(count)])
    return jnp.stack([pick(got, (here - i) % count) for i in range(count)])


def trade(block, across):
    route = []
    for z in range(2):
        for x in range(4):
            for low in range(4):
                for c in range(2):
                    to_low = 3 - low if across else low
                    to = (((z ^ across) * 4 + x - x % 2 + c) * 4 + to_low) * 2 + x % 2
                    here = ((z * 4 + x) * 4 + low) * 2 + c
                    if to != here:
                        route.append((here, to))
    return lax.ppermute(block, ("zh", "x", "zl", "c"), route)


def mirror(block):
    return lax.ppermute(block, ("zh", "zl"), [(i, 7 - i) for i in range(8)])


def shards(hidden_in, norm_gain, snap_qkv, snap_out, owner_index, block_order):
    rows, width = hidden_in.shape
    ys = ("yh", "yl")
    zh, yh, yl, x, c = (lax.axis_index(name) for name in ("zh", "yh", "yl", "x", "c"))
    y = lax.axis_index(ys)
    ny, nx = 8, 4
    half = rows // 2
    core = c.reshape(1)
    owner = owner_index[0]
    zh0, y0, x0 = owner // (ny * nx), (owner // nx) % ny, owner % nx

    mine = lax.dynamic_slice_in_dim(hidden_in, c * half, half, 0).astype(jnp.float32)
    normed = (
        mine * lax.rsqrt(jnp.mean(mine * mine, axis=-1, keepdims=True) + 1e-06) * norm_gain
    ).astype(jnp.bfloat16)

    order = block_order.reshape(2, ny, nx) * rows
    offsets = jnp.arange(half, dtype=jnp.int32)
    kpos = (pick(order, zh)[:, :, None] + offsets).reshape(-1)
    kpos = jnp.concatenate([kpos + c * half, kpos + (1 - c) * half]).reshape(1, -1)
    here = lax.dynamic_index_in_dim(order, y, 1, keepdims=False)
    start = pick(here, zh) + c * half
    start_other = pick(here, 1 - zh) + c * half

    part = width // (2 * ny)
    w = fold(snap_qkv[0], ny)
    w = pick(exchange(w, "x"), x0)
    wo = snap_out[0].reshape(2, ny // 2, -1, snap_out.shape[2])
    wo = jnp.stack([pick(wo, yh), jnp.flip(pick(wo, 1 - yh), 0)], axis=1)
    wo = take_shifts(pick(wo, yl), ahead(wo, "yl"), "yl", y0 % (ny // 2))
    w, wo, normed, kpos, start, start_other = lax.optimization_barrier(
        (w, wo, normed, kpos, start, start_other)
    )
    w = pick(exchange(w, ys), y0)
    wo = jnp.transpose(wo.reshape(2, -1, nx, snap_out.shape[2] // nx), (2, 0, 1, 3))
    wo = take_shifts(pick(wo, x), ahead(wo, "x"), "x", x0)
    wo = jnp.where(yh == y0 // (ny // 2), wo[0], lax.ppermute(wo[1], ys, [(i, 7 - i) for i in range(8)]))
    wo = jnp.transpose(wo.reshape(wo.shape[0], nx, HD), (1, 0, 2)).reshape(part, HD)
    w = jnp.concatenate([w, wo], axis=1)
    w, normed = lax.optimization_barrier((w, normed))
    w = jnp.where(zh == zh0, jnp.where(x % 2 == c, w, trade(w, 0)), trade(w, 1))
    w = spread(w, ys).reshape(ny * part, 4 * HD)
    normed = gather_by_shifts(normed, "x").reshape(-1, width)
    q, kv = project(core, normed, w, swap(w, "c"), ny)
    wo = w[:, 3 * HD :].reshape(ny, nx, part // nx, HD)
    wo = jnp.transpose(wo, (0, 2, 1, 3)).reshape(ny * part // nx, nx * HD)
    q, kv, wo = lax.optimization_barrier((q, kv, wo))

    near = exchange(kv, ys).reshape(-1, 2 * HD)
    q_other = mirror(q)
    wo = gather_by_shifts(wo, "x")
    near, q_other, wo = lax.optimization_barrier((near, q_other, wo))
    far = swap(near, "c")
    wo_far = swap(wo, "c")

    others = mirror(attend(start_other, q_other, near, far, kpos, half))
    context = merge(attend(start, q, near, far, kpos, half), others)
    context = exchange(context, "x")
    terms = finish(core, context, wo, wo_far)
    terms = exchange(terms, ("zl", "c")).reshape(-1, rows, terms.shape[2])
    return jnp.sum(terms.astype(jnp.float32), axis=0).astype(jnp.bfloat16)


def solution(mesh):
    fine = Mesh(mesh.devices.reshape(2, 2, 4, 4, 4, 2), ("zh", "yh", "yl", "x", "zl", "c"))
    ctx, tp = ("zh", "yh", "yl", "x"), ("zl", "c")
    in_specs = (P(ctx, None), P(), P(ctx, None, None, tp), P(ctx, tp, None), P(), P())
    return jax.shard_map(shards, mesh=fine, in_specs=in_specs, out_specs=P(ctx, tp), check_vma=False)
```

```python
import functools

import jax
import jax.numpy as jnp
import numpy as np
from jax import lax
from jax.experimental import pallas as pl
from jax.experimental.pallas import tpu as pltpu
from jax.sharding import Mesh
from jax.sharding import PartitionSpec as P

HD = 128
HIDE = -1e30
CHUNK = 640
EXTRA = 16
LIMIT = pltpu.CompilerParams(vmem_limit_bytes=24 * 1024 * 1024)


def fold_kernel(w_ref, out_ref):
    part = w_ref.shape[4]
    for h in range(2):
        for k in range(2):
            for j in range(3):
                for x in range(out_ref.shape[0]):
                    out_ref[x, 4 * h : 4 * h + 4, k * part : (k + 1) * part, j * HD : (j + 1) * HD] = w_ref[
                        j, k, :, x, :, h * HD : (h + 1) * HD
                    ]


def fold(w):
    part, steps = w.shape[1] // 32, 2
    return pl.pallas_call(
        fold_kernel,
        grid=(steps,),
        in_specs=[pl.BlockSpec((3, 2, 4, 4 // steps, part, 2 * HD), lambda i: (0, 0, 0, i, 0, 0))],
        out_specs=pl.BlockSpec((4 // steps, 8, 2 * part, 3 * HD), lambda i: (i, 0, 0, 0)),
        out_shape=jax.ShapeDtypeStruct((4, 8, 2 * part, 3 * HD), w.dtype),
        compiler_params=LIMIT,
        cost_estimate=pl.CostEstimate(flops=0, bytes_accessed=4 * w.size, transcendentals=0),
    )(w.reshape(3, 2, 4, 4, part, 2 * HD))


def near_kernel(c_ref, x_ref, w_ref, out_ref):
    depth = w_ref.shape[0]
    span = pl.ds(pl.multiple_of(c_ref[0] * depth, depth), depth)
    w = w_ref[:, : out_ref.shape[1]]
    out_ref[...] = jnp.dot(x_ref[:, span], w, preferred_element_type=jnp.float32)


def far_kernel(c_ref, x_ref, w_ref, sum_ref, q_ref, kv_ref):
    depth = w_ref.shape[0]
    span = pl.ds(pl.multiple_of((1 - c_ref[0]) * depth, depth), depth)
    w = w_ref[:, : sum_ref.shape[1]]
    out = sum_ref[...] + jnp.dot(x_ref[:, span], w, preferred_element_type=jnp.float32)
    q_ref[...] = out[:, :HD].astype(q_ref.dtype)
    kv = out[:, HD:].astype(kv_ref.dtype)
    for i in range(kv_ref.shape[0]):
        kv_ref[i] = kv


def project(core, x, near, far, count):
    n, cols = x.shape[0], 3 * HD
    smem, vmem = pl.BlockSpec(memory_space=pltpu.SMEM), pl.BlockSpec(memory_space=pltpu.VMEM)
    cost = pl.CostEstimate(
        flops=2 * n * near.shape[0] * cols, bytes_accessed=2 * (x.size + near.size), transcendentals=0
    )
    total = pl.pallas_call(
        near_kernel,
        in_specs=[smem, vmem, vmem],
        out_specs=vmem,
        out_shape=jax.ShapeDtypeStruct((n, cols), jnp.float32),
        compiler_params=LIMIT,
        cost_estimate=cost,
    )(core, x, near)
    return pl.pallas_call(
        far_kernel,
        in_specs=[smem, vmem, vmem, vmem],
        out_specs=[vmem, vmem],
        out_shape=[
            jax.ShapeDtypeStruct((n, HD), jnp.bfloat16),
            jax.ShapeDtypeStruct((count, n, 2 * HD), jnp.bfloat16),
        ],
        compiler_params=LIMIT,
        cost_estimate=cost,
    )(core, x, far, total)


def three_parts(value):
    first = value.astype(jnp.bfloat16).astype(jnp.float32)
    rest = value - first
    second = rest.astype(jnp.bfloat16).astype(jnp.float32)
    return first, second, rest - second


def attend_kernel(start_ref, q_ref, near_ref, far_ref, kpos_ref, o_ref, s_ref):
    factor = float(np.log2(np.e) / HD**0.5)
    rows = q_ref.shape[0]
    blocks, half = o_ref.shape[0], o_ref.shape[1] - EXTRA
    row = lax.broadcasted_iota(jnp.int32, (rows, 1), 0)
    first = blocks * pl.program_id(0)
    qpos = row + start_ref[first]
    for b in range(1, blocks):
        qpos = jnp.where(row < b * half, qpos, row - b * half + start_ref[first + b])
    pieces = [
        (ref, j * CHUNK, i * ref.shape[0] + j * CHUNK)
        for i, ref in enumerate((near_ref, far_ref))
        for j in range(ref.shape[0] // CHUNK)
    ]
    q = q_ref[...]
    high = jnp.full((rows, HD), HIDE, jnp.float32)
    for ref, at, column in pieces:
        span = pl.ds(column, CHUNK)
        s = lax.dot_general(
            q, ref[pl.ds(at, CHUNK), :HD], (((1,), (1,)), ((), ())), preferred_element_type=jnp.float32
        )
        s = jnp.where(kpos_ref[:, span] <= qpos, s * factor, HIDE)
        s_ref[:, span] = s
        for t in range(CHUNK // HD):
            high = jnp.maximum(high, s[:, t * HD : (t + 1) * HD])
    top = jnp.max(high, axis=1, keepdims=True)
    base = jnp.where(top <= 0.5 * HIDE, 0.0, top)
    total = jnp.zeros((rows, HD), jnp.float32)
    acc = jnp.zeros((rows, HD), jnp.float32)
    for ref, at, column in pieces:
        span = pl.ds(column, CHUNK)
        p = jnp.exp2(s_ref[:, span] - base)
        for t in range(CHUNK // HD):
            total = total + p[:, t * HD : (t + 1) * HD]
        acc = acc + jnp.dot(
            p.astype(jnp.bfloat16), ref[pl.ds(at, CHUNK), HD:], preferred_element_type=jnp.float32
        )
    total = jnp.sum(total, axis=1, keepdims=True)
    o = acc / jnp.where(total == 0.0, 1.0, total)
    lane = lax.broadcasted_iota(jnp.int32, (rows, HD), 1)
    stat = jnp.zeros((rows, HD), jnp.float32)
    for k, piece in enumerate(three_parts(top) + three_parts(total)):
        stat = jnp.where(lane == k, piece, stat)
    for b in range(blocks):
        o_ref[b, :half, :] = o[b * half : (b + 1) * half].astype(o_ref.dtype)
        block = jnp.concatenate(
            [stat[b * half : (b + 1) * half], jnp.zeros((HD - half, HD), jnp.float32)]
        )
        o_ref[b, half:, :] = block.T[:EXTRA].astype(o_ref.dtype)


def attend(start, q, near, far, kpos, half):
    nq, nk = q.shape[0], 2 * near.shape[0]
    tile = 2 * half
    return pl.pallas_call(
        attend_kernel,
        grid=(nq // tile,),
        in_specs=[
            pl.BlockSpec(memory_space=pltpu.SMEM),
            pl.BlockSpec((tile, HD), lambda i: (i, 0)),
            pl.BlockSpec((nk // 2, 2 * HD), lambda i: (0, 0)),
            pl.BlockSpec((nk // 2, 2 * HD), lambda i: (0, 0)),
            pl.BlockSpec((1, nk), lambda i: (0, 0)),
        ],
        out_specs=pl.BlockSpec((2, half + EXTRA, HD), lambda i: (i, 0, 0)),
        out_shape=jax.ShapeDtypeStruct((nq // half, half + EXTRA, HD), jnp.bfloat16),
        scratch_shapes=[pltpu.VMEM((tile, nk), jnp.float32)],
        compiler_params=LIMIT,
        cost_estimate=pl.CostEstimate(
            flops=4 * nq * nk * HD, bytes_accessed=nk * HD * 4, transcendentals=nq * nk
        ),
    )(start, q, near, far, kpos)


def merge_kernel(*refs):
    part_refs, out_ref = refs[:-1], refs[-1]
    half = out_ref.shape[1]
    for n in range(out_ref.shape[0]):
        tops, totals = [], []
        for ref in part_refs:
            stat = ref[n, half:, :].astype(jnp.float32)
            stat = jnp.concatenate([stat, jnp.zeros((HD - EXTRA, HD), jnp.float32)]).T[:half]
            tops.append(stat[:, 0:1] + stat[:, 1:2] + stat[:, 2:3])
            totals.append(stat[:, 3:4] + stat[:, 4:5] + stat[:, 5:6])
        top = functools.reduce(jnp.maximum, tops)
        weights = [total * jnp.exp2(mine - top) for mine, total in zip(tops, totals)]
        mixed = sum(ref[n, :half, :].astype(jnp.float32) * weight for ref, weight in zip(part_refs, weights))
        out_ref[n] = (mixed / sum(weights)).astype(out_ref.dtype)


def merge(parts):
    blocks, rows = parts[0].shape[0], parts[0].shape[1] - EXTRA
    size = len(parts) * parts[0].size
    vmem = pl.BlockSpec(memory_space=pltpu.VMEM)
    return pl.pallas_call(
        merge_kernel,
        in_specs=[vmem] * len(parts),
        out_specs=vmem,
        out_shape=jax.ShapeDtypeStruct((blocks, rows, HD), jnp.bfloat16),
        compiler_params=LIMIT,
        cost_estimate=pl.CostEstimate(flops=4 * size, bytes_accessed=3 * size, transcendentals=0),
    )(*parts)


def finish_kernel(c_ref, context_ref, near_ref, far_ref, out_ref):
    low = jnp.concatenate([context_ref[0], context_ref[1]], axis=1)
    high = jnp.concatenate([context_ref[2], context_ref[3]], axis=1)
    first = c_ref[0] == 0
    near = jnp.where(first, low, high)
    far = jnp.where(first, high, low)
    width = out_ref.shape[2]
    for n in range(near_ref.shape[0]):
        terms = jnp.dot(near, near_ref[n], preferred_element_type=jnp.float32)
        terms += jnp.dot(far, far_ref[n], preferred_element_type=jnp.float32)
        terms = terms.astype(out_ref.dtype)
        out_ref[2 * n] = terms[:, :width]
        out_ref[2 * n + 1] = terms[:, width:]


def finish(core, context, near, far):
    half = context.shape[1]
    blocks, _, cols = near.shape
    vmem = pl.BlockSpec(memory_space=pltpu.VMEM)
    return pl.pallas_call(
        finish_kernel,
        in_specs=[pl.BlockSpec(memory_space=pltpu.SMEM), vmem, vmem, vmem],
        out_specs=vmem,
        out_shape=jax.ShapeDtypeStruct((2 * blocks, half, cols // 2), jnp.bfloat16),
        compiler_params=LIMIT,
        cost_estimate=pl.CostEstimate(
            flops=4 * half * near.size, bytes_accessed=4 * near.size, transcendentals=0
        ),
    )(core, context, near, far)


def swap(block, axis):
    return lax.ppermute(block, axis, [(0, 1), (1, 0)])


def exchange(block, axis):
    return lax.all_to_all(block, axis, 0, 0, tiled=True)


def pick(blocks, index):
    return lax.dynamic_index_in_dim(blocks, index, 0, keepdims=False)


def spread(block, axis):
    count = lax.axis_size(axis)
    return exchange(jnp.broadcast_to(block[None], (count,) + block.shape), axis)


def shift(block, axis, distance):
    count = lax.axis_size(axis)
    return lax.ppermute(block, axis, [(i, (i + distance) % count) for i in range(count)])


def distances(axis):
    count = lax.axis_size(axis)
    return sorted(range(1, count), key=lambda s: -min(s, count - s))


def take_shifts(result, blocks, axis, source):
    behind = (lax.axis_index(axis) - source) % lax.axis_size(axis)
    for s, block in blocks.items():
        result = jnp.where(behind == s, shift(block, axis, s), result)
    return result


def ahead(blocks, axis):
    here, count = lax.axis_index(axis), blocks.shape[0]
    return {s: pick(blocks, (here + s) % count) for s in distances(axis)}


def mirror(block, axes):
    return lax.ppermute(block, axes, [(i, 7 - i) for i in range(8)])


def by_index(mine, other, index):
    return [jnp.where(index == 0, mine, other), jnp.where(index == 0, other, mine)]


def shards(hidden_in, norm_gain, snap_qkv, snap_out, owner_index, block_order):
    rows, width = hidden_in.shape
    ys = ("yh", "yl")
    zh, yh, yl, x, c = (lax.axis_index(name) for name in ("zh", "yh", "yl", "x", "c"))
    ny, nx = 8, 4
    half = rows // 2
    core = c.reshape(1)
    owner = owner_index[0]
    zh0, y0, x0 = owner // (ny * nx), (owner // nx) % ny, owner % nx

    mine = lax.dynamic_slice_in_dim(hidden_in, c * half, half, 0).astype(jnp.float32)
    normed = (
        mine * lax.rsqrt(jnp.mean(mine * mine, axis=-1, keepdims=True) + 1e-06) * norm_gain
    ).astype(jnp.bfloat16)
    normed = jnp.concatenate(by_index(normed, swap(normed, "yh"), yh))

    order = block_order.reshape(2, 2, ny // 2, nx) * rows
    offsets = jnp.arange(half, dtype=jnp.int32)
    kpos = jnp.transpose(lax.dynamic_index_in_dim(order, x, 3, keepdims=False), (2, 0, 1)).reshape(-1)
    kpos = (kpos[:, None] + offsets).reshape(-1)
    kpos = jnp.concatenate([kpos + c * half, kpos + (1 - c) * half]).reshape(1, -1)
    order = lax.dynamic_index_in_dim(order, yl, 2, keepdims=False).reshape(-1, nx) + c * half
    start = {s: lax.dynamic_index_in_dim(order, (x - s) % nx, 1, keepdims=False) for s in range(nx)}

    w = fold(snap_qkv[0])
    w = pick(exchange(w, "x"), x0)
    wo = snap_out[0].reshape(2, ny // 2, -1, snap_out.shape[2])
    wo = jnp.stack([pick(wo, yh), jnp.flip(pick(wo, 1 - yh), 0)], axis=1)
    wo = take_shifts(pick(wo, yl), ahead(wo, "yl"), "yl", y0 % (ny // 2))
    w, wo, normed, kpos, start = lax.optimization_barrier((w, wo, normed, kpos, start))
    w = pick(exchange(w, ys), y0)
    wo = jnp.transpose(wo.reshape(2, -1, nx, snap_out.shape[2] // nx), (2, 0, 1, 3))
    wo = take_shifts(pick(wo, x), ahead(wo, "x"), "x", x0)
    wo = jnp.where(yh == y0 // (ny // 2), wo[0], mirror(wo[1], ys))
    w, wo, normed = lax.optimization_barrier((w, wo, normed))

    w = w.reshape(2, -1, 3 * HD)
    same, cross = pick(w, c), pick(w, 1 - c)
    part = same.shape[0]
    there = jnp.where(
        c == zh,
        lax.ppermute(same, ("zh", "c"), [(2, 0), (1, 3)]),
        lax.ppermute(cross, ("zh", "c"), [(2, 1), (1, 2)]),
    )
    here = jnp.where(c == zh, same, lax.ppermute(cross, ("zh", "c"), [(0, 1), (3, 2)]))
    w = jnp.where(zh == zh0, here, there)
    wo = jnp.where(zh == zh0, wo, swap(wo, "zh"))
    wide = wo.shape[1] // 2
    w = jnp.concatenate([w, jnp.concatenate([wo[:, :wide], wo[:, wide:]])], axis=1)
    w = spread(w, ("yl", "x"))
    normed = jnp.concatenate(by_index(normed, mirror(normed, ("zh", "zl")), zh))
    wo = w[:, :, 3 * HD :].reshape(ny // 2, nx, 2, -1, wide)
    wo = jnp.transpose(wo, (1, 0, 3, 2, 4)).reshape(nx, -1, 2 * wide)
    w = w.reshape(nx * (ny // 2) * part, -1)
    q, kv = project(core, normed, w, swap(w, "c"), ny // 2)
    q, kv, wo = lax.optimization_barrier((q, kv, wo))

    near = exchange(kv, "yl").reshape(-1, 2 * HD)
    queries = {s: shift(q, "x", s) for s in distances("x")}
    wo = jnp.concatenate(by_index(wo, mirror(wo, ys), yh), axis=1)
    near, queries, wo = lax.optimization_barrier((near, queries, wo))
    far = swap(near, "c")
    wo_far = swap(wo, "c")

    parts = []
    for s in distances("x"):
        parts.append(shift(attend(start[s], queries[s], near, far, kpos, half), "x", nx - s))
    context = merge([attend(start[0], q, near, far, kpos, half)] + parts)
    context = exchange(context, ("zh", "yh"))
    terms = finish(core, context, wo, wo_far)
    terms = exchange(terms, ("zl", "c")).reshape(-1, rows, terms.shape[2])
    return jnp.sum(terms.astype(jnp.float32), axis=0).astype(jnp.bfloat16)


def solution(mesh):
    fine = Mesh(mesh.devices.reshape(2, 2, 4, 4, 4, 2), ("zh", "yh", "yl", "x", "zl", "c"))
    ctx, tp = ("zh", "yh", "yl", "x"), ("zl", "c")
    in_specs = (P(ctx, None), P(), P(ctx, None, None, tp), P(ctx, tp, None), P(), P())
    return jax.shard_map(shards, mesh=fine, in_specs=in_specs, out_specs=P(ctx, tp), check_vma=False)
```

```python
import jax
import jax.numpy as jnp
import numpy as np
from jax import lax
from jax.experimental import pallas as pl
from jax.experimental.pallas import tpu as pltpu
from jax.sharding import Mesh
from jax.sharding import PartitionSpec as P

HD = 128
HIDE = -1e30
CHUNK = 640
EXTRA = 16
WHOLE = pltpu.CompilerParams(vmem_limit_bytes=56 * 1024 * 1024)
LIMIT = pltpu.CompilerParams(vmem_limit_bytes=24 * 1024 * 1024)


def fold_kernel(w_ref, out_ref):
    for h in range(2):
        for r in range(2):
            for j in range(3):
                out_ref[2 * h + r, :, :, j * HD : (j + 1) * HD] = w_ref[j, r, :, :, h * HD : (h + 1) * HD]


def fold(w, ny):
    part, steps = w.shape[1] // (2 * ny), 2
    return pl.pallas_call(
        fold_kernel,
        grid=(steps,),
        in_specs=[pl.BlockSpec((3, 2, ny // steps, part, 2 * HD), lambda i: (0, 0, i, 0, 0))],
        out_specs=pl.BlockSpec((4, ny // steps, part, 3 * HD), lambda i: (0, i, 0, 0)),
        out_shape=jax.ShapeDtypeStruct((4, ny, part, 3 * HD), w.dtype),
        compiler_params=WHOLE,
        cost_estimate=pl.CostEstimate(flops=0, bytes_accessed=4 * w.size, transcendentals=0),
    )(w.reshape(3, 2, ny, part, 2 * HD))


def near_kernel(c_ref, x_ref, w_ref, out_ref):
    depth = w_ref.shape[0]
    span = pl.ds(pl.multiple_of(c_ref[0] * depth, depth), depth)
    w = w_ref[:, : out_ref.shape[1]]
    out_ref[...] = jnp.dot(x_ref[:, span], w, preferred_element_type=jnp.float32)


def far_kernel(c_ref, x_ref, w_ref, sum_ref, q_ref, kv_ref):
    depth = w_ref.shape[0]
    span = pl.ds(pl.multiple_of((1 - c_ref[0]) * depth, depth), depth)
    w = w_ref[:, : sum_ref.shape[1]]
    out = sum_ref[...] + jnp.dot(x_ref[:, span], w, preferred_element_type=jnp.float32)
    q_ref[...] = out[:, :HD].astype(q_ref.dtype)
    kv = out[:, HD:].astype(kv_ref.dtype)
    for i in range(kv_ref.shape[0]):
        kv_ref[i] = kv


def project(core, x, near, far, count):
    n, cols = x.shape[0], 3 * HD
    smem, vmem = pl.BlockSpec(memory_space=pltpu.SMEM), pl.BlockSpec(memory_space=pltpu.VMEM)
    cost = pl.CostEstimate(
        flops=2 * n * near.shape[0] * cols, bytes_accessed=2 * (x.size + near.size), transcendentals=0
    )
    total = pl.pallas_call(
        near_kernel,
        in_specs=[smem, vmem, vmem],
        out_specs=vmem,
        out_shape=jax.ShapeDtypeStruct((n, cols), jnp.float32),
        compiler_params=LIMIT,
        cost_estimate=cost,
    )(core, x, near)
    return pl.pallas_call(
        far_kernel,
        in_specs=[smem, vmem, vmem, vmem],
        out_specs=[vmem, vmem],
        out_shape=[
            jax.ShapeDtypeStruct((n, HD), jnp.bfloat16),
            jax.ShapeDtypeStruct((count, n, 2 * HD), jnp.bfloat16),
        ],
        compiler_params=LIMIT,
        cost_estimate=cost,
    )(core, x, far, total)


def three_parts(value):
    first = value.astype(jnp.bfloat16).astype(jnp.float32)
    rest = value - first
    second = rest.astype(jnp.bfloat16).astype(jnp.float32)
    return first, second, rest - second


def attend_kernel(start_ref, q_ref, near_ref, far_ref, kpos_ref, o_ref, s_ref):
    factor = float(np.log2(np.e) / HD**0.5)
    rows = q_ref.shape[0]
    blocks, half = o_ref.shape[0], o_ref.shape[1] - EXTRA
    row = lax.broadcasted_iota(jnp.int32, (rows, 1), 0)
    first = blocks * pl.program_id(0)
    qpos = row + start_ref[first]
    for b in range(1, blocks):
        qpos = jnp.where(row < b * half, qpos, row - b * half + start_ref[first + b])
    pieces = [
        (ref, j * CHUNK, i * ref.shape[0] + j * CHUNK)
        for i, ref in enumerate((near_ref, far_ref))
        for j in range(ref.shape[0] // CHUNK)
    ]
    q = q_ref[...]
    high = jnp.full((rows, HD), HIDE, jnp.float32)
    for ref, at, column in pieces:
        span = pl.ds(column, CHUNK)
        s = lax.dot_general(
            q, ref[pl.ds(at, CHUNK), :HD], (((1,), (1,)), ((), ())), preferred_element_type=jnp.float32
        )
        s = jnp.where(kpos_ref[:, span] <= qpos, s * factor, HIDE)
        s_ref[:, span] = s
        for t in range(CHUNK // HD):
            high = jnp.maximum(high, s[:, t * HD : (t + 1) * HD])
    top = jnp.max(high, axis=1, keepdims=True)
    base = jnp.where(top <= 0.5 * HIDE, 0.0, top)
    total = jnp.zeros((rows, HD), jnp.float32)
    acc = jnp.zeros((rows, HD), jnp.float32)
    for ref, at, column in pieces:
        span = pl.ds(column, CHUNK)
        p = jnp.exp2(s_ref[:, span] - base)
        for t in range(CHUNK // HD):
            total = total + p[:, t * HD : (t + 1) * HD]
        acc = acc + jnp.dot(
            p.astype(jnp.bfloat16), ref[pl.ds(at, CHUNK), HD:], preferred_element_type=jnp.float32
        )
    total = jnp.sum(total, axis=1, keepdims=True)
    o = acc / jnp.where(total == 0.0, 1.0, total)
    lane = lax.broadcasted_iota(jnp.int32, (rows, HD), 1)
    stat = jnp.zeros((rows, HD), jnp.float32)
    for k, piece in enumerate(three_parts(top) + three_parts(total)):
        stat = jnp.where(lane == k, piece, stat)
    for b in range(blocks):
        o_ref[b, :half, :] = o[b * half : (b + 1) * half].astype(o_ref.dtype)
        block = jnp.concatenate(
            [stat[b * half : (b + 1) * half], jnp.zeros((HD - half, HD), jnp.float32)]
        )
        o_ref[b, half:, :] = block.T[:EXTRA].astype(o_ref.dtype)


def attend(start, q, near, far, kpos, half):
    nq, nk = q.shape[0], 2 * near.shape[0]
    tile = 4 * half
    return pl.pallas_call(
        attend_kernel,
        grid=(nq // tile,),
        in_specs=[
            pl.BlockSpec(memory_space=pltpu.SMEM),
            pl.BlockSpec((tile, HD), lambda i: (i, 0)),
            pl.BlockSpec((nk // 2, 2 * HD), lambda i: (0, 0)),
            pl.BlockSpec((nk // 2, 2 * HD), lambda i: (0, 0)),
            pl.BlockSpec((1, nk), lambda i: (0, 0)),
        ],
        out_specs=pl.BlockSpec((4, half + EXTRA, HD), lambda i: (i, 0, 0)),
        out_shape=jax.ShapeDtypeStruct((nq // half, half + EXTRA, HD), jnp.bfloat16),
        scratch_shapes=[pltpu.VMEM((tile, nk), jnp.float32)],
        compiler_params=LIMIT,
        cost_estimate=pl.CostEstimate(
            flops=4 * nq * nk * HD, bytes_accessed=nk * HD * 4, transcendentals=nq * nk
        ),
    )(start, q, near, far, kpos)


def merge_kernel(near_ref, far_ref, out_ref):
    nx, half = out_ref.shape[0], out_ref.shape[1]
    for x in range(nx):
        tops, totals = [], []
        for ref in (near_ref, far_ref):
            stat = ref[x, half:, :].astype(jnp.float32)
            stat = jnp.concatenate([stat, jnp.zeros((HD - EXTRA, HD), jnp.float32)]).T[:half]
            tops.append(stat[:, 0:1] + stat[:, 1:2] + stat[:, 2:3])
            totals.append(stat[:, 3:4] + stat[:, 4:5] + stat[:, 5:6])
        top = jnp.maximum(tops[0], tops[1])
        a = totals[0] * jnp.exp2(tops[0] - top)
        b = totals[1] * jnp.exp2(tops[1] - top)
        mixed = near_ref[x, :half, :].astype(jnp.float32) * a + far_ref[x, :half, :].astype(jnp.float32) * b
        out_ref[x] = (mixed / (a + b)).astype(out_ref.dtype)


def merge(near, far):
    nx, rows = near.shape[0], near.shape[1] - EXTRA
    vmem = pl.BlockSpec(memory_space=pltpu.VMEM)
    return pl.pallas_call(
        merge_kernel,
        in_specs=[vmem, vmem],
        out_specs=vmem,
        out_shape=jax.ShapeDtypeStruct((nx, rows, HD), jnp.bfloat16),
        compiler_params=LIMIT,
        cost_estimate=pl.CostEstimate(flops=8 * near.size, bytes_accessed=6 * near.size, transcendentals=0),
    )(near, far)


def finish_kernel(c_ref, context_ref, near_ref, far_ref, out_ref):
    low = jnp.concatenate([context_ref[0], context_ref[2]], axis=1)
    high = jnp.concatenate([context_ref[1], context_ref[3]], axis=1)
    width = out_ref.shape[2]
    for ref, odd in ((near_ref, c_ref[0]), (far_ref, 1 - c_ref[0])):
        for h in range(2):
            terms = jnp.dot(low, ref[2 * h], preferred_element_type=jnp.float32)
            terms += jnp.dot(high, ref[2 * h + 1], preferred_element_type=jnp.float32)
            terms = terms.astype(out_ref.dtype)
            at = 2 * (2 * h + odd)
            out_ref[at] = terms[:, :width]
            out_ref[at + 1] = terms[:, width:]


def finish(core, context, near, far):
    half = context.shape[1]
    blocks, _, cols = near.shape
    vmem = pl.BlockSpec(memory_space=pltpu.VMEM)
    return pl.pallas_call(
        finish_kernel,
        in_specs=[pl.BlockSpec(memory_space=pltpu.SMEM), vmem, vmem, vmem],
        out_specs=vmem,
        out_shape=jax.ShapeDtypeStruct((2 * blocks, half, cols // 2), jnp.bfloat16),
        compiler_params=LIMIT,
        cost_estimate=pl.CostEstimate(
            flops=4 * half * near.size, bytes_accessed=4 * near.size, transcendentals=0
        ),
    )(core, context, near, far)


def swap(block, axis):
    return lax.ppermute(block, axis, [(0, 1), (1, 0)])


def exchange(block, axis):
    return lax.all_to_all(block, axis, 0, 0, tiled=True)


def pick(blocks, index):
    return lax.dynamic_index_in_dim(blocks, index, 0, keepdims=False)


def spread(block, axis):
    count = lax.axis_size(axis)
    return exchange(jnp.broadcast_to(block[None], (count,) + block.shape), axis)


def shift(block, axis, distance):
    count = lax.axis_size(axis)
    return lax.ppermute(block, axis, [(i, (i + distance) % count) for i in range(count)])


def distances(axis):
    count = lax.axis_size(axis)
    return sorted(range(1, count), key=lambda s: -min(s, count - s))


def take_shifts(result, blocks, axis, source):
    behind = (lax.axis_index(axis) - source) % lax.axis_size(axis)
    for s, block in blocks.items():
        result = jnp.where(behind == s, shift(block, axis, s), result)
    return result


def ahead(blocks, axis):
    here, count = lax.axis_index(axis), blocks.shape[0]
    return {s: pick(blocks, (here + s) % count) for s in distances(axis)}


def gather_by_shifts(block, axis):
    here, count = lax.axis_index(axis), lax.axis_size(axis)
    got = {0: block}
    for s in distances(axis):
        got[s] = shift(block, axis, s)
    got = jnp.stack([got[s] for s in range(count)])
    return jnp.stack([pick(got, (here - i) % count) for i in range(count)])


def trade(block, across):
    route = []
    for z in range(2):
        for x in range(4):
            for low in range(4):
                for c in range(2):
                    to_low = 3 - low if across else low
                    to = (((z ^ across) * 4 + x - x % 2 + c) * 4 + to_low) * 2 + x % 2
                    here = ((z * 4 + x) * 4 + low) * 2 + c
                    if to != here:
                        route.append((here, to))
    return lax.ppermute(block, ("zh", "x", "zl", "c"), route)


def mirror(block):
    return lax.ppermute(block, ("zh", "zl"), [(i, 7 - i) for i in range(8)])


def shards(hidden_in, norm_gain, snap_qkv, snap_out, owner_index, block_order):
    rows, width = hidden_in.shape
    ys = ("yh", "yl")
    zh, yh, yl, x, c = (lax.axis_index(name) for name in ("zh", "yh", "yl", "x", "c"))
    y = lax.axis_index(ys)
    ny, nx = 8, 4
    half = rows // 2
    core = c.reshape(1)
    owner = owner_index[0]
    zh0, y0, x0 = owner // (ny * nx), (owner // nx) % ny, owner % nx

    mine = lax.dynamic_slice_in_dim(hidden_in, c * half, half, 0).astype(jnp.float32)
    normed = (
        mine * lax.rsqrt(jnp.mean(mine * mine, axis=-1, keepdims=True) + 1e-06) * norm_gain
    ).astype(jnp.bfloat16)

    order = block_order.reshape(2, ny, nx) * rows
    offsets = jnp.arange(half, dtype=jnp.int32)
    kpos = (pick(order, zh)[:, :, None] + offsets).reshape(-1)
    kpos = jnp.concatenate([kpos + c * half, kpos + (1 - c) * half]).reshape(1, -1)
    here = lax.dynamic_index_in_dim(order, y, 1, keepdims=False)
    start = pick(here, zh) + c * half
    start_other = pick(here, 1 - zh) + c * half

    part = width // (2 * ny)
    w = fold(snap_qkv[0], ny)
    w = pick(exchange(w, "x"), x0)
    wo = snap_out[0].reshape(2, ny // 2, -1, snap_out.shape[2])
    wo = jnp.stack([pick(wo, yh), jnp.flip(pick(wo, 1 - yh), 0)], axis=1)
    wo = take_shifts(pick(wo, yl), ahead(wo, "yl"), "yl", y0 % (ny // 2))
    w, wo, normed, kpos, start, start_other = lax.optimization_barrier(
        (w, wo, normed, kpos, start, start_other)
    )
    w = pick(exchange(w, ys), y0)
    wo = jnp.transpose(wo.reshape(2, -1, nx, snap_out.shape[2] // nx), (2, 0, 1, 3))
    wo = take_shifts(pick(wo, x), ahead(wo, "x"), "x", x0)
    wo = jnp.where(yh == y0 // (ny // 2), wo[0], lax.ppermute(wo[1], ys, [(i, 7 - i) for i in range(8)]))
    wo = jnp.transpose(wo.reshape(wo.shape[0], nx, HD), (1, 0, 2)).reshape(part, HD)
    w = jnp.concatenate([w, wo], axis=1)
    w, normed = lax.optimization_barrier((w, normed))
    w = jnp.where(zh == zh0, jnp.where(x % 2 == c, w, trade(w, 0)), trade(w, 1))
    w = spread(w, ys).reshape(ny * part, 4 * HD)
    normed = gather_by_shifts(normed, "x").reshape(-1, width)
    q, kv = project(core, normed, w, swap(w, "c"), ny)
    wo = w[:, 3 * HD :].reshape(ny, nx, part // nx, HD)
    wo = jnp.transpose(wo, (0, 2, 1, 3)).reshape(ny * part // nx, nx * HD)
    q, kv, wo = lax.optimization_barrier((q, kv, wo))

    near = exchange(kv, ys).reshape(-1, 2 * HD)
    q_other = mirror(q)
    wo = gather_by_shifts(wo, "x")
    near, q_other, wo = lax.optimization_barrier((near, q_other, wo))
    far = swap(near, "c")
    wo_far = swap(wo, "c")

    others = mirror(attend(start_other, q_other, near, far, kpos, half))
    context = merge(attend(start, q, near, far, kpos, half), others)
    context = exchange(context, "x")
    terms = finish(core, context, wo, wo_far)
    terms = exchange(terms, ("zl", "c")).reshape(-1, rows, terms.shape[2])
    return jnp.sum(terms.astype(jnp.float32), axis=0).astype(jnp.bfloat16)


def solution(mesh):
    fine = Mesh(mesh.devices.reshape(2, 2, 4, 4, 4, 2), ("zh", "yh", "yl", "x", "zl", "c"))
    ctx, tp = ("zh", "yh", "yl", "x"), ("zl", "c")
    in_specs = (P(ctx, None), P(), P(ctx, None, None, tp), P(ctx, tp, None), P(), P())
    return jax.shard_map(shards, mesh=fine, in_specs=in_specs, out_specs=P(ctx, tp), check_vma=False)
```

```python
import jax
import jax.numpy as jnp
import numpy as np
from jax import lax
from jax.experimental import pallas as pl
from jax.experimental.pallas import tpu as pltpu
from jax.sharding import Mesh
from jax.sharding import PartitionSpec as P

HD = 128
HIDE = -1e30
CHUNK = 640
EXTRA = 16
WHOLE = pltpu.CompilerParams(vmem_limit_bytes=56 * 1024 * 1024)
LIMIT = pltpu.CompilerParams(vmem_limit_bytes=24 * 1024 * 1024)


def fold_kernel(w_ref, out_ref):
    for h in range(2):
        for r in range(2):
            for j in range(3):
                out_ref[2 * h + r, :, :, j * HD : (j + 1) * HD] = w_ref[j, r, :, :, h * HD : (h + 1) * HD]


def fold(w, ny):
    part, steps = w.shape[1] // (2 * ny), 2
    return pl.pallas_call(
        fold_kernel,
        grid=(steps,),
        in_specs=[pl.BlockSpec((3, 2, ny // steps, part, 2 * HD), lambda i: (0, 0, i, 0, 0))],
        out_specs=pl.BlockSpec((4, ny // steps, part, 3 * HD), lambda i: (0, i, 0, 0)),
        out_shape=jax.ShapeDtypeStruct((4, ny, part, 3 * HD), w.dtype),
        compiler_params=WHOLE,
        cost_estimate=pl.CostEstimate(flops=0, bytes_accessed=4 * w.size, transcendentals=0),
    )(w.reshape(3, 2, ny, part, 2 * HD))


def near_kernel(c_ref, *refs):
    x_refs, w_ref, out_ref = refs[:-2], refs[-2], refs[-1]
    depth = w_ref.shape[0]
    span = pl.ds(pl.multiple_of(c_ref[0] * depth, depth), depth)
    x = jnp.concatenate([ref[:, span] for ref in x_refs])
    out_ref[...] = jnp.dot(x, w_ref[:, : out_ref.shape[1]], preferred_element_type=jnp.float32)


def far_kernel(c_ref, *refs):
    x_refs, (w_ref, sum_ref, q_ref, kv_ref) = refs[:-4], refs[-4:]
    depth = w_ref.shape[0]
    span = pl.ds(pl.multiple_of((1 - c_ref[0]) * depth, depth), depth)
    x = jnp.concatenate([ref[:, span] for ref in x_refs])
    w = w_ref[:, : sum_ref.shape[1]]
    out = sum_ref[...] + jnp.dot(x, w, preferred_element_type=jnp.float32)
    q_ref[...] = out[:, :HD].astype(q_ref.dtype)
    kv = out[:, HD:].astype(kv_ref.dtype)
    for i in range(kv_ref.shape[0]):
        kv_ref[i] = kv


def project(core, x, near, far, count):
    n, cols = sum(block.shape[0] for block in x), 3 * HD
    smem, vmem = pl.BlockSpec(memory_space=pltpu.SMEM), pl.BlockSpec(memory_space=pltpu.VMEM)
    cost = pl.CostEstimate(
        flops=2 * n * near.shape[0] * cols, bytes_accessed=2 * (2 * n + cols) * near.shape[0], transcendentals=0
    )
    total = pl.pallas_call(
        near_kernel,
        in_specs=[smem] + [vmem] * (len(x) + 1),
        out_specs=vmem,
        out_shape=jax.ShapeDtypeStruct((n, cols), jnp.float32),
        compiler_params=LIMIT,
        cost_estimate=cost,
    )(core, *x, near)
    return pl.pallas_call(
        far_kernel,
        in_specs=[smem] + [vmem] * (len(x) + 2),
        out_specs=[vmem, vmem],
        out_shape=[
            jax.ShapeDtypeStruct((n, HD), jnp.bfloat16),
            jax.ShapeDtypeStruct((count, n, 2 * HD), jnp.bfloat16),
        ],
        compiler_params=LIMIT,
        cost_estimate=cost,
    )(core, *x, far, total)


def three_parts(value):
    first = value.astype(jnp.bfloat16).astype(jnp.float32)
    rest = value - first
    second = rest.astype(jnp.bfloat16).astype(jnp.float32)
    return first, second, rest - second


def attend_kernel(start_ref, q_ref, near_ref, far_ref, kpos_ref, o_ref, s_ref):
    factor = float(np.log2(np.e) / HD**0.5)
    rows = q_ref.shape[0]
    blocks, half = o_ref.shape[0], o_ref.shape[1] - EXTRA
    row = lax.broadcasted_iota(jnp.int32, (rows, 1), 0)
    first = blocks * pl.program_id(0)
    qpos = row + start_ref[first]
    for b in range(1, blocks):
        qpos = jnp.where(row < b * half, qpos, row - b * half + start_ref[first + b])
    pieces = [
        (ref, j * CHUNK, i * ref.shape[0] + j * CHUNK)
        for i, ref in enumerate((near_ref, far_ref))
        for j in range(ref.shape[0] // CHUNK)
    ]
    q = q_ref[...]
    high = jnp.full((rows, HD), HIDE, jnp.float32)
    for ref, at, column in pieces:
        span = pl.ds(column, CHUNK)
        s = lax.dot_general(
            q, ref[pl.ds(at, CHUNK), :HD], (((1,), (1,)), ((), ())), preferred_element_type=jnp.float32
        )
        s = jnp.where(kpos_ref[:, span] <= qpos, s * factor, HIDE)
        s_ref[:, span] = s
        for t in range(CHUNK // HD):
            high = jnp.maximum(high, s[:, t * HD : (t + 1) * HD])
    top = jnp.max(high, axis=1, keepdims=True)
    base = jnp.where(top <= 0.5 * HIDE, 0.0, top)
    total = jnp.zeros((rows, HD), jnp.float32)
    acc = jnp.zeros((rows, HD), jnp.float32)
    for ref, at, column in pieces:
        span = pl.ds(column, CHUNK)
        p = jnp.exp2(s_ref[:, span] - base)
        for t in range(CHUNK // HD):
            total = total + p[:, t * HD : (t + 1) * HD]
        acc = acc + jnp.dot(
            p.astype(jnp.bfloat16), ref[pl.ds(at, CHUNK), HD:], preferred_element_type=jnp.float32
        )
    total = jnp.sum(total, axis=1, keepdims=True)
    o = acc / jnp.where(total == 0.0, 1.0, total)
    lane = lax.broadcasted_iota(jnp.int32, (rows, HD), 1)
    stat = jnp.zeros((rows, HD), jnp.float32)
    for k, piece in enumerate(three_parts(top) + three_parts(total)):
        stat = jnp.where(lane == k, piece, stat)
    for b in range(blocks):
        o_ref[b, :half, :] = o[b * half : (b + 1) * half].astype(o_ref.dtype)
        block = jnp.concatenate(
            [stat[b * half : (b + 1) * half], jnp.zeros((HD - half, HD), jnp.float32)]
        )
        o_ref[b, half:, :] = block.T[:EXTRA].astype(o_ref.dtype)


def attend(start, q, near, far, kpos, half):
    nq, nk = q.shape[0], 2 * near.shape[0]
    tile = 4 * half
    return pl.pallas_call(
        attend_kernel,
        grid=(nq // tile,),
        in_specs=[
            pl.BlockSpec(memory_space=pltpu.SMEM),
            pl.BlockSpec((tile, HD), lambda i: (i, 0)),
            pl.BlockSpec((nk // 2, 2 * HD), lambda i: (0, 0)),
            pl.BlockSpec((nk // 2, 2 * HD), lambda i: (0, 0)),
            pl.BlockSpec((1, nk), lambda i: (0, 0)),
        ],
        out_specs=pl.BlockSpec((4, half + EXTRA, HD), lambda i: (i, 0, 0)),
        out_shape=jax.ShapeDtypeStruct((nq // half, half + EXTRA, HD), jnp.bfloat16),
        scratch_shapes=[pltpu.VMEM((tile, nk), jnp.float32)],
        compiler_params=LIMIT,
        cost_estimate=pl.CostEstimate(
            flops=4 * nq * nk * HD, bytes_accessed=nk * HD * 4, transcendentals=nq * nk
        ),
    )(start, q, near, far, kpos)


def merge_kernel(x_ref, near_ref, far_ref, out_ref):
    nx, half = out_ref.shape[0], out_ref.shape[1]
    for s in range(nx):
        tops, totals = [], []
        for ref in (near_ref, far_ref):
            stat = ref[s, half:, :].astype(jnp.float32)
            stat = jnp.concatenate([stat, jnp.zeros((HD - EXTRA, HD), jnp.float32)]).T[:half]
            tops.append(stat[:, 0:1] + stat[:, 1:2] + stat[:, 2:3])
            totals.append(stat[:, 3:4] + stat[:, 4:5] + stat[:, 5:6])
        top = jnp.maximum(tops[0], tops[1])
        a = totals[0] * jnp.exp2(tops[0] - top)
        b = totals[1] * jnp.exp2(tops[1] - top)
        mixed = near_ref[s, :half, :].astype(jnp.float32) * a + far_ref[s, :half, :].astype(jnp.float32) * b
        out_ref[lax.rem(x_ref[0] + nx - s, nx)] = (mixed / (a + b)).astype(out_ref.dtype)


def merge(x, near, far):
    nx, rows = near.shape[0], near.shape[1] - EXTRA
    vmem = pl.BlockSpec(memory_space=pltpu.VMEM)
    return pl.pallas_call(
        merge_kernel,
        in_specs=[pl.BlockSpec(memory_space=pltpu.SMEM), vmem, vmem],
        out_specs=vmem,
        out_shape=jax.ShapeDtypeStruct((nx, rows, HD), jnp.bfloat16),
        compiler_params=LIMIT,
        cost_estimate=pl.CostEstimate(flops=8 * near.size, bytes_accessed=6 * near.size, transcendentals=0),
    )(x, near, far)


def finish_kernel(c_ref, context_ref, near_ref, far_ref, out_ref):
    low = jnp.concatenate([context_ref[0], context_ref[2]], axis=1)
    high = jnp.concatenate([context_ref[1], context_ref[3]], axis=1)
    width = out_ref.shape[2]
    for ref, odd in ((near_ref, c_ref[0]), (far_ref, 1 - c_ref[0])):
        for h in range(2):
            terms = jnp.dot(low, ref[2 * h], preferred_element_type=jnp.float32)
            terms += jnp.dot(high, ref[2 * h + 1], preferred_element_type=jnp.float32)
            terms = terms.astype(out_ref.dtype)
            at = 2 * (2 * h + odd)
            out_ref[at] = terms[:, :width]
            out_ref[at + 1] = terms[:, width:]


def finish(core, context, near, far):
    half = context.shape[1]
    blocks, _, cols = near.shape
    vmem = pl.BlockSpec(memory_space=pltpu.VMEM)
    return pl.pallas_call(
        finish_kernel,
        in_specs=[pl.BlockSpec(memory_space=pltpu.SMEM), vmem, vmem, vmem],
        out_specs=vmem,
        out_shape=jax.ShapeDtypeStruct((2 * blocks, half, cols // 2), jnp.bfloat16),
        compiler_params=LIMIT,
        cost_estimate=pl.CostEstimate(
            flops=4 * half * near.size, bytes_accessed=4 * near.size, transcendentals=0
        ),
    )(core, context, near, far)


def swap(block, axis):
    return lax.ppermute(block, axis, [(0, 1), (1, 0)])


def exchange(block, axis):
    return lax.all_to_all(block, axis, 0, 0, tiled=True)


def pick(blocks, index):
    return lax.dynamic_index_in_dim(blocks, index, 0, keepdims=False)


def spread(block, axis):
    count = lax.axis_size(axis)
    return exchange(jnp.broadcast_to(block[None], (count,) + block.shape), axis)


def shift(block, axis, distance):
    count = lax.axis_size(axis)
    return lax.ppermute(block, axis, [(i, (i + distance) % count) for i in range(count)])


def distances(axis):
    count = lax.axis_size(axis)
    return sorted(range(1, count), key=lambda s: -min(s, count - s))


def take_shifts(result, blocks, axis, source):
    behind = (lax.axis_index(axis) - source) % lax.axis_size(axis)
    for s, block in blocks.items():
        result = jnp.where(behind == s, shift(block, axis, s), result)
    return result


def ahead(blocks, axis):
    here, count = lax.axis_index(axis), blocks.shape[0]
    return {s: pick(blocks, (here + s) % count) for s in distances(axis)}


def gather_shifts(block, axis):
    got = {s: shift(block, axis, s) for s in distances(axis)}
    return [block] + [got[s] for s in range(1, lax.axis_size(axis))]


def in_order(got, axis):
    here, count = lax.axis_index(axis), len(got)
    got = jnp.stack(got)
    return jnp.stack([pick(got, (here - i) % count) for i in range(count)])


def trade(block, across):
    route = []
    for z in range(2):
        for x in range(4):
            for low in range(4):
                for c in range(2):
                    to_low = 3 - low if across else low
                    to = (((z ^ across) * 4 + x - x % 2 + c) * 4 + to_low) * 2 + x % 2
                    here = ((z * 4 + x) * 4 + low) * 2 + c
                    if to != here:
                        route.append((here, to))
    return lax.ppermute(block, ("zh", "x", "zl", "c"), route)


def mirror(block):
    return lax.ppermute(block, ("zh", "zl"), [(i, 7 - i) for i in range(8)])


def shards(hidden_in, norm_gain, snap_qkv, snap_out, owner_index, block_order):
    rows, width = hidden_in.shape
    ys = ("yh", "yl")
    zh, yh, yl, x, c = (lax.axis_index(name) for name in ("zh", "yh", "yl", "x", "c"))
    y = lax.axis_index(ys)
    ny, nx = 8, 4
    half = rows // 2
    core = c.reshape(1)
    owner = owner_index[0]
    zh0, y0, x0 = owner // (ny * nx), (owner // nx) % ny, owner % nx

    mine = lax.dynamic_slice_in_dim(hidden_in, c * half, half, 0).astype(jnp.float32)
    normed = (
        mine * lax.rsqrt(jnp.mean(mine * mine, axis=-1, keepdims=True) + 1e-06) * norm_gain
    ).astype(jnp.bfloat16)

    order = block_order.reshape(2, ny, nx) * rows + c * half
    order = jnp.stack([lax.dynamic_index_in_dim(order, (x + nx - s) % nx, 2, False) for s in range(nx)], axis=2)
    kpos = (pick(order, zh)[:, :, None] + jnp.arange(half, dtype=jnp.int32)).reshape(-1)
    kpos = jnp.concatenate([kpos, kpos + (1 - 2 * c) * half]).reshape(1, -1)
    here = lax.dynamic_index_in_dim(order, y, 1, keepdims=False)
    start, start_other = pick(here, zh), pick(here, 1 - zh)

    part = width // (2 * ny)
    w = fold(snap_qkv[0], ny)
    w = pick(exchange(w, "x"), x0)
    wo = snap_out[0].reshape(2, ny // 2, -1, snap_out.shape[2])
    wo = jnp.stack([pick(wo, yh), jnp.flip(pick(wo, 1 - yh), 0)], axis=1)
    wo = take_shifts(pick(wo, yl), ahead(wo, "yl"), "yl", y0 % (ny // 2))
    w, wo, normed, kpos, start, start_other = lax.optimization_barrier(
        (w, wo, normed, kpos, start, start_other)
    )
    w = pick(exchange(w, ys), y0)
    wo = jnp.transpose(wo.reshape(2, -1, nx, snap_out.shape[2] // nx), (2, 0, 1, 3))
    wo = take_shifts(pick(wo, x), ahead(wo, "x"), "x", x0)
    wo = jnp.where(yh == y0 // (ny // 2), wo[0], lax.ppermute(wo[1], ys, [(i, 7 - i) for i in range(8)]))
    wo = jnp.transpose(wo.reshape(wo.shape[0], nx, HD), (1, 0, 2)).reshape(part, HD)
    w = jnp.concatenate([w, wo], axis=1)
    w, normed = lax.optimization_barrier((w, normed))
    w = jnp.where(zh == zh0, jnp.where(x % 2 == c, w, trade(w, 0)), trade(w, 1))
    w = spread(w, ys).reshape(ny * part, 4 * HD)
    normed = gather_shifts(normed, "x")
    w, normed = lax.optimization_barrier((w, normed))
    q, kv = project(core, normed, w, swap(w, "c"), ny)
    wo = w[:, 3 * HD :].reshape(ny, nx, part // nx, HD)
    wo = jnp.transpose(wo, (0, 2, 1, 3)).reshape(ny * part // nx, nx * HD)
    q, kv, wo = lax.optimization_barrier((q, kv, wo))

    near = exchange(kv, ys).reshape(-1, 2 * HD)
    q_other = mirror(q)
    wo = in_order(gather_shifts(wo, "x"), "x")
    wo_far = swap(wo, "c")
    near, q_other, wo, wo_far = lax.optimization_barrier((near, q_other, wo, wo_far))
    far = swap(near, "c")

    others = mirror(attend(start_other, q_other, near, far, kpos, half))
    context = merge(x.reshape(1), attend(start, q, near, far, kpos, half), others)
    context = exchange(context, "x")
    terms = finish(core, context, wo, wo_far)
    terms = exchange(terms, ("zl", "c")).reshape(-1, rows, terms.shape[2])
    return jnp.sum(terms.astype(jnp.float32), axis=0).astype(jnp.bfloat16)


def solution(mesh):
    fine = Mesh(mesh.devices.reshape(2, 2, 4, 4, 4, 2), ("zh", "yh", "yl", "x", "zl", "c"))
    ctx, tp = ("zh", "yh", "yl", "x"), ("zl", "c")
    in_specs = (P(ctx, None), P(), P(ctx, None, None, tp), P(ctx, tp, None), P(), P())
    return jax.shard_map(shards, mesh=fine, in_specs=in_specs, out_specs=P(ctx, tp), check_vma=False)
```

```python
import functools

import jax
import jax.numpy as jnp
import numpy as np
from jax import lax
from jax.experimental import pallas as pl
from jax.experimental.pallas import tpu as pltpu
from jax.sharding import Mesh
from jax.sharding import PartitionSpec as P

HD = 128
HIDE = -1e30
CHUNK = 640
EXTRA = 16
WHOLE = pltpu.CompilerParams(vmem_limit_bytes=56 * 1024 * 1024)
LIMIT = pltpu.CompilerParams(vmem_limit_bytes=24 * 1024 * 1024)


def fold_kernel(w_ref, out_ref):
    for h in range(2):
        for r in range(2):
            for j in range(3):
                out_ref[2 * h + r, :, :, j * HD : (j + 1) * HD] = w_ref[j, r, :, :, h * HD : (h + 1) * HD]


def fold(w, ny):
    part, steps = w.shape[1] // (2 * ny), 2
    return pl.pallas_call(
        fold_kernel,
        grid=(steps,),
        in_specs=[pl.BlockSpec((3, 2, ny // steps, part, 2 * HD), lambda i: (0, 0, i, 0, 0))],
        out_specs=pl.BlockSpec((4, ny // steps, part, 3 * HD), lambda i: (0, i, 0, 0)),
        out_shape=jax.ShapeDtypeStruct((4, ny, part, 3 * HD), w.dtype),
        compiler_params=WHOLE,
        cost_estimate=pl.CostEstimate(flops=0, bytes_accessed=4 * w.size, transcendentals=0),
    )(w.reshape(3, 2, ny, part, 2 * HD))


def near_kernel(c_ref, *refs):
    x_refs, w_ref, out_ref = refs[:-2], refs[-2], refs[-1]
    depth = w_ref.shape[0]
    span = pl.ds(pl.multiple_of(c_ref[0] * depth, depth), depth)
    x = jnp.concatenate([ref[:, span] for ref in x_refs])
    out_ref[...] = jnp.dot(x, w_ref[:, : out_ref.shape[1]], preferred_element_type=jnp.float32)


def far_kernel(c_ref, *refs):
    x_refs, (w_ref, sum_ref, q_ref, kv_ref) = refs[:-4], refs[-4:]
    depth = w_ref.shape[0]
    span = pl.ds(pl.multiple_of((1 - c_ref[0]) * depth, depth), depth)
    x = jnp.concatenate([ref[:, span] for ref in x_refs])
    w = w_ref[:, : sum_ref.shape[1]]
    out = sum_ref[...] + jnp.dot(x, w, preferred_element_type=jnp.float32)
    q_ref[...] = out[:, :HD].astype(q_ref.dtype)
    kv = out[:, HD:].astype(kv_ref.dtype)
    for i in range(kv_ref.shape[0]):
        kv_ref[i] = kv


def project(core, x, near, far, count):
    n, cols = sum(block.shape[0] for block in x), 3 * HD
    smem, vmem = pl.BlockSpec(memory_space=pltpu.SMEM), pl.BlockSpec(memory_space=pltpu.VMEM)
    cost = pl.CostEstimate(
        flops=2 * n * near.shape[0] * cols, bytes_accessed=2 * (2 * n + cols) * near.shape[0], transcendentals=0
    )
    total = pl.pallas_call(
        near_kernel,
        in_specs=[smem] + [vmem] * (len(x) + 1),
        out_specs=vmem,
        out_shape=jax.ShapeDtypeStruct((n, cols), jnp.float32),
        compiler_params=LIMIT,
        cost_estimate=cost,
    )(core, *x, near)
    return pl.pallas_call(
        far_kernel,
        in_specs=[smem] + [vmem] * (len(x) + 2),
        out_specs=[vmem, vmem],
        out_shape=[
            jax.ShapeDtypeStruct((n, HD), jnp.bfloat16),
            jax.ShapeDtypeStruct((count, n, 2 * HD), jnp.bfloat16),
        ],
        compiler_params=LIMIT,
        cost_estimate=cost,
    )(core, *x, far, total)


def three_parts(value):
    first = value.astype(jnp.bfloat16).astype(jnp.float32)
    rest = value - first
    second = rest.astype(jnp.bfloat16).astype(jnp.float32)
    return first, second, rest - second


def score(start_ref, q_ref, kv_refs, kpos_refs, s_ref, half):
    factor = float(np.log2(np.e) / HD**0.5)
    rows = q_ref.shape[0]
    row = lax.broadcasted_iota(jnp.int32, (rows, 1), 0)
    qpos = row + start_ref[0]
    for b in range(1, rows // half):
        qpos = jnp.where(row < b * half, qpos, row - b * half + start_ref[b])
    q = q_ref[...]
    high = jnp.full((rows, HD), HIDE, jnp.float32)
    for i, (kv_ref, kpos_ref) in enumerate(zip(kv_refs, kpos_refs)):
        for at in range(0, kv_ref.shape[0], CHUNK):
            s = lax.dot_general(
                q, kv_ref[pl.ds(at, CHUNK), :HD], (((1,), (1,)), ((), ())), preferred_element_type=jnp.float32
            )
            s = jnp.where(kpos_ref[:, pl.ds(at, CHUNK)] <= qpos, s * factor, HIDE)
            s_ref[:, pl.ds(i * kv_ref.shape[0] + at, CHUNK)] = s
            for t in range(CHUNK // HD):
                high = jnp.maximum(high, s[:, t * HD : (t + 1) * HD])
    return jnp.max(high, axis=1, keepdims=True)


def weigh(top, kv_refs, s_ref):
    rows = s_ref.shape[0]
    base = jnp.where(top <= 0.5 * HIDE, 0.0, top)
    total = jnp.zeros((rows, HD), jnp.float32)
    acc = jnp.zeros((rows, HD), jnp.float32)
    for i, kv_ref in enumerate(kv_refs):
        for at in range(0, kv_ref.shape[0], CHUNK):
            p = jnp.exp2(s_ref[:, pl.ds(i * kv_ref.shape[0] + at, CHUNK)] - base)
            for t in range(CHUNK // HD):
                total = total + p[:, t * HD : (t + 1) * HD]
            acc = acc + jnp.dot(
                p.astype(jnp.bfloat16), kv_ref[pl.ds(at, CHUNK), HD:], preferred_element_type=jnp.float32
            )
    return jnp.sum(total, axis=1, keepdims=True), acc


def write_parts(top, total, acc, o_ref):
    half = o_ref.shape[1] - EXTRA
    o = acc / jnp.where(total == 0.0, 1.0, total)
    lane = lax.broadcasted_iota(jnp.int32, acc.shape, 1)
    stat = jnp.zeros(acc.shape, jnp.float32)
    for k, piece in enumerate(three_parts(top) + three_parts(total)):
        stat = jnp.where(lane == k, piece, stat)
    for b in range(o_ref.shape[0]):
        o_ref[b, :half, :] = o[b * half : (b + 1) * half].astype(o_ref.dtype)
        block = jnp.concatenate(
            [stat[b * half : (b + 1) * half], jnp.zeros((HD - half, HD), jnp.float32)]
        )
        o_ref[b, half:, :] = block.T[:EXTRA].astype(o_ref.dtype)


def whole_kernel(half, start_ref, q_ref, near_ref, far_ref, near_pos, far_pos, o_ref, s_ref):
    kv_refs = (near_ref, far_ref)
    top = score(start_ref, q_ref, kv_refs, (near_pos, far_pos), s_ref, half)
    write_parts(top, *weigh(top, kv_refs, s_ref), o_ref)


def first_kernel(half, start_ref, q_ref, kv_ref, kpos_ref, acc_ref, stat_ref, s_ref):
    top = score(start_ref, q_ref, (kv_ref,), (kpos_ref,), s_ref, half)
    total, acc = weigh(top, (kv_ref,), s_ref)
    acc_ref[...] = acc
    stat_ref[...] = jnp.where(lax.broadcasted_iota(jnp.int32, acc.shape, 1) == 0, top, total)


def second_kernel(half, start_ref, q_ref, kv_ref, kpos_ref, acc_ref, stat_ref, o_ref, s_ref):
    before = stat_ref[:, 0:1]
    top = jnp.maximum(before, score(start_ref, q_ref, (kv_ref,), (kpos_ref,), s_ref, half))
    total, acc = weigh(top, (kv_ref,), s_ref)
    keep = jnp.exp2(before - top)
    write_parts(top, total + stat_ref[:, 1:2] * keep, acc + acc_ref[...] * keep, o_ref)


def attend(kernel, half, start, q, kv, kpos, state=()):
    nq, nk = q.shape[0], sum(block.shape[0] for block in kv)
    vmem = pl.BlockSpec(memory_space=pltpu.VMEM)
    if kernel is first_kernel:
        out_shape = [jax.ShapeDtypeStruct((nq, HD), jnp.float32)] * 2
    else:
        out_shape = jax.ShapeDtypeStruct((nq // half, half + EXTRA, HD), jnp.bfloat16)
    return pl.pallas_call(
        functools.partial(kernel, half),
        in_specs=[pl.BlockSpec(memory_space=pltpu.SMEM)] + [vmem] * (1 + 2 * len(kv) + len(state)),
        out_specs=[vmem, vmem] if kernel is first_kernel else vmem,
        out_shape=out_shape,
        scratch_shapes=[pltpu.VMEM((nq, nk), jnp.float32)],
        compiler_params=LIMIT,
        cost_estimate=pl.CostEstimate(
            flops=4 * nq * nk * HD, bytes_accessed=nk * HD * 4, transcendentals=nq * nk
        ),
    )(start, q, *kv, *kpos, *state)


def merge_kernel(x_ref, near_ref, far_ref, out_ref):
    nx, half = out_ref.shape[0], out_ref.shape[1]
    for s in range(nx):
        tops, totals = [], []
        for ref in (near_ref, far_ref):
            stat = ref[s, half:, :].astype(jnp.float32)
            stat = jnp.concatenate([stat, jnp.zeros((HD - EXTRA, HD), jnp.float32)]).T[:half]
            tops.append(stat[:, 0:1] + stat[:, 1:2] + stat[:, 2:3])
            totals.append(stat[:, 3:4] + stat[:, 4:5] + stat[:, 5:6])
        top = jnp.maximum(tops[0], tops[1])
        a = totals[0] * jnp.exp2(tops[0] - top)
        b = totals[1] * jnp.exp2(tops[1] - top)
        mixed = near_ref[s, :half, :].astype(jnp.float32) * a + far_ref[s, :half, :].astype(jnp.float32) * b
        out_ref[lax.rem(x_ref[0] + nx - s, nx)] = (mixed / (a + b)).astype(out_ref.dtype)


def merge(x, near, far):
    nx, rows = near.shape[0], near.shape[1] - EXTRA
    vmem = pl.BlockSpec(memory_space=pltpu.VMEM)
    return pl.pallas_call(
        merge_kernel,
        in_specs=[pl.BlockSpec(memory_space=pltpu.SMEM), vmem, vmem],
        out_specs=vmem,
        out_shape=jax.ShapeDtypeStruct((nx, rows, HD), jnp.bfloat16),
        compiler_params=LIMIT,
        cost_estimate=pl.CostEstimate(flops=8 * near.size, bytes_accessed=6 * near.size, transcendentals=0),
    )(x, near, far)


def finish_kernel(c_ref, context_ref, near_ref, far_ref, out_ref):
    low = jnp.concatenate([context_ref[0], context_ref[2]], axis=1)
    high = jnp.concatenate([context_ref[1], context_ref[3]], axis=1)
    width = out_ref.shape[2]
    for ref, odd in ((near_ref, c_ref[0]), (far_ref, 1 - c_ref[0])):
        for h in range(2):
            terms = jnp.dot(low, ref[2 * h], preferred_element_type=jnp.float32)
            terms += jnp.dot(high, ref[2 * h + 1], preferred_element_type=jnp.float32)
            terms = terms.astype(out_ref.dtype)
            at = 2 * (2 * h + odd)
            out_ref[at] = terms[:, :width]
            out_ref[at + 1] = terms[:, width:]


def finish(core, context, near, far):
    half = context.shape[1]
    blocks, _, cols = near.shape
    vmem = pl.BlockSpec(memory_space=pltpu.VMEM)
    return pl.pallas_call(
        finish_kernel,
        in_specs=[pl.BlockSpec(memory_space=pltpu.SMEM), vmem, vmem, vmem],
        out_specs=vmem,
        out_shape=jax.ShapeDtypeStruct((2 * blocks, half, cols // 2), jnp.bfloat16),
        compiler_params=LIMIT,
        cost_estimate=pl.CostEstimate(
            flops=4 * half * near.size, bytes_accessed=4 * near.size, transcendentals=0
        ),
    )(core, context, near, far)


def swap(block, axis):
    return lax.ppermute(block, axis, [(0, 1), (1, 0)])


def exchange(block, axis):
    return lax.all_to_all(block, axis, 0, 0, tiled=True)


def pick(blocks, index):
    return lax.dynamic_index_in_dim(blocks, index, 0, keepdims=False)


def spread(block, axis):
    count = lax.axis_size(axis)
    return exchange(jnp.broadcast_to(block[None], (count,) + block.shape), axis)


def shift(block, axis, distance):
    count = lax.axis_size(axis)
    return lax.ppermute(block, axis, [(i, (i + distance) % count) for i in range(count)])


def distances(axis):
    count = lax.axis_size(axis)
    return sorted(range(1, count), key=lambda s: -min(s, count - s))


def take_shifts(result, blocks, axis, source):
    behind = (lax.axis_index(axis) - source) % lax.axis_size(axis)
    for s, block in blocks.items():
        result = jnp.where(behind == s, shift(block, axis, s), result)
    return result


def ahead(blocks, axis):
    here, count = lax.axis_index(axis), blocks.shape[0]
    return {s: pick(blocks, (here + s) % count) for s in distances(axis)}


def gather_shifts(block, axis):
    got = {s: shift(block, axis, s) for s in distances(axis)}
    return [block] + [got[s] for s in range(1, lax.axis_size(axis))]


def in_order(got, axis):
    here, count = lax.axis_index(axis), len(got)
    got = jnp.stack(got)
    return jnp.stack([pick(got, (here - i) % count) for i in range(count)])


def trade(block, across):
    route = []
    for z in range(2):
        for x in range(4):
            for low in range(4):
                for c in range(2):
                    to_low = 3 - low if across else low
                    to = (((z ^ across) * 4 + x - x % 2 + c) * 4 + to_low) * 2 + x % 2
                    here = ((z * 4 + x) * 4 + low) * 2 + c
                    if to != here:
                        route.append((here, to))
    return lax.ppermute(block, ("zh", "x", "zl", "c"), route)


def mirror(block):
    return lax.ppermute(block, ("zh", "zl"), [(i, 7 - i) for i in range(8)])


def shards(hidden_in, norm_gain, snap_qkv, snap_out, owner_index, block_order):
    rows, width = hidden_in.shape
    ys = ("yh", "yl")
    zh, yh, yl, x, c = (lax.axis_index(name) for name in ("zh", "yh", "yl", "x", "c"))
    y = lax.axis_index(ys)
    ny, nx = 8, 4
    half = rows // 2
    core = c.reshape(1)
    owner = owner_index[0]
    zh0, y0, x0 = owner // (ny * nx), (owner // nx) % ny, owner % nx

    mine = lax.dynamic_slice_in_dim(hidden_in, c * half, half, 0).astype(jnp.float32)
    normed = (
        mine * lax.rsqrt(jnp.mean(mine * mine, axis=-1, keepdims=True) + 1e-06) * norm_gain
    ).astype(jnp.bfloat16)

    order = block_order.reshape(2, ny, nx) * rows + c * half
    order = jnp.stack([lax.dynamic_index_in_dim(order, (x + nx - s) % nx, 2, False) for s in range(nx)], axis=2)
    kpos = (pick(order, zh)[:, :, None] + jnp.arange(half, dtype=jnp.int32)).reshape(-1)
    kpos = [kpos.reshape(1, -1), (kpos + (1 - 2 * c) * half).reshape(1, -1)]
    here = lax.dynamic_index_in_dim(order, y, 1, keepdims=False)
    start, start_other = pick(here, zh), pick(here, 1 - zh)

    part = width // (2 * ny)
    w = fold(snap_qkv[0], ny)
    w = pick(exchange(w, "x"), x0)
    wo = snap_out[0].reshape(2, ny // 2, -1, snap_out.shape[2])
    wo = jnp.stack([pick(wo, yh), jnp.flip(pick(wo, 1 - yh), 0)], axis=1)
    wo = take_shifts(pick(wo, yl), ahead(wo, "yl"), "yl", y0 % (ny // 2))
    w, wo, normed, kpos, start, start_other = lax.optimization_barrier(
        (w, wo, normed, kpos, start, start_other)
    )
    w = pick(exchange(w, ys), y0)
    wo = jnp.transpose(wo.reshape(2, -1, nx, snap_out.shape[2] // nx), (2, 0, 1, 3))
    wo = take_shifts(pick(wo, x), ahead(wo, "x"), "x", x0)
    wo = jnp.where(yh == y0 // (ny // 2), wo[0], lax.ppermute(wo[1], ys, [(i, 7 - i) for i in range(8)]))
    wo = jnp.transpose(wo.reshape(wo.shape[0], nx, HD), (1, 0, 2)).reshape(part, HD)
    w = jnp.concatenate([w, wo], axis=1)
    w, normed = lax.optimization_barrier((w, normed))
    w = jnp.where(zh == zh0, jnp.where(x % 2 == c, w, trade(w, 0)), trade(w, 1))
    w = spread(w, ys).reshape(ny * part, 4 * HD)
    normed = gather_shifts(normed, "x")
    w, normed = lax.optimization_barrier((w, normed))
    q, kv = project(core, normed, w, swap(w, "c"), ny)
    wo = w[:, 3 * HD :].reshape(ny, nx, part // nx, HD)
    wo = jnp.transpose(wo, (0, 2, 1, 3)).reshape(ny * part // nx, nx * HD)
    kv, wo = lax.optimization_barrier((kv, wo))

    near = exchange(kv, ys).reshape(-1, 2 * HD)
    q_other = mirror(q)
    wo = in_order(gather_shifts(wo, "x"), "x")
    wo_far = swap(wo, "c")
    near, q_other, wo, wo_far = lax.optimization_barrier((near, q_other, wo, wo_far))
    far = swap(near, "c")

    state = attend(first_kernel, half, start_other, q_other, [near], kpos[:1])
    others = mirror(attend(second_kernel, half, start_other, q_other, [far], kpos[1:], state))
    context = merge(x.reshape(1), attend(whole_kernel, half, start, q, [near, far], kpos), others)
    context = exchange(context, "x")
    terms = finish(core, context, wo, wo_far)
    terms = exchange(terms, ("zl", "c")).reshape(-1, rows, terms.shape[2])
    return jnp.sum(terms.astype(jnp.float32), axis=0).astype(jnp.bfloat16)


def solution(mesh):
    fine = Mesh(mesh.devices.reshape(2, 2, 4, 4, 4, 2), ("zh", "yh", "yl", "x", "zl", "c"))
    ctx, tp = ("zh", "yh", "yl", "x"), ("zl", "c")
    in_specs = (P(ctx, None), P(), P(ctx, None, None, tp), P(ctx, tp, None), P(), P())
    return jax.shard_map(shards, mesh=fine, in_specs=in_specs, out_specs=P(ctx, tp), check_vma=False)
```

```python
import functools

import jax
import jax.numpy as jnp
import numpy as np
from jax import lax
from jax.experimental import pallas as pl
from jax.experimental.pallas import tpu as pltpu
from jax.sharding import Mesh
from jax.sharding import PartitionSpec as P

HD = 128
HIDE = -1e30
CHUNK = 640
EXTRA = 16
WHOLE = pltpu.CompilerParams(vmem_limit_bytes=56 * 1024 * 1024)
LIMIT = pltpu.CompilerParams(vmem_limit_bytes=24 * 1024 * 1024)


def fold_kernel(w_ref, out_ref):
    for h in range(2):
        for r in range(2):
            for j in range(3):
                out_ref[2 * h + r, :, :, j * HD : (j + 1) * HD] = w_ref[j, r, :, :, h * HD : (h + 1) * HD]


def fold(w, ny):
    part, steps = w.shape[1] // (2 * ny), 2
    return pl.pallas_call(
        fold_kernel,
        grid=(steps,),
        in_specs=[pl.BlockSpec((3, 2, ny // steps, part, 2 * HD), lambda i: (0, 0, i, 0, 0))],
        out_specs=pl.BlockSpec((4, ny // steps, part, 3 * HD), lambda i: (0, i, 0, 0)),
        out_shape=jax.ShapeDtypeStruct((4, ny, part, 3 * HD), w.dtype),
        compiler_params=WHOLE,
        cost_estimate=pl.CostEstimate(flops=0, bytes_accessed=4 * w.size, transcendentals=0),
    )(w.reshape(3, 2, ny, part, 2 * HD))


def near_kernel(c_ref, *refs):
    x_refs, w_ref, out_ref = refs[:-2], refs[-2], refs[-1]
    depth = w_ref.shape[0]
    span = pl.ds(pl.multiple_of(c_ref[0] * depth, depth), depth)
    x = jnp.concatenate([ref[:, span] for ref in x_refs])
    out_ref[...] = jnp.dot(x, w_ref[:, : out_ref.shape[1]], preferred_element_type=jnp.float32)


def far_kernel(c_ref, *refs):
    x_refs, (w_ref, sum_ref, q_ref, kv_ref) = refs[:-4], refs[-4:]
    depth = w_ref.shape[0]
    span = pl.ds(pl.multiple_of((1 - c_ref[0]) * depth, depth), depth)
    x = jnp.concatenate([ref[:, span] for ref in x_refs])
    w = w_ref[:, : sum_ref.shape[1]]
    out = sum_ref[...] + jnp.dot(x, w, preferred_element_type=jnp.float32)
    q_ref[...] = out[:, :HD].astype(q_ref.dtype)
    kv = out[:, HD:].astype(kv_ref.dtype)
    for i in range(kv_ref.shape[0]):
        kv_ref[i] = kv


def project(core, x, near, far, count):
    n, cols = sum(block.shape[0] for block in x), 3 * HD
    smem, vmem = pl.BlockSpec(memory_space=pltpu.SMEM), pl.BlockSpec(memory_space=pltpu.VMEM)
    cost = pl.CostEstimate(
        flops=2 * n * near.shape[0] * cols, bytes_accessed=2 * (2 * n + cols) * near.shape[0], transcendentals=0
    )
    total = pl.pallas_call(
        near_kernel,
        in_specs=[smem] + [vmem] * (len(x) + 1),
        out_specs=vmem,
        out_shape=jax.ShapeDtypeStruct((n, cols), jnp.float32),
        compiler_params=LIMIT,
        cost_estimate=cost,
    )(core, *x, near)
    return pl.pallas_call(
        far_kernel,
        in_specs=[smem] + [vmem] * (len(x) + 2),
        out_specs=[vmem, vmem],
        out_shape=[
            jax.ShapeDtypeStruct((n, HD), jnp.bfloat16),
            jax.ShapeDtypeStruct((count, n, 2 * HD), jnp.bfloat16),
        ],
        compiler_params=LIMIT,
        cost_estimate=cost,
    )(core, *x, far, total)


def three_parts(value):
    first = value.astype(jnp.bfloat16).astype(jnp.float32)
    rest = value - first
    second = rest.astype(jnp.bfloat16).astype(jnp.float32)
    return first, second, rest - second


def score(start_ref, q_ref, kv_refs, kpos_refs, s_ref, half):
    factor = float(np.log2(np.e) / HD**0.5)
    rows = q_ref.shape[0]
    row = lax.broadcasted_iota(jnp.int32, (rows, 1), 0)
    qpos = row + start_ref[0]
    for b in range(1, rows // half):
        qpos = jnp.where(row < b * half, qpos, row - b * half + start_ref[b])
    q = q_ref[...]
    high = jnp.full((rows, HD), HIDE, jnp.float32)
    for i, (kv_ref, kpos_ref) in enumerate(zip(kv_refs, kpos_refs)):
        for at in range(0, kv_ref.shape[0], CHUNK):
            s = lax.dot_general(
                q, kv_ref[pl.ds(at, CHUNK), :HD], (((1,), (1,)), ((), ())), preferred_element_type=jnp.float32
            )
            s = jnp.where(kpos_ref[:, pl.ds(at, CHUNK)] <= qpos, s * factor, HIDE)
            s_ref[:, pl.ds(i * kv_ref.shape[0] + at, CHUNK)] = s
            for t in range(CHUNK // HD):
                high = jnp.maximum(high, s[:, t * HD : (t + 1) * HD])
    return jnp.max(high, axis=1, keepdims=True)


def weigh(top, kv_refs, s_ref):
    rows = s_ref.shape[0]
    base = jnp.where(top <= 0.5 * HIDE, 0.0, top)
    total = jnp.zeros((rows, HD), jnp.float32)
    acc = jnp.zeros((rows, HD), jnp.float32)
    for i, kv_ref in enumerate(kv_refs):
        for at in range(0, kv_ref.shape[0], CHUNK):
            p = jnp.exp2(s_ref[:, pl.ds(i * kv_ref.shape[0] + at, CHUNK)] - base)
            for t in range(CHUNK // HD):
                total = total + p[:, t * HD : (t + 1) * HD]
            acc = acc + jnp.dot(
                p.astype(jnp.bfloat16), kv_ref[pl.ds(at, CHUNK), HD:], preferred_element_type=jnp.float32
            )
    return jnp.sum(total, axis=1, keepdims=True), acc


def write_parts(top, total, acc, o_ref):
    half = o_ref.shape[1] - EXTRA
    o = acc / jnp.where(total == 0.0, 1.0, total)
    lane = lax.broadcasted_iota(jnp.int32, acc.shape, 1)
    stat = jnp.zeros(acc.shape, jnp.float32)
    for k, piece in enumerate(three_parts(top) + three_parts(total)):
        stat = jnp.where(lane == k, piece, stat)
    for b in range(o_ref.shape[0]):
        o_ref[b, :half, :] = o[b * half : (b + 1) * half].astype(o_ref.dtype)
        block = jnp.concatenate(
            [stat[b * half : (b + 1) * half], jnp.zeros((HD - half, HD), jnp.float32)]
        )
        o_ref[b, half:, :] = block.T[:EXTRA].astype(o_ref.dtype)


def whole_kernel(half, start_ref, q_ref, near_ref, far_ref, near_pos, far_pos, o_ref, s_ref):
    kv_refs = (near_ref, far_ref)
    top = score(start_ref, q_ref, kv_refs, (near_pos, far_pos), s_ref, half)
    write_parts(top, *weigh(top, kv_refs, s_ref), o_ref)


def first_kernel(half, start_ref, q_ref, kv_ref, kpos_ref, acc_ref, stat_ref, s_ref):
    top = score(start_ref, q_ref, (kv_ref,), (kpos_ref,), s_ref, half)
    total, acc = weigh(top, (kv_ref,), s_ref)
    acc_ref[...] = acc
    stat_ref[...] = jnp.where(lax.broadcasted_iota(jnp.int32, acc.shape, 1) == 0, top, total)


def second_kernel(half, start_ref, q_ref, kv_ref, kpos_ref, acc_ref, stat_ref, o_ref, s_ref):
    before = stat_ref[:, 0:1]
    top = jnp.maximum(before, score(start_ref, q_ref, (kv_ref,), (kpos_ref,), s_ref, half))
    total, acc = weigh(top, (kv_ref,), s_ref)
    keep = jnp.exp2(before - top)
    write_parts(top, total + stat_ref[:, 1:2] * keep, acc + acc_ref[...] * keep, o_ref)


def attend(kernel, half, start, q, kv, kpos, state=()):
    nq, nk = q.shape[0], sum(block.shape[0] for block in kv)
    vmem = pl.BlockSpec(memory_space=pltpu.VMEM)
    if kernel is first_kernel:
        out_shape = [jax.ShapeDtypeStruct((nq, HD), jnp.float32)] * 2
    else:
        out_shape = jax.ShapeDtypeStruct((nq // half, half + EXTRA, HD), jnp.bfloat16)
    return pl.pallas_call(
        functools.partial(kernel, half),
        in_specs=[pl.BlockSpec(memory_space=pltpu.SMEM)] + [vmem] * (1 + 2 * len(kv) + len(state)),
        out_specs=[vmem, vmem] if kernel is first_kernel else vmem,
        out_shape=out_shape,
        scratch_shapes=[pltpu.VMEM((nq, nk), jnp.float32)],
        compiler_params=LIMIT,
        cost_estimate=pl.CostEstimate(
            flops=4 * nq * nk * HD, bytes_accessed=nk * HD * 4, transcendentals=nq * nk
        ),
    )(start, q, *kv, *kpos, *state)


def merge_kernel(x_ref, near_ref, far_ref, out_ref):
    nx, half = out_ref.shape[0], out_ref.shape[1]
    for s in range(nx):
        tops, totals = [], []
        for ref in (near_ref, far_ref):
            stat = ref[s, half:, :].astype(jnp.float32)
            stat = jnp.concatenate([stat, jnp.zeros((HD - EXTRA, HD), jnp.float32)]).T[:half]
            tops.append(stat[:, 0:1] + stat[:, 1:2] + stat[:, 2:3])
            totals.append(stat[:, 3:4] + stat[:, 4:5] + stat[:, 5:6])
        top = jnp.maximum(tops[0], tops[1])
        a = totals[0] * jnp.exp2(tops[0] - top)
        b = totals[1] * jnp.exp2(tops[1] - top)
        mixed = near_ref[s, :half, :].astype(jnp.float32) * a + far_ref[s, :half, :].astype(jnp.float32) * b
        out_ref[lax.rem(x_ref[0] + nx - s, nx)] = (mixed / (a + b)).astype(out_ref.dtype)


def merge(x, near, far):
    nx, rows = near.shape[0], near.shape[1] - EXTRA
    vmem = pl.BlockSpec(memory_space=pltpu.VMEM)
    return pl.pallas_call(
        merge_kernel,
        in_specs=[pl.BlockSpec(memory_space=pltpu.SMEM), vmem, vmem],
        out_specs=vmem,
        out_shape=jax.ShapeDtypeStruct((nx, rows, HD), jnp.bfloat16),
        compiler_params=LIMIT,
        cost_estimate=pl.CostEstimate(flops=8 * near.size, bytes_accessed=6 * near.size, transcendentals=0),
    )(x, near, far)


def finish_kernel(c_ref, context_ref, near_ref, far_ref, out_ref):
    low = jnp.concatenate([context_ref[0], context_ref[2]], axis=1)
    high = jnp.concatenate([context_ref[1], context_ref[3]], axis=1)
    width = out_ref.shape[2]
    for ref, odd in ((near_ref, c_ref[0]), (far_ref, 1 - c_ref[0])):
        for h in range(2):
            terms = jnp.dot(low, ref[2 * h], preferred_element_type=jnp.float32)
            terms += jnp.dot(high, ref[2 * h + 1], preferred_element_type=jnp.float32)
            terms = terms.astype(out_ref.dtype)
            at = 2 * (2 * h + odd)
            out_ref[at] = terms[:, :width]
            out_ref[at + 1] = terms[:, width:]


def finish(core, context, near, far):
    half = context.shape[1]
    blocks, _, cols = near.shape
    vmem = pl.BlockSpec(memory_space=pltpu.VMEM)
    return pl.pallas_call(
        finish_kernel,
        in_specs=[pl.BlockSpec(memory_space=pltpu.SMEM), vmem, vmem, vmem],
        out_specs=vmem,
        out_shape=jax.ShapeDtypeStruct((2 * blocks, half, cols // 2), jnp.bfloat16),
        compiler_params=LIMIT,
        cost_estimate=pl.CostEstimate(
            flops=4 * half * near.size, bytes_accessed=4 * near.size, transcendentals=0
        ),
    )(core, context, near, far)


def swap(block, axis):
    return lax.ppermute(block, axis, [(0, 1), (1, 0)])


def exchange(block, axis):
    return lax.all_to_all(block, axis, 0, 0, tiled=True)


def pick(blocks, index):
    return lax.dynamic_index_in_dim(blocks, index, 0, keepdims=False)


def spread(block, axis):
    count = lax.axis_size(axis)
    return exchange(jnp.broadcast_to(block[None], (count,) + block.shape), axis)


def shift(block, axis, distance):
    count = lax.axis_size(axis)
    return lax.ppermute(block, axis, [(i, (i + distance) % count) for i in range(count)])


def distances(axis):
    count = lax.axis_size(axis)
    return sorted(range(1, count), key=lambda s: -min(s, count - s))


def take_shifts(result, blocks, axis, source):
    behind = (lax.axis_index(axis) - source) % lax.axis_size(axis)
    for s, block in blocks.items():
        result = jnp.where(behind == s, shift(block, axis, s), result)
    return result


def ahead(blocks, axis):
    here, count = lax.axis_index(axis), blocks.shape[0]
    return {s: pick(blocks, (here + s) % count) for s in distances(axis)}


def gather_shifts(block, axis):
    got = {s: shift(block, axis, s) for s in distances(axis)}
    return [block] + [got[s] for s in range(1, lax.axis_size(axis))]


def in_order(got, axis):
    here, count = lax.axis_index(axis), len(got)
    got = jnp.stack(got)
    return jnp.stack([pick(got, (here - i) % count) for i in range(count)])


def trade(block, across):
    route = []
    for z in range(2):
        for x in range(4):
            for low in range(4):
                for c in range(2):
                    to_low = 3 - low if across else low
                    to = (((z ^ across) * 4 + x - x % 2 + c) * 4 + to_low) * 2 + x % 2
                    here = ((z * 4 + x) * 4 + low) * 2 + c
                    if to != here:
                        route.append((here, to))
    return lax.ppermute(block, ("zh", "x", "zl", "c"), route)


def mirror(block):
    return lax.ppermute(block, ("zh", "zl"), [(i, 7 - i) for i in range(8)])


def shards(hidden_in, norm_gain, snap_qkv, snap_out, owner_index, block_order):
    rows, width = hidden_in.shape
    ys = ("yh", "yl")
    zh, yh, yl, x, c = (lax.axis_index(name) for name in ("zh", "yh", "yl", "x", "c"))
    y = lax.axis_index(ys)
    ny, nx = 8, 4
    half = rows // 2
    core = c.reshape(1)
    owner = owner_index[0]
    zh0, y0, x0 = owner // (ny * nx), (owner // nx) % ny, owner % nx

    mine = lax.dynamic_slice_in_dim(hidden_in, c * half, half, 0).astype(jnp.float32)
    normed = (
        mine * lax.rsqrt(jnp.mean(mine * mine, axis=-1, keepdims=True) + 1e-06) * norm_gain
    ).astype(jnp.bfloat16)

    order = block_order.reshape(2, ny, nx) * rows + c * half
    order = jnp.stack([lax.dynamic_index_in_dim(order, (x + nx - s) % nx, 2, False) for s in range(nx)], axis=2)
    kpos = (pick(order, zh)[:, :, None] + jnp.arange(half, dtype=jnp.int32)).reshape(-1)
    kpos = [kpos.reshape(1, -1), (kpos + (1 - 2 * c) * half).reshape(1, -1)]
    here = lax.dynamic_index_in_dim(order, y, 1, keepdims=False)
    start, start_other = pick(here, zh), pick(here, 1 - zh)

    part = width // (2 * ny)
    w = fold(snap_qkv[0], ny)
    w = pick(exchange(w, "x"), x0)
    wo = snap_out[0].reshape(2, ny // 2, -1, snap_out.shape[2])
    wo = jnp.stack([pick(wo, yh), jnp.flip(pick(wo, 1 - yh), 0)], axis=1)
    wo = take_shifts(pick(wo, yl), ahead(wo, "yl"), "yl", y0 % (ny // 2))
    wo = jnp.transpose(wo.reshape(2, -1, nx, snap_out.shape[2] // nx), (2, 0, 1, 3))
    wo, blocks = pick(wo, x), ahead(wo, "x")
    w, wo, blocks, normed, kpos, start, start_other = lax.optimization_barrier(
        (w, wo, blocks, normed, kpos, start, start_other)
    )
    w = pick(exchange(w, ys), y0)
    wo = take_shifts(wo, blocks, "x", x0)
    wo = jnp.where(yh == y0 // (ny // 2), wo[0], lax.ppermute(wo[1], ys, [(i, 7 - i) for i in range(8)]))
    wo = jnp.transpose(wo.reshape(wo.shape[0], nx, HD), (1, 0, 2)).reshape(part, HD)
    w = jnp.concatenate([w, wo], axis=1)
    w, normed = lax.optimization_barrier((w, normed))
    w = jnp.where(zh == zh0, jnp.where(x % 2 == c, w, trade(w, 0)), trade(w, 1))
    w = spread(w, ys).reshape(ny * part, 4 * HD)
    normed = gather_shifts(normed, "x")
    w, normed = lax.optimization_barrier((w, normed))
    q, kv = project(core, normed, w, swap(w, "c"), ny)
    wo = w[:, 3 * HD :].reshape(ny, nx, part // nx, HD)
    wo = jnp.transpose(wo, (0, 2, 1, 3)).reshape(ny * part // nx, nx * HD)
    kv, wo = lax.optimization_barrier((kv, wo))

    near = exchange(kv, ys).reshape(-1, 2 * HD)
    q_other = mirror(q)
    wo = in_order(gather_shifts(wo, "x"), "x")
    wo_far = swap(wo, "c")
    near, q_other, wo, wo_far = lax.optimization_barrier((near, q_other, wo, wo_far))
    far = swap(near, "c")

    state = attend(first_kernel, half, start_other, q_other, [near], kpos[:1])
    others = mirror(attend(second_kernel, half, start_other, q_other, [far], kpos[1:], state))
    context = merge(x.reshape(1), attend(whole_kernel, half, start, q, [near, far], kpos), others)
    context = exchange(context, "x")
    terms = finish(core, context, wo, wo_far)
    terms = exchange(terms, ("zl", "c")).reshape(-1, rows, terms.shape[2])
    return jnp.sum(terms.astype(jnp.float32), axis=0).astype(jnp.bfloat16)


def solution(mesh):
    fine = Mesh(mesh.devices.reshape(2, 2, 4, 4, 4, 2), ("zh", "yh", "yl", "x", "zl", "c"))
    ctx, tp = ("zh", "yh", "yl", "x"), ("zl", "c")
    in_specs = (P(ctx, None), P(), P(ctx, None, None, tp), P(ctx, tp, None), P(), P())
    return jax.shard_map(shards, mesh=fine, in_specs=in_specs, out_specs=P(ctx, tp), check_vma=False)
```
